32 devices in a mesh: pipe: 4 (over y, x), dp: 8 (over z, core).
Axes of the slice: x: 2, y: 2, z: 4, core: 2. Of those that a mesh axis runs over, the one named last changes fastest.
Arguments:
- tokens: bfloat16 [128, 49, 768], P('dp', None, 'pipe'), may hold values from -6 to 6
- cotangent: bfloat16 [128, 49, 768], P('dp', None, 'pipe'), may hold values from -6 to 6
- in_weight: bfloat16 [4, 768, 3072], P('pipe')
- down_weight: bfloat16 [4, 1536, 768], P('pipe'), may hold values from -0.109375 to 0.109375
- norm_gain: float32 [4, 768], replicated, may hold values from 0.5 to 1.5
- norm_shift: float32 [4, 768], replicated, may hold values from -1 to 1
- out_bias: float32 [4, 768], replicated, may hold values from -1 to 1
- qv_bias: float32 [2, 2, 768], replicated, may hold values from -1 to 1
- fc1_bias: float32 [2, 3072], replicated, may hold values from -1 to 1
- rel_table: float32 [2, 169, 24], replicated, may hold values from -3 to 3
- shift_regions: int32 [49], replicated, may hold values from 0 to 8
- crop_global: int32 [128], P('dp'), may hold values 0 or 1
- micro_of: int32 [128, 1], P('dp'), may hold values from 0 to 3; in each aligned block of 16 rows (0 to 15, 16 to 31, ...) at most 6 rows name the same one
Outputs:
- output_rows: bfloat16 [128, 49, 768], P('dp', None, 'pipe')
- tokens_grad: float32 [128, 49, 768], P('dp', None, 'pipe')
- in_weight_grad: float32 [4, 768, 3072], P('pipe')
- down_weight_grad: float32 [4, 1536, 768], P('pipe')
- norm_gain_grad: float32 [4, 768], replicated
- norm_shift_grad: float32 [4, 768], replicated
- out_bias_grad: float32 [4, 768], replicated
- qv_bias_grad: float32 [2, 2, 768], replicated
- fc1_bias_grad: float32 [2, 3072], replicated
- rel_table_grad: float32 [2, 169, 24], replicated
The draws below stay inside these ranges and needn't reach their ends.
Inputs may be any that keep to these rules, and one draw needn't show every extreme that they name: `micro_of`: in the crops of one device (aligned blocks of 16) no micro-batch is named more than 6 times, and some micro-batch is named exactly 6 times; every micro-batch is named somewhere.
All inputs are finite; a program needn't handle non-finite values. No bound on the sum of `crop_global` on one device may be relied on, other than what follows from the above.
Results may differ from the reference program's by a relative error of at most 0.02.
Values may be sent and summed in bfloat16 or wider, within the bound.
No kernel may reach another device: no remote copies, remote signals or barrier semaphores. Data moves between devices by JAX's collectives and lax.ppermute only.
A program may use at most 512 MiB of HBM per device.

```python
import math
import jax
import jax.numpy as jnp
import numpy as np
from jax import lax

D = 768
HEADS = 24
HEAD = 32
FF = 3072
WIN = 7
SMALL_SIDE = 3
SECTIONS = 4
MICRO = 4
CROPS_DEV = 16
POS = 49
SPAN = 169
CAP = 6
CROPS = 128


def draw_in_weight(key, part):
    key = jax.random.fold_in(key, 11)
    base = jax.random.normal(key, (SECTIONS, D, FF), jnp.float32) * D ** (-0.5)
    section_index = jnp.arange(SECTIONS)[:, None, None]
    column = jnp.arange(FF)[None, None, :]
    lift = jnp.where((section_index % 2 == 0) & (column >= 3 * D), 5.0, 1.0)
    return (base * lift).astype(jnp.bfloat16)


def touch_ends(entries, own_key, low, largest):
    place = [jax.random.randint(jax.random.fold_in(own_key, axis), (), 0, length) for axis, length in enumerate(entries.shape)]
    longest = entries.shape.index(max(entries.shape))
    beside = place[:longest] + [(place[longest] + 1) % entries.shape[longest]] + place[longest + 1:]
    return entries.at[tuple(place)].set(low).at[tuple(beside)].set(largest)


def steps_of(own_key, extent, pieces, least, top_value):
    loudness = 1.0
    for dim, blocks in pieces:
        heights = jax.random.uniform(jax.random.fold_in(jax.random.fold_in(own_key, 6), dim), (blocks,), jnp.float32, least / len(pieces), top_value / len(pieces))
        loudness = loudness * jnp.repeat(jnp.exp(heights), extent[dim] // blocks).reshape((-1,) + (1,) * (len(extent) - 1 - dim))
    return loudness


def shared_out(rng, own, number, rows, count, top, most, skew):
    sequence = jax.random.permutation(rng, count)
    crowded, common = load_shares(count, rows * top, most, skew, True), load_shares(count, rows * top, most, skew, False)
    places = jnp.arange(count)

    def named(lengths, turn):
        used = int((lengths > 0).sum())
        fixed = max(1, used // 4)
        passed = fixed + (places - fixed + turn * (used - fixed)) % max(1, count - fixed)
        return jnp.zeros((count,), jnp.int32).at[sequence[jnp.where(places < fixed, places, passed)]].set(jnp.asarray(lengths, jnp.int32))

    lengths = jnp.where(number % 4 == 0, named(crowded, number // 4), named(common, number - number // 4 - 1))
    mixed = jax.random.permutation(jax.random.fold_in(own, 3), count)
    donor, taker = mixed[0:count // 2 * 2:2], mixed[1:count // 2 * 2:2]
    room = jnp.minimum(lengths[donor] - 1, most - lengths[taker]) // 2
    room = jnp.where((donor == sequence[0]) | (taker == sequence[0]) | (lengths[taker] == 0), 0, jnp.maximum(room, 0))
    passed = jax.random.randint(jax.random.fold_in(own, 4), (count // 2,), 0, 1 << 20) % (room + 1)
    lengths = lengths.at[donor].add(-passed).at[taker].add(passed)
    items = jnp.searchsorted(jnp.cumsum(lengths), jnp.arange(rows * top), side="right").astype(jnp.int32)
    table = items.reshape(top, rows).T
    table = table[jax.random.permutation(jax.random.fold_in(own, 1), rows)]
    turn = jax.random.randint(jax.random.fold_in(own, 2), (rows, 1), 0, top)
    return jnp.take_along_axis(table, (jnp.arange(top)[None, :] + turn) % top, axis=1)


def load_shares(number_of, total, limit, lean, full):
    loads = [(1 << 20) // math.isqrt(rank ** lean) + 1 for rank in range(1, number_of + 1)]
    largest = limit if full else min(limit, max(-(-total // number_of), total * loads[0] // sum(loads)))
    least = 1 if total - largest >= number_of - 1 else 0
    holding, rest = [largest] + [least] * (number_of - 1), total - largest - least * (number_of - 1)
    while rest > 0:
        free = [i for i in range(1, number_of) if holding[i] < largest] or [i for i in range(1, number_of) if holding[i] < limit]
        pool, remaining = sum([loads[i] for i in free]), rest
        for i in free:
            addition = min(limit - holding[i], max(1, remaining * loads[i] // pool), rest)
            holding[i] = holding[i] + addition
            rest = rest - addition
    return np.array(holding)


def gaussian(rng, extent, scale, reach, pieces=(), kind=jnp.bfloat16):
    values = jax.random.normal(rng, extent, jnp.float32) * scale
    if len(pieces) > 0:
        values = steps_of(rng, extent, pieces, -0.22, 0.18) * values
    return jnp.clip(values, min=-reach, max=reach).astype(kind)


def setup_inputs(seed: int = 0) -> dict:
    key_list = jax.random.split(jax.random.key(seed), 14)
    tokens = gaussian(key_list[0], (CROPS, POS, D), 1.0, 6.0, ((0, 8), (2, 4)))
    cotangent = gaussian(key_list[1], (CROPS, POS, D), 1.0, 6.0, ((0, 8), (2, 4)))
    in_weight = draw_in_weight(jax.random.fold_in(key_list[13], 71), 0)
    down_weight = gaussian(key_list[3], (SECTIONS, FF // 2, D), FF ** -0.5, 0.109375, ((0, 4),))
    norm_gain = jnp.clip(1.0 + 0.1 * jax.random.normal(key_list[4], (SECTIONS, D), jnp.float32), 0.5, 1.5)
    norm_shift = gaussian(key_list[5], (SECTIONS, D), 0.2, 1.0, (), jnp.float32)
    out_bias = gaussian(key_list[6], (SECTIONS, D), 0.2, 1.0, (), jnp.float32)
    qv_bias = gaussian(key_list[7], (2, 2, D), 0.2, 1.0, (), jnp.float32)
    fc1_bias = gaussian(key_list[8], (2, FF), 0.2, 1.0, (), jnp.float32)
    rel_table = gaussian(key_list[9], (2, SPAN, HEADS), 0.7, 3.0, (), jnp.float32)
    shift_regions = touch_ends(jax.random.randint(key_list[10], (POS,), 0, 9), jax.random.fold_in(key_list[10], 1), 0, 8).astype(jnp.int32)
    crop_global = touch_ends((jax.random.randint(key_list[11], (CROPS,), 0, 2) < 1).astype(jnp.int32), jax.random.fold_in(key_list[11], 1), 0, 1)
    micro_of_keys = jax.random.split(jax.random.fold_in(key_list[12], 1), CROPS // CROPS_DEV)
    micro_of_turns = jax.random.permutation(jax.random.fold_in(key_list[12], 3), CROPS // CROPS_DEV)
    micro_of = jax.vmap(lambda own, number: shared_out(jax.random.fold_in(key_list[12], 2), own, number, CROPS_DEV, MICRO, 1, CAP, 2))(micro_of_keys, micro_of_turns).reshape((CROPS, 1))
    return dict(tokens=tokens, cotangent=cotangent, in_weight=in_weight, down_weight=down_weight, norm_gain=norm_gain, norm_shift=norm_shift, out_bias=out_bias, qv_bias=qv_bias, fc1_bias=fc1_bias, rel_table=rel_table, shift_regions=shift_regions, crop_global=crop_global, micro_of=micro_of)


EPSILON = 1e-05
NEGATIVE = -1e+30
HIGHEST = lax.Precision.HIGHEST

@jax.custom_vjp
def low(v):
    return lax.optimization_barrier(v.astype(jnp.bfloat16)).astype(jnp.float32)

@jax.custom_vjp
def low_back(v):
    return v

def low_keep(v):
    return (low(v), None)

def low_pass(kept, grad):
    return (grad,)

def back_keep(v):
    return (v, None)

def back_low(kept, grad):
    return (low(grad),)
low.defvjp(low_keep, low_pass)
low_back.defvjp(back_keep, back_low)

def layer_norm(hidden_rows, gain_vec, shift_vec):
    row_mean = lax.optimization_barrier(jnp.mean(hidden_rows, -1, keepdims=True))
    centered = hidden_rows - row_mean
    variance = lax.optimization_barrier(jnp.mean(centered * centered, -1, keepdims=True))
    return centered * lax.rsqrt(variance + EPSILON) * gain_vec + shift_vec

def matmul(left, right):
    return jnp.einsum('gpd,df->gpf', left, right, precision=HIGHEST)

def roll_grid(rows, amount):
    grid = rows.reshape((rows.shape[0], WIN, WIN) + rows.shape[2:])
    grid = jnp.roll(grid, (amount, amount), axis=(1, 2))
    return grid.reshape(rows.shape)

def attention_section(hidden_rows, valid_group, weight, gain_vec, shift_vec, out_vec, qv_vec, rel_bias, rel_index, region_same, shifted):
    model_width = hidden_rows.shape[-1]
    group_size = hidden_rows.shape[0]
    offset = WIN // 2
    normed = layer_norm(hidden_rows, gain_vec, shift_vec)
    key_ok = valid_group
    if shifted:
        normed = roll_grid(normed, -offset)
        key_ok = roll_grid(valid_group, -offset)
    normed = low(normed)
    query = low_back(low(matmul(normed, weight[:, :model_width]) + qv_vec[0]))
    key_rows = low_back(low(matmul(normed, weight[:, model_width:2 * model_width])))
    value_rows = low_back(low(matmul(normed, weight[:, 2 * model_width:3 * model_width]) + qv_vec[1]))
    head_shape = (group_size, POS, HEADS, HEAD)
    scores = jnp.einsum('gihe,gjhe->ghij', query.reshape(head_shape), key_rows.reshape(head_shape), precision=HIGHEST) * HEAD ** (-0.5)
    scores = low_back(scores + rel_bias[rel_index].transpose(2, 0, 1)[None])
    allowed = key_ok[:, None, None, :]
    if shifted:
        allowed = allowed & region_same[None, None]
    scores = jnp.where(allowed, scores, NEGATIVE)
    softened = low(jax.nn.softmax(scores, -1))
    mixed = jnp.einsum('ghij,gjhe->gihe', softened, value_rows.reshape(head_shape), precision=HIGHEST).reshape(hidden_rows.shape)
    mixed = low_back(low(mixed))
    branch = matmul(mixed, weight[:, 3 * model_width:]) + out_vec
    if shifted:
        branch = roll_grid(branch, offset)
    return low(hidden_rows + branch)

def mlp_section(hidden_rows, weight, down_mat, gain_vec, shift_vec, out_vec, first_bias):
    normed = low(layer_norm(hidden_rows, gain_vec, shift_vec))
    inner = low_back(matmul(normed, weight) + first_bias)
    activated = low_back(low(jax.nn.gelu(inner, approximate=False)))
    branch = jnp.einsum('gpf,fd->gpd', activated, down_mat, precision=HIGHEST) + out_vec
    return low(hidden_rows + branch)

def reference(tokens, cotangent, in_weight, down_weight, norm_gain, norm_shift, out_bias, qv_bias, fc1_bias, rel_table, shift_regions, crop_global, micro_of):
    positions = jnp.arange(POS, dtype=jnp.int32)
    grid_row = positions // WIN
    grid_col = positions % WIN
    small_patch = (grid_row < SMALL_SIDE) & (grid_col < SMALL_SIDE)
    valid_rows = (crop_global[:, None] == 1) | small_patch[None, :]
    rel_index = (grid_row[:, None] - grid_row[None, :] + WIN - 1) * (2 * WIN - 1) + (grid_col[:, None] - grid_col[None, :] + WIN - 1)
    region_same = shift_regions[:, None] == shift_regions[None, :]
    micro_index = micro_of[:, 0]
    member = (micro_index[:, None] == jnp.arange(MICRO, dtype=jnp.int32)[None, :]).astype(jnp.float32)
    crop_rows = jnp.where(crop_global == 1, POS, SMALL_SIDE * SMALL_SIDE).astype(jnp.float32)
    counts = lax.optimization_barrier(jnp.sum(member * crop_rows[:, None], 0))
    batch_scale = jnp.sum(counts) / (MICRO * counts)
    row_scale = lax.optimization_barrier(jnp.sum(member * batch_scale[None, :], 1))
    seed_grad = low(cotangent.astype(jnp.float32) * row_scale[:, None, None])
    group_size = math.gcd(CROPS, 64)
    group_count = CROPS // group_size
    params = (in_weight.astype(jnp.float32), down_weight.astype(jnp.float32), norm_gain, norm_shift, out_bias, qv_bias, fc1_bias, rel_table)

    def run_group(rows, valid_group, param_set):
        in_mats, down_mats, gain_rows, shift_rows, out_vecs, qv_rows, first_biases, rel_tables = param_set
        hidden_rows = attention_section(rows, valid_group, in_mats[0], gain_rows[0], shift_rows[0], out_vecs[0], qv_rows[0], rel_tables[0], rel_index, region_same, False)
        hidden_rows = low_back(hidden_rows)
        hidden_rows = mlp_section(hidden_rows, in_mats[1], jnp.concatenate([down_mats[1], down_mats[0]], 0), gain_rows[1], shift_rows[1], out_vecs[1], first_biases[0])
        hidden_rows = low_back(hidden_rows)
        hidden_rows = attention_section(hidden_rows, valid_group, in_mats[2], gain_rows[2], shift_rows[2], out_vecs[2], qv_rows[1], rel_tables[1], rel_index, region_same, True)
        hidden_rows = low_back(hidden_rows)
        hidden_rows = mlp_section(hidden_rows, in_mats[3], jnp.concatenate([down_mats[3], down_mats[2]], 0), gain_rows[3], shift_rows[3], out_vecs[3], first_biases[1])
        return jnp.where(valid_group[..., None], hidden_rows, jnp.float32(0.0))
    checked = jax.checkpoint(run_group)

    def forward(token_rows, param_set):

        def one_group(items):
            return checked(items[0], items[1], param_set)
        grouped = lax.map(one_group, (token_rows.reshape(group_count, group_size, POS, D), valid_rows.reshape(group_count, group_size, POS)))
        return grouped.reshape(CROPS, POS, D)
    output, pull = jax.vjp(forward, tokens.astype(jnp.float32), params)
    token_grad, grads = pull(seed_grad)
    return (output.astype(jnp.bfloat16), token_grad, grads[0], grads[1], grads[2], grads[3], grads[4], grads[5], grads[6], grads[7])
```

```python
import functools

import jax
import jax.numpy as jnp
import numpy as np
from jax import lax
from jax.experimental import pallas as pl
from jax.experimental.pallas import tpu as pltpu
from jax.sharding import PartitionSpec as P

HEADS = 24
HEAD = 32
FF = 3072
D = 768
WIN = 7
SMALL_SIDE = 3
SECTIONS = 4
MICRO = 4
POS = 49
SPAN = 169
SMALL = SMALL_SIDE * SMALL_SIDE

T = 128
PAIR = 2
R = PAIR * T
SMALL_AT = 2 * POS
GROUP = 4
TABLE = 256
IN_CHUNKS = 4
DOWN_CHUNKS = 2
CHUNKS = IN_CHUNKS + DOWN_CHUNKS
LINE = D // IN_CHUNKS

EPSILON = 1e-05
NEGATIVE = -1e30
SQRT_HALF = 0.7071067811865476
INV_SQRT_TAU = 0.3989422804014327
SCALE = HEAD**-0.5
BF = jnp.bfloat16
F32 = jnp.float32
VM = pl.BlockSpec(memory_space=pltpu.VMEM)
SM = pl.BlockSpec(memory_space=pltpu.SMEM)
LIMIT = 20 << 20
SMALL_LIMIT = 14 << 20
TINY_LIMIT = 8 << 20


def pin(x):
    return pltpu.with_memory_space_constraint(x, pltpu.VMEM)


def like(x):
    return jax.ShapeDtypeStruct(x.shape, x.dtype)


def shape(dims, kind):
    return jax.ShapeDtypeStruct(dims, kind)


def nn(a, b):
    return lax.dot_general(a, b, (((1,), (0,)), ((), ())), preferred_element_type=F32)


def nt(a, b):
    return lax.dot_general(a, b, (((1,), (1,)), ((), ())), preferred_element_type=F32)


def tn(a, b):
    return lax.dot_general(a, b, (((0,), (0,)), ((), ())), preferred_element_type=F32)


def tile_layout():
    slot = np.full((T,), -1, np.int32)
    place = np.zeros((T,), np.int32)
    for big in range(2):
        slot[big * POS : (big + 1) * POS] = big
        place[big * POS : (big + 1) * POS] = np.arange(POS)
    small = np.array([r * WIN + c for r in range(SMALL_SIDE) for c in range(SMALL_SIDE)], np.int32)
    for k in range(3):
        at = SMALL_AT + SMALL * k
        slot[at : at + SMALL] = 2 + k
        place[at : at + SMALL] = small
    return slot, place


def pair_index():
    slot, place = tile_layout()
    row, col = place // WIN, place % WIN
    half = WIN // 2
    out, where = [], []
    for block in range(2):
        r, c = (row, col) if block == 0 else ((row - half) % WIN, (col - half) % WIN)
        index = (r[:, None] - r[None, :] + WIN - 1) * (2 * WIN - 1) + c[:, None] - c[None, :] + WIN - 1
        same = (slot[:, None] == slot[None, :]) & (slot[:, None] >= 0)
        out.append(np.where(same, index, TABLE - 1).astype(np.int32))
        where.append((r * WIN + c).astype(np.int32))
    return np.stack(out), where[1]


def crop_bases(flags, crops, skipped):
    bigs, smalls, found = jnp.int32(0), jnp.int32(0), []
    for c in range(crops):
        flag = flags[c]
        third = (smalls * 11) >> 5
        big_at = (bigs >> 1) * T + (bigs & 1) * POS
        small_at = third * T + SMALL_AT + SMALL * (smalls - 3 * third)
        at = jnp.where(flag == 1, big_at, small_at)
        found.append((flag, at + jnp.where(at >= R, skipped * R, 0)))
        bigs = bigs + flag
        smalls = smalls + (1 - flag)
    return found


def landing(flags, crops, skipped, axis):
    rows = POS * crops
    dims = (rows, 1) if axis == 0 else (1, rows)
    at = lax.broadcasted_iota(jnp.int32, dims, axis)
    place = at // crops
    crop = at - place * crops
    row = place // WIN
    col = place - row * WIN
    inside = (row < SMALL_SIDE) & (col < SMALL_SIDE)
    small = jnp.where(inside, row * SMALL_SIDE + col, -T * crops)
    out = jnp.full(dims, -1, jnp.int32)
    for c, (flag, base) in enumerate(crop_bases(flags, crops, skipped)):
        out = jnp.where(crop == c, base + jnp.where(flag == 1, place, small), out)
    return out


def filled(c, skipped, chunks):
    return (c == 0) | ((c > skipped) & (c < chunks))


def empty(c, skipped):
    return (c > 0) & (c <= skipped)


def pack_kernel(crops, info, flags, tokens, cotangent, *outs):
    section = info[0]
    target = lax.broadcasted_iota(jnp.int32, (R, POS * crops), 0)
    lands = landing(flags, crops, info[1], 1)

    def chunk(t, refs, at):
        picks = (target + t * R == lands).astype(F32).astype(BF)
        packed = [nn(picks, rows[...]).astype(BF) for rows in (tokens, cotangent)]
        for r, out in enumerate(refs):
            is_last = section == SECTIONS - 1 - r

            @pl.when(is_last)
            def _():
                out[at] = packed[1]

            @pl.when(jnp.logical_not(is_last))
            def _():
                out[at] = packed[0]

    chunk(0, outs[:SECTIONS], 0)

    @pl.loop(0, outs[SECTIONS].shape[0])
    def _(t):
        chunk(t + 1, outs[SECTIONS:], t)


def pack_rows(info, flags, tokens, cotangent, chunks):
    rows, width = tokens.shape
    crops = rows // POS
    return pl.pallas_call(
        functools.partial(pack_kernel, crops),
        out_shape=[shape((1, R, width), BF)] * SECTIONS + [shape((chunks - 1, R, width), BF)] * SECTIONS,
        in_specs=[SM, SM, VM, VM],
        out_specs=[VM] * (2 * SECTIONS),
        compiler_params=pltpu.CompilerParams(vmem_limit_bytes=TINY_LIMIT),
        name="pack_rows",
    )(info, flags, tokens, cotangent)


def unpack_kernel(crops, info, flags, own, came1, came2, came3, rows_out, grad_out):
    section = info[0]
    lands = landing(flags, crops, info[1], 0)
    total = own.shape[0] * R
    target = lax.broadcasted_iota(jnp.int32, (POS * crops, total), 1)
    picks = (target == lands).astype(F32).astype(BF)
    came = (own, came1, came2, came3)
    for s in range(SECTIONS):

        @pl.when(section == s)
        def _():
            y = came[(s + 1) % SECTIONS][...].reshape(total, -1)
            rows_out[...] = nn(picks, y).astype(BF)
            grad_out[...] = nn(picks, came[s][...].reshape(total, -1))


def unpack_rows(info, flags, own, came):
    width = own.shape[2]
    crops = flags.shape[0]
    return pl.pallas_call(
        functools.partial(unpack_kernel, crops),
        out_shape=[shape((POS * crops, width), BF), shape((POS * crops, width), F32)],
        in_specs=[SM, SM] + [VM] * 4,
        out_specs=[VM, VM],
        compiler_params=pltpu.CompilerParams(vmem_limit_bytes=TINY_LIMIT),
        name="unpack_rows",
    )(info, flags, own, *came)


ROWS_AT_ONCE = 8


def onehot_rows(index, it):
    rows = index[pl.ds(it * ROWS_AT_ONCE, ROWS_AT_ONCE), :]
    entry = lax.broadcasted_iota(jnp.int32, (TABLE, T), 0)
    parts = [(entry == rows[r : r + 1, :]).astype(F32).astype(BF) for r in range(ROWS_AT_ONCE)]
    return jnp.concatenate(parts, 1)


def split3(x):
    top = x.astype(BF)
    rest = x - top.astype(F32)
    middle = rest.astype(BF)
    return top, middle, (rest - middle.astype(F32)).astype(BF)


def spread_kernel(index, table, out):
    parts = split3(table[...])

    @pl.loop(0, T // ROWS_AT_ONCE)
    def _(it):
        picks = onehot_rows(index, it)
        values = nn(parts[0], picks) + nn(parts[1], picks) + nn(parts[2], picks)
        for r in range(ROWS_AT_ONCE):
            out[:, it * ROWS_AT_ONCE + r, :] = values[:HEADS, r * T : (r + 1) * T]


def spread_table(index, table):
    return pl.pallas_call(
        spread_kernel,
        out_shape=shape((HEADS, T, T), F32),
        in_specs=[VM, VM],
        out_specs=VM,
        compiler_params=pltpu.CompilerParams(vmem_limit_bytes=TINY_LIMIT),
        name="spread_table",
    )(index, table)


def fold_kernel(index, sums, out):
    out[...] = jnp.zeros_like(out)

    @pl.loop(0, T // ROWS_AT_ONCE)
    def _(it):
        picks = onehot_rows(index, it)
        rows = jnp.concatenate([sums[:, it * ROWS_AT_ONCE + r, :] for r in range(ROWS_AT_ONCE)], 1)
        top = rows.astype(BF)
        rest = (rows - top.astype(F32)).astype(BF)
        out[...] += nt(top, picks) + nt(rest, picks)


def fold_table(index, sums):
    return pl.pallas_call(
        fold_kernel,
        out_shape=shape((HEADS, TABLE), F32),
        in_specs=[VM, VM],
        out_specs=VM,
        compiler_params=pltpu.CompilerParams(vmem_limit_bytes=TINY_LIMIT),
        name="fold_table",
    )(index, pin(sums))


def row_norm(x):
    mean = jnp.sum(x, -1, keepdims=True) * (1.0 / D)
    centered = x - mean
    var = jnp.sum(centered * centered, -1, keepdims=True) * (1.0 / D)
    inv = lax.rsqrt(var + EPSILON)
    return centered * inv, inv


def head_masks():
    lane = lax.broadcasted_iota(jnp.int32, (T, T), 1)
    return [(lane >= HEAD * h) & (lane < HEAD * (h + 1)) for h in range(GROUP)]


def spread_heads(block, masks):
    zero = jnp.zeros_like(block)
    return jnp.concatenate([jnp.where(m, block, zero) for m in masks], 0)


def gather_heads(stacked, masks):
    total = stacked[0:T]
    for h in range(1, GROUP):
        total = jnp.where(masks[h], stacked[h * T : (h + 1) * T], total)
    return total


def lanes(at, size=T):
    return pl.ds(pl.multiple_of(at, T), size)


STEP = 512
BLOCKS = FF // STEP


def attention_forward(x, n, vec, wide, w, bias, a, b, save_b, y):

    @pl.loop(0, 3)
    def _(s):
        cols = lanes(s * D, D)
        a[:, cols] = (nn(n, w[:, cols]) + wide[0:1, cols]).astype(BF)

    masks = head_masks()

    @pl.loop(0, PAIR)
    def _(t):
        rows = pl.ds(pl.multiple_of(t * T, T), T)
        for grp in range(HEADS // GROUP):
            lo = grp * T
            heads = slice(grp * GROUP, (grp + 1) * GROUP)
            q, k, v = (a[rows, lo + s * D : lo + s * D + T] for s in range(3))
            s = nt(spread_heads(q, masks), k) * SCALE + bias[heads].reshape(GROUP * T, T)
            e = jnp.exp(s - jnp.max(s, -1, keepdims=True))
            p = (e * (1.0 / jnp.sum(e, -1, keepdims=True))).astype(BF)
            b[t, heads] = p.reshape(GROUP, T, T)
            a[rows, 3 * D + lo : 3 * D + lo + T] = gather_heads(nn(p, v), masks).astype(BF)

    save_b.start()
    branch = nn(a[:, 3 * D :], w[:, 3 * D :]) + vec[2:3, :]
    y[...] = (x + branch).astype(BF)


ERF_SLOPE = 0.3275911 * SQRT_HALF
ERF_TERMS = (1.061405429, -1.453152027, 1.421413741, -0.284496736, 0.254829592)


def normal_parts(u):
    bell = jnp.exp(-0.5 * u * u)
    base = 1.0 + ERF_SLOPE * jnp.abs(u)
    t = pl.reciprocal(base, approx=True)
    t = t * (2.0 - base * t)
    poly = 0.5 * ERF_TERMS[0]
    for term in ERF_TERMS[1:]:
        poly = poly * t + 0.5 * term
    tail = poly * t * bell
    return jnp.where(u >= 0, 1.0 - tail, tail), u * (bell * INV_SQRT_TAU)


def mlp_forward(x, n, vec, wide, w, v, a, b, acc):
    acc[...] = x + vec[2:3, :]

    @pl.loop(0, BLOCKS, step=2)
    def _(j0):
        blocks = []
        for jb in (j0, j0 + 1):
            cols = lanes(jb * STEP, STEP)
            u = nn(n, w[:, cols]) + wide[0:1, cols]
            cdf, rise = normal_parts(u)
            blocks.append((jb, cols, (u * cdf).astype(BF), (cdf + rise).astype(BF)))
        part = None
        for jb, cols, act, slope in blocks:
            a[:, cols] = act
            for t in range(PAIR):
                for i in range(STEP // T):
                    b[t, jb * (STEP // T) + i] = slope[t * T : (t + 1) * T, i * T : (i + 1) * T]
            term = nn(act, v[cols, :])
            part = term if part is None else part + term
        acc[...] += part


def forward_kernel(both, info, slot, vec, wide, bias, w, *refs):
    v = refs[0] if both else None
    p0, p1, p2, p3, came = refs[both : both + 5]
    y, *kept = refs[both + 13 :]
    xs, keep_n, keep_a, keep_b, *outs = kept[:8]
    x_in, n, a, b, acc, parts, sems = kept[8:]
    chunks = xs.shape[0]
    width = parts.shape[-1]
    section, skipped = info[0], info[1]
    c = slot[0] - section

    def copy(source, target, k):
        return pltpu.make_async_copy(source, target, sems.at[k])

    save_x, save_n = copy(x_in, xs.at[c], 0), copy(n, keep_n.at[c], 1)
    save_a, save_b = copy(a, keep_a.at[c], 2), copy(b, keep_b.at[c], 3)
    put = [copy(parts.at[d], outs[(d + 1) % SECTIONS].at[c], 4 + d) for d in range(SECTIONS)]

    @pl.when(filled(c, skipped, chunks))
    def _():
        @pl.when(section == 0)
        def _():
            bring = [copy(p.at[c - slot[1]], parts.at[d], 4 + d) for d, p in enumerate((p0, p3, p2, p1))]
            for one in bring:
                one.start()
            for one in bring:
                one.wait()
            x_in[...] = jnp.concatenate([parts[d] for d in range(SECTIONS)], -1)

        @pl.when(section != 0)
        def _():
            bring = copy(came, x_in, 0)
            bring.start()
            bring.wait()

        save_x.start()
        x = x_in[...].astype(F32)
        raw, _ = row_norm(x)
        normed = (raw * vec[0:1, :] + vec[1:2, :]).astype(BF)
        n[...] = normed
        save_n.start()

        @pl.when(section % 2 == 0)
        def _():
            attention_forward(x, normed, vec, wide, w, bias, a, b, save_b, y)

        if both:

            @pl.when(section % 2 == 1)
            def _():
                mlp_forward(x, normed, vec, wide, w, v, a, b, acc)
                save_b.start()
                y[...] = acc[...].astype(BF)

        save_a.start()

        @pl.when(both & (section == SECTIONS - 1))
        def _():
            for d in range(SECTIONS):
                parts[d] = y[:, d * width : (d + 1) * width]
                put[d].start()
            for d in range(SECTIONS):
                put[d].wait()

        save_x.wait()
        save_n.wait()
        save_a.wait()
        save_b.wait()

    @pl.when((section == SECTIONS - 1) & empty(c, skipped))
    def _():
        parts[...] = jnp.zeros_like(parts)
        for d in range(SECTIONS):
            put[d].start()
        for d in range(SECTIONS):
            put[d].wait()


ANY = pl.BlockSpec(memory_space=pl.ANY)


def far(x):
    return pltpu.with_memory_space_constraint(x, pltpu.HBM)


def run_forward(info, slot, pieces, came, vec, wide, w, v, bias, kept):
    count = len(kept)
    width = pieces[0].shape[-1]
    both = v is not None
    weights = [pin(w), pin(v)] if both else [pin(w)]
    outs = pl.pallas_call(
        functools.partial(forward_kernel, both),
        out_shape=[shape((R, D), BF)] + [like(r) for r in kept],
        in_specs=[SM, SM] + [VM] * (4 + both) + [ANY] * (5 + count),
        out_specs=[VM] + [ANY] * count,
        scratch_shapes=[
            pltpu.VMEM((R, D), BF),
            pltpu.VMEM((R, D), BF),
            pltpu.VMEM((R, FF), BF),
            pltpu.VMEM((PAIR, HEADS, T, T), BF),
            pltpu.VMEM((R, D), F32),
            pltpu.VMEM((SECTIONS, R, width), BF),
            pltpu.SemaphoreType.DMA((4 + SECTIONS,)),
        ],
        input_output_aliases={11 + both + i: 1 + i for i in range(count)},
        compiler_params=pltpu.CompilerParams(vmem_limit_bytes=SMALL_LIMIT),
        name="section_forward",
    )(info, slot, vec, wide, pin(bias), *weights, *pieces, came, *[far(r) for r in kept])
    return outs[0], list(outs[1:])


def norm_backward(x, g, dn, vec, sums, gx):
    raw, inv = row_norm(x)
    sums[0:1, :] += jnp.sum(dn * raw, 0, keepdims=True)
    sums[1:2, :] += jnp.sum(dn, 0, keepdims=True)
    sums[2:3, :] += jnp.sum(g, 0, keepdims=True)
    s = dn * vec[0:1, :]
    m1 = jnp.sum(s, -1, keepdims=True) * (1.0 / D)
    m2 = jnp.sum(s * raw, -1, keepdims=True) * (1.0 / D)
    gx[...] = (g + inv * (s - m1 - raw * m2)).astype(BF)


def attention_backward(g, w, a, b, bring_a, bring_b, d, acc, save_d, dsum):
    masks = head_masks()
    bring_a.start()
    d[:, 3 * D :] = g
    d[:, 0:D] = nt(g, w[:, 3 * D :]).astype(BF)
    bring_a.wait()
    bring_b.wait()

    @pl.loop(0, PAIR)
    def _(t):
        rows = pl.ds(pl.multiple_of(t * T, T), T)
        for grp in range(HEADS // GROUP):
            lo = grp * T
            heads = slice(grp * GROUP, (grp + 1) * GROUP)
            q, k, v = (a[rows, lo + s * D : lo + s * D + T] for s in range(3))
            p = b[t, heads].reshape(GROUP * T, T)
            do_heads = spread_heads(d[rows, lo : lo + T], masks)
            dv = tn(p, do_heads)
            pf = p.astype(F32)
            pdp = pf * nt(do_heads, v)
            ds = (pdp - pf * jnp.sum(pdp, -1, keepdims=True)).astype(BF)
            dsum[heads] += ds.astype(F32).reshape(GROUP, T, T)
            dq = gather_heads(nn(ds, k), masks) * SCALE
            dk = tn(ds, spread_heads(q, masks)) * SCALE
            d[rows, lo : lo + T] = dq.astype(BF)
            d[rows, D + lo : D + lo + T] = dk.astype(BF)
            d[rows, 2 * D + lo : 2 * D + lo + T] = dv.astype(BF)

    save_d.start()
    acc[...] = jnp.zeros_like(acc)

    @pl.loop(0, 3)
    def _(s):
        cols = lanes(s * D, D)
        acc[...] += nt(d[:, cols], w[:, cols])


def mlp_backward(g, w, v, b, bring_b, d, acc):
    acc[...] = jnp.zeros_like(acc)
    bring_b.wait()

    @pl.loop(0, BLOCKS, step=2)
    def _(j0):
        blocks = []
        for jb in (j0, j0 + 1):
            cols = lanes(jb * STEP, STEP)
            da = nt(g, v[cols, :]).astype(BF).astype(F32)
            slope = jnp.concatenate(
                [
                    jnp.concatenate([b[t, jb * (STEP // T) + i] for i in range(STEP // T)], 1)
                    for t in range(PAIR)
                ],
                0,
            )
            blocks.append((cols, (da * slope.astype(F32)).astype(BF)))
        part = None
        for cols, du in blocks:
            d[:, cols] = du
            term = nt(du, w[:, cols])
            part = term if part is None else part + term
        acc[...] += part


def seed_rows(scales, c):
    row = lax.broadcasted_iota(jnp.int32, (T, 1), 0)
    parts = []
    for t in range(PAIR):
        base = (c * PAIR + t) * 8
        out = jnp.full((T, 1), scales[base], F32)
        for k, at in enumerate([POS] + [SMALL_AT + SMALL * i for i in range(3)]):
            out = jnp.where(row >= at, scales[base + 1 + k], out)
        parts.append(out)
    return jnp.concatenate(parts, 0)


def backward_kernel(info, slot, scales, vec, w, v, dsum_in, sums_in, p0, p1, p2, p3, came, *refs):
    gx, dsum, sums, *kept = refs[9:]
    xs, keep_a, keep_b, gs, keep_d, *outs = kept[:9]
    x_in, g_tile, a, b, d, acc, parts, sems = kept[9:]
    chunks = xs.shape[0]
    width = parts.shape[-1]
    section, skipped = info[0], info[1]
    c = slot[0] - (SECTIONS - 1 - section)

    def copy(source, target, k):
        return pltpu.make_async_copy(source, target, sems.at[k])

    bring_x, bring_a, bring_b = copy(xs.at[c], x_in, 0), copy(keep_a.at[c], a, 1), copy(keep_b.at[c], b, 2)
    save_g, save_d = copy(g_tile, gs.at[c], 3), copy(d, keep_d.at[c], 4)
    put = [copy(parts.at[k], outs[k].at[c], 5 + k) for k in range(SECTIONS)]

    @pl.when(filled(c, skipped, chunks))
    def _():
        @pl.when(section == SECTIONS - 1)
        def _():
            bring = [copy(p.at[c - slot[1]], parts.at[k], 5 + k) for k, p in enumerate((p3, p2, p1, p0))]
            for one in bring:
                one.start()
            bring_b.start()
            for one in bring:
                one.wait()
            seed = jnp.concatenate([parts[k] for k in range(SECTIONS)], -1).astype(F32)
            g_tile[...] = (seed * seed_rows(scales, c)).astype(BF)

        @pl.when(section != SECTIONS - 1)
        def _():
            bring = copy(came, g_tile, 3)
            bring.start()
            bring_b.start()
            bring.wait()

        bring_x.start()
        save_g.start()

        @pl.when(c == 0)
        def _():
            dsum[...] = jnp.zeros_like(dsum)
            sums[...] = jnp.zeros_like(sums)

        g = g_tile[...]

        @pl.when(section % 2 == 0)
        def _():
            attention_backward(g, w, a, b, bring_a, bring_b, d, acc, save_d, dsum)

        @pl.when(section % 2 == 1)
        def _():
            mlp_backward(g, w, v, b, bring_b, d, acc)
            save_d.start()

        bring_x.wait()
        norm_backward(x_in[...].astype(F32), g.astype(F32), acc[...], vec, sums, gx)

        @pl.when(section == 0)
        def _():
            for k in range(SECTIONS):
                parts[k] = gx[:, k * width : (k + 1) * width]
                put[k].start()
            for k in range(SECTIONS):
                put[k].wait()

        save_g.wait()
        save_d.wait()

    @pl.when((section == 0) & empty(c, skipped))
    def _():
        parts[...] = jnp.zeros_like(parts)
        for k in range(SECTIONS):
            put[k].start()
        for k in range(SECTIONS):
            put[k].wait()


def run_backward(info, slot, scales, pieces, came, vec, w, v, dsum, sums, kept):
    count = len(kept)
    width = pieces[0].shape[-1]
    outs = pl.pallas_call(
        backward_kernel,
        out_shape=[shape((R, D), BF)] + [like(r) for r in (dsum, sums, *kept)],
        in_specs=[SM, SM, SM] + [VM] * 5 + [ANY] * (5 + count),
        out_specs=[VM] * 3 + [ANY] * count,
        scratch_shapes=[
            pltpu.VMEM((R, D), BF),
            pltpu.VMEM((R, D), BF),
            pltpu.VMEM((R, FF), BF),
            pltpu.VMEM((PAIR, HEADS, T, T), BF),
            pltpu.VMEM((R, FF), BF),
            pltpu.VMEM((R, D), F32),
            pltpu.VMEM((SECTIONS, R, width), BF),
            pltpu.SemaphoreType.DMA((5 + SECTIONS,)),
        ],
        input_output_aliases={6: 1, 7: 2} | {13 + i: 3 + i for i in range(count)},
        compiler_params=pltpu.CompilerParams(vmem_limit_bytes=SMALL_LIMIT),
        name="section_backward",
    )(
        info, slot, scales, vec, pin(w), pin(v), pin(dsum), pin(sums), *pieces, came,
        *[far(r) for r in kept],
    )
    return outs[0], outs[1], outs[2], list(outs[3:])


def make_room(dims):
    def body(*refs):
        pass

    return pl.pallas_call(
        body,
        out_shape=[pltpu.VMEM(d, k) if near else pltpu.HBM(d, k) for d, k, near in dims],
        out_specs=[VM if near else ANY for _, _, near in dims],
        compiler_params=pltpu.CompilerParams(vmem_limit_bytes=TINY_LIMIT),
        name="make_room",
    )()


def clear(ref, skipped, *at):
    @pl.loop(1, skipped + 1)
    def _(t):
        ref[(*at, t)] = jnp.zeros(ref.shape[-2:], BF)


def in_kernel(info, keep_n, keep_a, keep_d, top, low, wide_sums, turned, n, a, d, out, in_sems, out_sems):
    chunks = keep_n.shape[0]
    rows = chunks * R
    mlp, skipped = info[0] % 2, info[1]
    part = D // 2

    def bring(jb):
        return pltpu.make_async_copy(keep_d.at[:, :, pl.ds(jb * STEP, STEP)], d.at[jb], in_sems.at[jb])

    def put(jb):
        to = pl.ds(jb * STEP, STEP)
        return [
            pltpu.make_async_copy(
                out.at[jb % 2, pl.ds(k * part, part)], ref.at[:, to], out_sems.at[2 * (jb % 2) + k]
            )
            for k, ref in enumerate((top, low))
        ]

    bring_n = pltpu.make_async_copy(keep_n, n, in_sems.at[BLOCKS])
    bring_a = pltpu.make_async_copy(keep_a.at[:, :, pl.ds(3 * D, D)], a, in_sems.at[BLOCKS + 1])
    bring_n.start()
    for jb in range(BLOCKS):
        bring(jb).start()
    bring_a.start()
    bring_n.wait()
    clear(n, skipped)
    turned[0] = n[...].reshape(rows, D).T
    bring_a.wait()
    clear(a, skipped)

    @pl.when(mlp == 0)
    def _():
        turned[1] = a[...].reshape(rows, D).T

    @pl.when(mlp == 1)
    def _():
        turned[1] = turned[0]

    @pl.loop(0, BLOCKS)
    def _(jb):
        bring(jb).wait()
        clear(d, skipped, jb)
        block = d[jb].reshape(rows, STEP)
        wide_sums[0:1, lanes(jb * STEP, STEP)] = jnp.sum(block.astype(F32), 0, keepdims=True)

        @pl.when(jb >= 2)
        def _():
            for one in put(jb - 2):
                one.wait()

        half = STEP // 2
        for k in range(2):
            late = (jb * 2 + k >= 3 * D // half).astype(jnp.int32)
            out[jb % 2, :, k * half : (k + 1) * half] = nn(
                turned[late], block[:, k * half : (k + 1) * half]
            ).astype(BF)
        for one in put(jb):
            one.start()

    for jb in (BLOCKS - 2, BLOCKS - 1):
        for one in put(jb):
            one.wait()


def in_grads(info, keep_n, keep_a, keep_d):
    chunks = keep_n.shape[0]
    dma = pltpu.SemaphoreType.DMA
    return pl.pallas_call(
        in_kernel,
        out_shape=[shape((D // 2, FF), BF)] * 2 + [shape((8, FF), F32)],
        in_specs=[SM] + [ANY] * 3,
        out_specs=[ANY, ANY, VM],
        scratch_shapes=[
            pltpu.VMEM((2, D, chunks * R), BF),
            pltpu.VMEM(keep_n.shape, BF),
            pltpu.VMEM(keep_n.shape, BF),
            pltpu.VMEM((BLOCKS, chunks, R, STEP), BF),
            pltpu.VMEM((2, D, STEP), BF),
            dma((BLOCKS + 2,)),
            dma((4,)),
        ],
        compiler_params=pltpu.CompilerParams(vmem_limit_bytes=LIMIT),
        name="in_grads",
    )(info, *[far(r) for r in (keep_n, keep_a, keep_d)])


def down_kernel(info, keep_a, gs, grad, a, g, out, in_sems, out_sems):
    chunks = gs.shape[0]
    rows = chunks * R
    mlp, skipped = info[0] % 2, info[1]

    def bring(jb):
        return pltpu.make_async_copy(keep_a.at[:, :, pl.ds(jb * STEP, STEP)], a.at[jb], in_sems.at[jb])

    def put(jb):
        return pltpu.make_async_copy(out.at[jb % 2], grad.at[pl.ds(jb * STEP, STEP), :], out_sems.at[jb % 2])

    @pl.when(mlp == 1)
    def _():
        bring_g = pltpu.make_async_copy(gs, g, in_sems.at[BLOCKS])
        bring_g.start()
        for jb in range(BLOCKS):
            bring(jb).start()
        bring_g.wait()
        clear(g, skipped)
        flat_g = g[...].reshape(rows, D)

        @pl.loop(0, BLOCKS)
        def _(jb):
            bring(jb).wait()
            clear(a, skipped, jb)

            @pl.when(jb >= 2)
            def _():
                put(jb - 2).wait()

            out[jb % 2] = tn(a[jb].reshape(rows, STEP), flat_g).astype(BF)
            put(jb).start()

        for jb in (BLOCKS - 2, BLOCKS - 1):
            put(jb).wait()


def down_grads(info, keep_a, gs):
    chunks = gs.shape[0]
    dma = pltpu.SemaphoreType.DMA
    return pl.pallas_call(
        down_kernel,
        out_shape=shape((FF, D), BF),
        in_specs=[SM] + [ANY] * 2,
        out_specs=ANY,
        scratch_shapes=[
            pltpu.VMEM((BLOCKS, chunks, R, STEP), BF),
            pltpu.VMEM(gs.shape, BF),
            pltpu.VMEM((2, STEP, D), BF),
            dma((BLOCKS + 1,)),
            dma((2,)),
        ],
        compiler_params=pltpu.CompilerParams(vmem_limit_bytes=LIMIT),
        name="down_grads",
    )(info, far(keep_a), far(gs))


def swapped(block, axis, bit):
    size = lax.axis_size(axis)
    return lax.ppermute(block, axis, [(i, i ^ bit) for i in range(size)])


def butterfly(block, axis):
    size = lax.axis_size(axis)
    if size & (size - 1):
        return lax.psum(block, axis)
    bit = 1
    while bit < size:
        block = block + swapped(block, axis, bit)
        bit *= 2
    return block


def pair_sum_kernel(mine, came, own):
    own[...] = (mine[...].astype(F32) + came[...].astype(F32)).astype(BF)


def pair_sum(mine, came):
    return pl.pallas_call(
        pair_sum_kernel,
        out_shape=pltpu.VMEM(mine.shape, BF),
        in_specs=[VM, VM],
        out_specs=VM,
        compiler_params=pltpu.CompilerParams(vmem_limit_bytes=TINY_LIMIT),
        name="pair_sum",
    )(mine, came)


def line_kernel(stream, with_down, step, rank, came, top, low, *refs):
    down = refs[0] if with_down else None
    send = refs[with_down]
    chunk = step[0] - rank[0]
    at = stream * FF // 2

    def put(source, row, cuts):
        for k, (down_by, col) in enumerate(cuts):
            rows = pl.ds(pl.multiple_of(row + down_by, LINE), LINE)
            value = source[rows, col : col + D]

            @pl.when(rank[0] == 0)
            def _():
                send[k] = value

            @pl.when(rank[0] > 0)
            def _():
                send[k] = (value.astype(F32) + came[k].astype(F32)).astype(BF)

    side_by_side = ((0, at), (0, at + D))
    for half, source in enumerate((top, low)):
        first = half * IN_CHUNKS // 2

        @pl.when((chunk >= first) & (chunk < first + IN_CHUNKS // 2))
        def _():
            put(source, (chunk - first) * LINE, side_by_side)

    if with_down:

        @pl.when((chunk >= IN_CHUNKS) & (chunk < CHUNKS))
        def _():
            put(down, (chunk - IN_CHUNKS + stream * DOWN_CHUNKS) * 2 * LINE, ((0, 0), (LINE, 0)))


class LineSum:
    def __init__(self, place, core, length, stream):
        self.length, self.stream = length, stream
        self.rank = jnp.where(core == 0, place, length - 1 - place).reshape(1)
        self.came = jnp.zeros((2, LINE, D), BF)
        self.sends = CHUNKS + length - 2
        self.route = [(2 * z, 2 * z + 2) for z in range(length - 1)]
        self.route += [(2 * z + 3, 2 * z + 1) for z in range(length - 1)]
        self.kept = []

    def advance(self, step, top, low, down):
        with_down = step >= IN_CHUNKS
        owns = [top, low, down] if with_down else [top, low]
        send = pl.pallas_call(
            functools.partial(line_kernel, self.stream, with_down),
            out_shape=like(self.came),
            in_specs=[SM, SM] + [VM] * (1 + len(owns)),
            out_specs=VM,
            compiler_params=pltpu.CompilerParams(vmem_limit_bytes=TINY_LIMIT),
            name="line_step",
        )(np.array([step], np.int32), self.rank, self.came, *[pin(x) for x in owns])
        self.came = lax.ppermute(send, "dp", self.route)
        self.kept.append(self.came)


def collect_kernel(length, where, rank, *refs):
    kept, (out, zero, sems) = refs[:-3], refs[-3:]
    zero[...] = jnp.zeros_like(zero)

    def move(item, k, ref):
        row, col = where[item][1][k]
        to = out.at[pl.ds(row, LINE), pl.ds(col, D)]
        return pltpu.make_async_copy(ref, to, sems.at[item, k])

    for item, (index, _) in enumerate(where):
        for k in range(2):
            pl.when(rank[0] == 0)(move(item, k, zero).start)
            for r in range(1, length):
                pl.when(rank[0] == r)(move(item, k, kept[index[r - 1]].at[k]).start)
    for item in range(len(where)):
        for k in range(2):
            move(item, k, zero).wait()


def collect_rows(streams, first, count, dims):
    length = streams[0].length
    kept, where = [], []
    for k, stream in enumerate(streams):
        for c in range(count):
            index = []
            for r in range(1, length):
                index.append(len(kept))
                kept.append(stream.kept[first + c + r - 1])
            if dims[1] == FF:
                spots = [(c * LINE, k * FF // 2), (c * LINE, k * FF // 2 + D)]
            else:
                spots = [((c + k * count) * 2 * LINE + half * LINE, 0) for half in range(2)]
            where.append((index, spots))
    return pl.pallas_call(
        functools.partial(collect_kernel, length, where),
        out_shape=pltpu.VMEM(dims, BF),
        in_specs=[SM] + [ANY] * len(kept),
        out_specs=VM,
        scratch_shapes=[pltpu.VMEM((LINE, D), BF), pltpu.SemaphoreType.DMA((len(where), 2))],
        compiler_params=pltpu.CompilerParams(vmem_limit_bytes=TINY_LIMIT),
        name="collect_rows",
    )(streams[0].rank, *kept)


def added(*parts):
    return sum(p.astype(F32) for p in parts)


def after(x, *first):
    return lax.optimization_barrier((x, *first))[0]


def flat_rows(x):
    return x.transpose(1, 0, 2).reshape(-1, x.shape[2])


def stacked_rows(x, crops):
    return x.reshape(POS, crops, -1).transpose(1, 0, 2)


def on_device(
    tokens,
    cotangent,
    in_weight,
    down_weight,
    norm_gain,
    norm_shift,
    out_bias,
    qv_bias,
    fc1_bias,
    rel_table,
    shift_regions,
    crop_global,
    micro_of,
):
    section = lax.axis_index("pipe")
    dp_index = lax.axis_index("dp")
    core, place = dp_index % 2, dp_index // 2
    dp_size = lax.axis_size("dp")
    mlp = section % 2
    block = section // 2
    crops = tokens.shape[0]
    chunks = (crops + 2 * PAIR - 1) // (2 * PAIR)
    last = SECTIONS - 1

    half = FF // 4
    sent = lax.dynamic_slice_in_dim(down_weight[0], core * half, half, 0)
    mine = lax.ppermute(sent, "pipe", [(s, s + 1) for s in range(0, SECTIONS, 2)])

    bigs_all = jnp.sum(crop_global)
    needed = jnp.maximum(
        (bigs_all + 2 * PAIR - 1) // (2 * PAIR), (crops - bigs_all + 3 * PAIR - 1) // (3 * PAIR)
    )
    info = jnp.stack([section, chunks - needed, core]).astype(jnp.int32)
    packs = pack_rows(info, crop_global, flat_rows(tokens), flat_rows(cotangent), chunks)
    pieces = [
        [packs[at]]
        + [
            lax.ppermute(packs[at + r], "pipe", [(SECTIONS - r, 0), (last - r, last)])
            for r in range(1, SECTIONS)
        ]
        for at in (0, SECTIONS)
    ]

    w = in_weight[0]

    vec = jnp.stack([norm_gain[section], norm_shift[section], out_bias[section]])
    qv = qv_bias[block]
    wide_attention = jnp.concatenate([qv[0], jnp.zeros((D,), F32), qv[1], jnp.zeros((D,), F32)])
    wide = jnp.where(mlp == 1, fc1_bias[block], wide_attention)[None]

    both, rolled = pair_index()
    regions = jnp.where(block == 1, shift_regions[rolled], 0)
    index = jnp.where(block == 1, both[1], both[0])
    index = jnp.where(regions[:, None] == regions[None, :], index, TABLE - 1)
    table = jnp.pad(
        rel_table[block].T, ((0, 32 - HEADS), (0, TABLE - SPAN)), constant_values=((0, 0), (0, NEGATIVE))
    )
    bias = spread_table(after(index, packs[0]), table)

    member = (micro_of == jnp.arange(MICRO, dtype=jnp.int32)[None, :]).astype(F32)
    crop_rows = jnp.where(crop_global == 1, POS, SMALL).astype(F32)
    counts = jnp.sum(member * crop_rows[:, None], 0, keepdims=True)
    count_rounds = [1 << k for k in range((dp_size - 1).bit_length())]
    before = np.tril(np.ones((crops, crops), np.int32), -1)
    bigs = jnp.sum(before * crop_global[None, :], 1)
    smalls = jnp.arange(crops, dtype=jnp.int32) - bigs
    entry = jnp.where(crop_global == 1, bigs // 2 * 8 + bigs % 2, smalls // 3 * 8 + 2 + smalls % 3)
    entry = entry + jnp.where(entry >= 8 * PAIR, 8 * PAIR * info[1], 0)

    def tile_scales(counts):
        scales = jnp.sum(member * (jnp.sum(counts) / (MICRO * counts)), 1)
        here = entry[:, None] == jnp.arange(chunks * PAIR * 8, dtype=jnp.int32)[None, :]
        return jnp.sum(jnp.where(here, scales[:, None], 0.0), 0)

    width = tokens.shape[2]
    room = make_room(
        [((HEADS, T, T), F32, True), ((8, D), F32, True)]
        + [((chunks, R, D), BF, False)] * 3
        + [((chunks, R, FF), BF, False)] * 2
        + [((chunks, PAIR, HEADS, T, T), BF, False)]
        + [((chunks, R, width), BF, False)] * 4
    )
    dsum, sums, xs, keep_n, gs, keep_a, keep_d, keep_b, *outs = room
    slots = chunks + last
    came_f = came_b = jnp.zeros((R, D), BF)
    down_pipe = [(s, s + 1) for s in range(last)]
    up_pipe = [(s, s - 1) for s in range(1, SECTIONS)]

    v = None
    for i in range(slots + last):
        if i < slots:
            part = 0 if i == 0 else 1
            y, (xs, keep_n, keep_a, keep_b, *outs) = run_forward(
                info, np.array([i, part], np.int32), pieces[part], came_f, vec, wide, w, v, bias,
                [xs, keep_n, keep_a, keep_b, *outs],
            )
            if i < slots - 1:
                came_f = lax.ppermute(y, "pipe", down_pipe)
            if i == 0:
                mine = after(mine, y)
                other = swapped(mine, "dp", 1)
                v = jnp.concatenate(
                    [down_weight[0], jnp.where(core == 0, mine, other), jnp.where(core == 0, other, mine)], 0
                )
            if i < last:
                take = -(-len(count_rounds) // last)
                for bit in count_rounds[i * take : (i + 1) * take]:
                    counts = counts + swapped(after(counts, y), "dp", bit)
        if i == last:
            scales = tile_scales(counts)
        if i >= last:
            part = 0 if i == last else 1
            gx, dsum, sums, (xs, keep_a, keep_b, gs, keep_d, *outs) = run_backward(
                info, np.array([i - last, part], np.int32), scales, pieces[part], came_b, vec, w, v,
                dsum, sums, [xs, keep_a, keep_b, gs, keep_d, *outs],
            )
            if i < slots + last - 1:
                came_b = lax.ppermute(gx, "pipe", up_pipe)

    v_grad = down_grads(info, keep_a, gs)
    route = [
        (s * dp_size + i, s * dp_size + (i ^ 1)) for s in range(1, SECTIONS, 2) for i in range(dp_size)
    ]
    v_came = lax.ppermute(v_grad, ("pipe", "dp"), route)
    *w_grad, wide_sums = in_grads(info, after(keep_n, v_grad), keep_a, keep_d)
    w_came = [swapped(x, "dp", 1) for x in w_grad]
    at = FF // 2 + half * core
    v_part = added(*[lax.dynamic_slice_in_dim(x, at, half, 0) for x in (v_grad, v_came)]).astype(BF)
    v_back = lax.ppermute(v_part, "pipe", [(s + 1, s) for s in range(0, SECTIONS, 2)])
    rel_grad = fold_table(index, after(dsum, w_grad[0]))
    w_own = [pair_sum(x, y) for x, y in zip(w_grad, w_came)]

    length = dp_size // 2
    streams = [LineSum(place, core, length, k) for k in range(2)]
    d_own = None
    narrow = jnp.where(
        mlp == 1,
        wide_sums[0],
        jnp.concatenate([wide_sums[0, :D], wide_sums[0, 2 * D : 3 * D], jnp.zeros((2 * D,), F32)]),
    )
    packed = jnp.concatenate([sums[:3].reshape(-1), narrow, rel_grad[:, :SPAN].reshape(-1)])
    rounds = [("dp", 1 << k) for k in range((dp_size - 1).bit_length())]
    rounds += [("pick", 0)] + [("pipe", 1), ("pipe", 2)]
    came = []
    due = [[], []]
    waiting = None
    w_done = streams[0].sends - DOWN_CHUNKS
    for step in range(streams[0].sends):
        if step == IN_CHUNKS - 1:
            v_back = after(v_back, streams[0].came)
            v_other = swapped(v_back, "dp", 1)
        if step == IN_CHUNKS:
            v_high = jnp.concatenate(
                [jnp.where(core == 0, v_back, v_other), jnp.where(core == 0, v_other, v_back)], 0
            )
            v_low = added(v_grad[: FF // 2], v_came[: FF // 2]).astype(BF)
            d_own = jnp.where(mlp == 1, v_low, v_high)
        streams[0].came = after(streams[0].came, *due.pop(0))
        started = []
        for stream in streams:
            stream.advance(step, *w_own, d_own)
        now = streams[0].came if step == 0 else streams[0].kept[step - 1]
        if 0 < step <= last:
            came.append(lax.ppermute(after(outs[step], now), "pipe", [(last, step - 1), (0, step)]))
            started.append(came[-1])
        if waiting is not None:
            packed = packed + after(waiting, now)
            waiting = None
            started.append(packed)
        if step > 0 and rounds:
            axis, bit = rounds.pop(0)
            packed = after(packed, now)
            if axis == "pick":
                packed = (jnp.arange(SECTIONS) == section).astype(F32)[:, None] * packed[None]
                axis, bit = rounds.pop(0)
            waiting = swapped(packed, axis, bit)
        if step == last + 2:
            rows_flat, grads_flat = unpack_rows(info, after(crop_global, now), outs[0], came)
            started.append(rows_flat)
        if step == w_done:
            w_came = collect_rows(streams, 0, IN_CHUNKS, (D, FF))
            w_other = swapped(w_came, "dp", 1)
        due.append(started)
    if waiting is not None:
        packed = packed + waiting
    for axis, bit in rounds:
        if axis == "pick":
            packed = (jnp.arange(SECTIONS) == section).astype(F32)[:, None] * packed[None]
        else:
            packed = packed + swapped(packed, axis, bit)
    output_rows, tokens_grad = stacked_rows(rows_flat, crops), stacked_rows(grads_flat, crops)

    gain_grad = packed[:, :D]
    shift_grad = packed[:, D : 2 * D]
    outbias_grad = packed[:, 2 * D : 3 * D]
    qv_grad = packed[0::2, 3 * D : 5 * D].reshape(2, 2, D)
    first_grad = packed[1::2, 3 * D : 3 * D + FF]
    rel_out = packed[0::2, 3 * D + FF :].reshape(2, HEADS, SPAN).transpose(0, 2, 1)

    in_grad = added(jnp.concatenate(w_own, 0), w_came, w_other)
    streams[0].rank = after(streams[0].rank, in_grad)
    d_came = collect_rows(streams, IN_CHUNKS, DOWN_CHUNKS, (FF // 2, D))
    down_grad = added(d_own, d_came, swapped(d_came, "dp", 1))
    return (
        output_rows,
        tokens_grad,
        in_grad[None],
        down_grad[None],
        gain_grad,
        shift_grad,
        outbias_grad,
        qv_grad,
        first_grad,
        rel_out,
    )


def solution(mesh):
    return jax.shard_map(
        on_device,
        mesh=mesh,
        in_specs=(
            P("dp", None, "pipe"),
            P("dp", None, "pipe"),
            P("pipe", None, None),
            P("pipe", None, None),
            P(),
            P(),
            P(),
            P(),
            P(),
            P(),
            P(),
            P("dp"),
            P("dp", None),
        ),
        out_specs=(
            P("dp", None, "pipe"),
            P("dp", None, "pipe"),
            P("pipe", None, None),
            P("pipe", None, None),
            P(),
            P(),
            P(),
            P(),
            P(),
            P(),
        ),
        check_vma=False,
    )
```

```python
import functools

import jax
import jax.numpy as jnp
import numpy as np
from jax import lax
from jax.experimental import pallas as pl
from jax.experimental.pallas import tpu as pltpu
from jax.sharding import PartitionSpec as P

HEADS = 24
HEAD = 32
FF = 3072
D = 768
WIN = 7
SMALL_SIDE = 3
SECTIONS = 4
MICRO = 4
POS = 49
SPAN = 169
SMALL = SMALL_SIDE * SMALL_SIDE

T = 128
PAIR = 2
R = PAIR * T
SMALL_AT = 2 * POS
GROUP = 4
TABLE = 256
IN_CHUNKS = 4
DOWN_CHUNKS = 2
CHUNKS = IN_CHUNKS + DOWN_CHUNKS
LINE = D // IN_CHUNKS

EPSILON = 1e-05
NEGATIVE = -1e30
SQRT_HALF = 0.7071067811865476
INV_SQRT_TAU = 0.3989422804014327
SCALE = HEAD**-0.5
BF = jnp.bfloat16
F32 = jnp.float32
VM = pl.BlockSpec(memory_space=pltpu.VMEM)
SM = pl.BlockSpec(memory_space=pltpu.SMEM)
LIMIT = 17 << 20
SMALL_LIMIT = 13 << 20
TINY_LIMIT = 8 << 20


LITTLE = pl.CostEstimate(flops=0, transcendentals=0, bytes_accessed=1024)


def pin(x):
    return pltpu.with_memory_space_constraint(x, pltpu.VMEM)


def like(x):
    return jax.ShapeDtypeStruct(x.shape, x.dtype)


def shape(dims, kind):
    return jax.ShapeDtypeStruct(dims, kind)


def nn(a, b):
    return lax.dot_general(a, b, (((1,), (0,)), ((), ())), preferred_element_type=F32)


def nt(a, b):
    return lax.dot_general(a, b, (((1,), (1,)), ((), ())), preferred_element_type=F32)


def tn(a, b):
    return lax.dot_general(a, b, (((0,), (0,)), ((), ())), preferred_element_type=F32)


def tile_layout():
    slot = np.full((T,), -1, np.int32)
    place = np.zeros((T,), np.int32)
    for big in range(2):
        slot[big * POS : (big + 1) * POS] = big
        place[big * POS : (big + 1) * POS] = np.arange(POS)
    small = np.array([r * WIN + c for r in range(SMALL_SIDE) for c in range(SMALL_SIDE)], np.int32)
    for k in range(3):
        at = SMALL_AT + SMALL * k
        slot[at : at + SMALL] = 2 + k
        place[at : at + SMALL] = small
    return slot, place


def pair_index():
    slot, place = tile_layout()
    row, col = place // WIN, place % WIN
    half = WIN // 2
    out, where = [], []
    for block in range(2):
        r, c = (row, col) if block == 0 else ((row - half) % WIN, (col - half) % WIN)
        index = (r[:, None] - r[None, :] + WIN - 1) * (2 * WIN - 1) + c[:, None] - c[None, :] + WIN - 1
        same = (slot[:, None] == slot[None, :]) & (slot[:, None] >= 0)
        out.append(np.where(same, index, TABLE - 1).astype(np.int32))
        where.append((r * WIN + c).astype(np.int32))
    return np.stack(out), where[1]


def crop_bases(flags, crops):
    bigs, smalls, found = jnp.int32(0), jnp.int32(0), []
    for c in range(crops):
        flag = flags[c]
        third = (smalls * 11) >> 5
        big_at = (bigs >> 1) * T + (bigs & 1) * POS
        small_at = third * T + SMALL_AT + SMALL * (smalls - 3 * third)
        found.append((flag, jnp.where(flag == 1, big_at, small_at)))
        bigs = bigs + flag
        smalls = smalls + (1 - flag)
    return found


def landing(flags, crops, axis):
    rows = POS * crops
    dims = (rows, 1) if axis == 0 else (1, rows)
    at = lax.broadcasted_iota(jnp.int32, dims, axis)
    place = at // crops
    crop = at - place * crops
    row = place // WIN
    col = place - row * WIN
    inside = (row < SMALL_SIDE) & (col < SMALL_SIDE)
    small = jnp.where(inside, row * SMALL_SIDE + col, -T * crops)
    out = jnp.full(dims, -1, jnp.int32)
    for c, (flag, base) in enumerate(crop_bases(flags, crops)):
        out = jnp.where(crop == c, base + jnp.where(flag == 1, place, small), out)
    return out


def pack_kernel(crops, info, flags, tokens, cotangent, *outs):
    section = info[0]
    target = lax.broadcasted_iota(jnp.int32, (R, POS * crops), 0)
    lands = landing(flags, crops, 1)

    @pl.loop(0, info[1])
    def _(t):
        picks = (target + t * R == lands).astype(F32).astype(BF)
        packed = [nn(picks, rows[...]).astype(BF) for rows in (tokens, cotangent)]
        for r, out in enumerate(outs):
            is_last = section == SECTIONS - 1 - r

            @pl.when(is_last)
            def _():
                out[t] = packed[1]

            @pl.when(jnp.logical_not(is_last))
            def _():
                out[t] = packed[0]


def pack_rows(info, flags, tokens, cotangent, chunks):
    rows, width = tokens.shape
    crops = rows // POS
    return pl.pallas_call(
        functools.partial(pack_kernel, crops),
        out_shape=[shape((chunks, R, width), BF)] * SECTIONS,
        in_specs=[SM, SM, VM, VM],
        out_specs=[VM] * SECTIONS,
        compiler_params=pltpu.CompilerParams(vmem_limit_bytes=TINY_LIMIT),
        cost_estimate=LITTLE,
        name="pack_rows",
    )(info, flags, tokens, cotangent)


def unpack_kernel(crops, info, flags, own, came1, came2, came3, rows_out, grad_out):
    section = info[0]
    lands = landing(flags, crops, 0)
    total = own.shape[0] * R
    target = lax.broadcasted_iota(jnp.int32, (POS * crops, total), 1)
    picks = (target == lands).astype(F32).astype(BF)
    came = (own, came1, came2, came3)
    used = lax.broadcasted_iota(jnp.int32, (total, own.shape[2]), 0) < info[1] * R

    def rows_of(ref):
        block = ref[...].reshape(total, -1).astype(F32)
        return jnp.where(used, block, 0.0).astype(BF)

    for s in range(SECTIONS):

        @pl.when(section == s)
        def _():
            rows_out[...] = nn(picks, rows_of(came[(s + 1) % SECTIONS])).astype(BF)
            grad_out[...] = nn(picks, rows_of(came[s]))


def unpack_rows(info, flags, own, came):
    width = own.shape[2]
    crops = flags.shape[0]
    return pl.pallas_call(
        functools.partial(unpack_kernel, crops),
        out_shape=[shape((POS * crops, width), BF), shape((POS * crops, width), F32)],
        in_specs=[SM, SM] + [VM] * 4,
        out_specs=[VM, VM],
        compiler_params=pltpu.CompilerParams(vmem_limit_bytes=TINY_LIMIT),
        cost_estimate=LITTLE,
        name="unpack_rows",
    )(info, flags, own, *came)


ROWS_AT_ONCE = 8


def onehot_rows(index, it):
    rows = index[pl.ds(it * ROWS_AT_ONCE, ROWS_AT_ONCE), :]
    entry = lax.broadcasted_iota(jnp.int32, (TABLE, T), 0)
    parts = [(entry == rows[r : r + 1, :]).astype(F32).astype(BF) for r in range(ROWS_AT_ONCE)]
    return jnp.concatenate(parts, 1)


def split3(x):
    top = x.astype(BF)
    rest = x - top.astype(F32)
    middle = rest.astype(BF)
    return top, middle, (rest - middle.astype(F32)).astype(BF)


def spread_kernel(index, table, out):
    parts = split3(table[...])

    @pl.loop(0, T // ROWS_AT_ONCE)
    def _(it):
        picks = onehot_rows(index, it)
        values = nn(parts[0], picks) + nn(parts[1], picks) + nn(parts[2], picks)
        for r in range(ROWS_AT_ONCE):
            out[:, it * ROWS_AT_ONCE + r, :] = values[:HEADS, r * T : (r + 1) * T]


def spread_table(index, table):
    return pl.pallas_call(
        spread_kernel,
        out_shape=shape((HEADS, T, T), F32),
        in_specs=[VM, VM],
        out_specs=VM,
        compiler_params=pltpu.CompilerParams(vmem_limit_bytes=TINY_LIMIT),
        cost_estimate=LITTLE,
        name="spread_table",
    )(index, table)


def fold_kernel(index, sums, out):
    out[...] = jnp.zeros_like(out)

    @pl.loop(0, T // ROWS_AT_ONCE)
    def _(it):
        picks = onehot_rows(index, it)
        rows = jnp.concatenate([sums[:, it * ROWS_AT_ONCE + r, :] for r in range(ROWS_AT_ONCE)], 1)
        top = rows.astype(BF)
        rest = (rows - top.astype(F32)).astype(BF)
        out[...] += nt(top, picks) + nt(rest, picks)


def fold_table(index, sums):
    return pl.pallas_call(
        fold_kernel,
        out_shape=shape((HEADS, TABLE), F32),
        in_specs=[VM, VM],
        out_specs=VM,
        compiler_params=pltpu.CompilerParams(vmem_limit_bytes=TINY_LIMIT),
        cost_estimate=LITTLE,
        name="fold_table",
    )(index, pin(sums))


def row_norm(x):
    mean = jnp.sum(x, -1, keepdims=True) * (1.0 / D)
    centered = x - mean
    var = jnp.sum(centered * centered, -1, keepdims=True) * (1.0 / D)
    inv = lax.rsqrt(var + EPSILON)
    return centered * inv, inv


def head_masks():
    lane = lax.broadcasted_iota(jnp.int32, (T, T), 1)
    return [(lane >= HEAD * h) & (lane < HEAD * (h + 1)) for h in range(GROUP)]


def spread_heads(block, masks):
    zero = jnp.zeros_like(block)
    return jnp.concatenate([jnp.where(m, block, zero) for m in masks], 0)


def gather_heads(stacked, masks):
    total = stacked[0:T]
    for h in range(1, GROUP):
        total = jnp.where(masks[h], stacked[h * T : (h + 1) * T], total)
    return total


def lanes(at, size=T):
    return pl.ds(pl.multiple_of(at, T), size)


STEP = 512
BLOCKS = FF // STEP


def attention_forward(x, n, vec, wide, w, bias, a, b, save_a, save_b, y):

    @pl.loop(0, 3)
    def _(s):
        cols = lanes(s * D, D)
        a[:, cols] = (nn(n, w[:, cols]) + wide[0:1, cols]).astype(BF)

    save_a[0].start()
    masks = head_masks()

    @pl.loop(0, PAIR)
    def _(t):
        rows = pl.ds(pl.multiple_of(t * T, T), T)
        for grp in range(HEADS // GROUP):
            lo = grp * T
            heads = slice(grp * GROUP, (grp + 1) * GROUP)
            q, k, v = (a[rows, lo + s * D : lo + s * D + T] for s in range(3))
            s = nt(spread_heads(q, masks), k) * SCALE + bias[heads].reshape(GROUP * T, T)
            e = jnp.exp(s - jnp.max(s, -1, keepdims=True))
            p = (e * (1.0 / jnp.sum(e, -1, keepdims=True))).astype(BF)
            b[t, heads] = p.reshape(GROUP, T, T)
            a[rows, 3 * D + lo : 3 * D + lo + T] = gather_heads(nn(p, v), masks).astype(BF)

    save_a[1].start()
    save_b.start()
    branch = nn(a[:, 3 * D :], w[:, 3 * D :]) + vec[2:3, :]
    y[...] = (x + branch).astype(BF)


ERF_SLOPE = 0.3275911 * SQRT_HALF
ERF_TERMS = (1.061405429, -1.453152027, 1.421413741, -0.284496736, 0.254829592)


def normal_parts(u):
    bell = jnp.exp(-0.5 * u * u)
    base = 1.0 + ERF_SLOPE * jnp.abs(u)
    t = pl.reciprocal(base, approx=True)
    t = t * (2.0 - base * t)
    poly = 0.5 * ERF_TERMS[0]
    for term in ERF_TERMS[1:]:
        poly = poly * t + 0.5 * term
    tail = poly * t * bell
    return jnp.where(u >= 0, 1.0 - tail, tail), u * (bell * INV_SQRT_TAU)


def mlp_forward(x, n, vec, wide, w, v, a, b, acc):
    acc[...] = x + vec[2:3, :]

    @pl.loop(0, BLOCKS, step=2)
    def _(j0):
        blocks = []
        for jb in (j0, j0 + 1):
            cols = lanes(jb * STEP, STEP)
            u = nn(n, w[:, cols]) + wide[0:1, cols]
            cdf, rise = normal_parts(u)
            blocks.append((jb, cols, (u * cdf).astype(BF), (cdf + rise).astype(BF)))
        part = None
        for jb, cols, act, slope in blocks:
            a[:, cols] = act
            for t in range(PAIR):
                for i in range(STEP // T):
                    b[t, jb * (STEP // T) + i] = slope[t * T : (t + 1) * T, i * T : (i + 1) * T]
            term = nn(act, v[cols, :])
            part = term if part is None else part + term
        acc[...] += part


def forward_kernel(both, info, slot, vec, wide, bias, w, *refs):
    v = refs[0] if both else None
    p0, p1, p2, p3, came = refs[both : both + 5]
    y, *kept = refs[both + 13 :]
    xs, keep_n, keep_a, keep_b, *outs = kept[:8]
    x_in, n, a, b, acc, parts, sems = kept[8:]
    width = parts.shape[-1]
    section, used = info[0], info[1]
    c = slot[0] - section

    def copy(source, target, k):
        return pltpu.make_async_copy(source, target, sems.at[k])

    save_x, save_n = copy(x_in, xs.at[c], 0), copy(n, keep_n.at[c], 1)
    save_b = copy(b, keep_b.at[c], 3)
    early = [copy(a.at[:, cut], keep_a.at[c, :, cut], 2) for cut in (pl.ds(0, 3 * D), pl.ds(3 * D, D))]
    put = [copy(parts.at[d], outs[(d + 1) % SECTIONS].at[c], 4 + d) for d in range(SECTIONS)]

    @pl.when((c >= slot[1]) & (c < jnp.minimum(slot[2], used)))
    def _():
        @pl.when(section == 0)
        def _():
            bring = [copy(p.at[c], parts.at[d], 4 + d) for d, p in enumerate((p0, p3, p2, p1))]
            for one in bring:
                one.start()
            for one in bring:
                one.wait()
            x_in[...] = jnp.concatenate([parts[d] for d in range(SECTIONS)], -1)

        @pl.when(section != 0)
        def _():
            x_in[...] = came[...]

        save_x.start()
        x = x_in[...].astype(F32)
        raw, _ = row_norm(x)
        normed = (raw * vec[0:1, :] + vec[1:2, :]).astype(BF)
        n[...] = normed
        save_n.start()

        @pl.when(section % 2 == 0)
        def _():
            attention_forward(x, normed, vec, wide, w, bias, a, b, early, save_b, y)

        if both:

            @pl.when(section % 2 == 1)
            def _():
                mlp_forward(x, normed, vec, wide, w, v, a, b, acc)
                for one in early:
                    one.start()
                save_b.start()
                y[...] = acc[...].astype(BF)

        @pl.when(both & (section == SECTIONS - 1))
        def _():
            for d in range(SECTIONS):
                parts[d] = y[:, d * width : (d + 1) * width]
                put[d].start()
            for d in range(SECTIONS):
                put[d].wait()

        save_x.wait()
        save_n.wait()
        for one in early:
            one.wait()
        save_b.wait()


ANY = pl.BlockSpec(memory_space=pl.ANY)


def far(x):
    return pltpu.with_memory_space_constraint(x, pltpu.HBM)


def run_forward(info, slot, pieces, came, vec, wide, w, v, bias, kept):
    count = len(kept)
    width = pieces[0].shape[-1]
    both = v is not None
    weights = [pin(w), pin(v)] if both else [pin(w)]
    outs = pl.pallas_call(
        functools.partial(forward_kernel, both),
        out_shape=[shape((R, D), BF)] + [like(r) for r in kept],
        in_specs=[SM, SM] + [VM] * (4 + both) + [ANY] * 4 + [VM] + [ANY] * count,
        out_specs=[VM] + [ANY] * count,
        scratch_shapes=[
            pltpu.VMEM((R, D), BF),
            pltpu.VMEM((R, D), BF),
            pltpu.VMEM((R, FF), BF),
            pltpu.VMEM((PAIR, HEADS, T, T), BF),
            pltpu.VMEM((R, D), F32),
            pltpu.VMEM((SECTIONS, R, width), BF),
            pltpu.SemaphoreType.DMA((4 + SECTIONS,)),
        ],
        input_output_aliases={11 + both + i: 1 + i for i in range(count)},
        compiler_params=pltpu.CompilerParams(vmem_limit_bytes=SMALL_LIMIT),
        cost_estimate=LITTLE,
        name="section_forward",
    )(info, slot, vec, wide, pin(bias), *weights, *pieces, came, *[far(r) for r in kept])
    return outs[0], list(outs[1:])


def norm_backward(x, g, dn, vec, sums, gx):
    raw, inv = row_norm(x)
    sums[0:1, :] += jnp.sum(dn * raw, 0, keepdims=True)
    sums[1:2, :] += jnp.sum(dn, 0, keepdims=True)
    sums[2:3, :] += jnp.sum(g, 0, keepdims=True)
    s = dn * vec[0:1, :]
    m1 = jnp.sum(s, -1, keepdims=True) * (1.0 / D)
    m2 = jnp.sum(s * raw, -1, keepdims=True) * (1.0 / D)
    gx[...] = (g + inv * (s - m1 - raw * m2)).astype(BF)


def attention_backward(g, w, a, b, bring_a, bring_b, d, acc, save_d, dsum):
    masks = head_masks()
    d[:, 3 * D :] = g
    d[:, 0:D] = nt(g, w[:, 3 * D :]).astype(BF)
    bring_a.wait()
    bring_b.wait()

    @pl.loop(0, PAIR)
    def _(t):
        rows = pl.ds(pl.multiple_of(t * T, T), T)
        for grp in range(HEADS // GROUP):
            lo = grp * T
            heads = slice(grp * GROUP, (grp + 1) * GROUP)
            q, k, v = (a[rows, lo + s * D : lo + s * D + T] for s in range(3))
            p = b[t, heads].reshape(GROUP * T, T)
            do_heads = spread_heads(d[rows, lo : lo + T], masks)
            dv = tn(p, do_heads)
            pf = p.astype(F32)
            pdp = pf * nt(do_heads, v)
            ds = (pdp - pf * jnp.sum(pdp, -1, keepdims=True)).astype(BF)
            dsum[heads] += ds.astype(F32).reshape(GROUP, T, T)
            dq = gather_heads(nn(ds, k), masks) * SCALE
            dk = tn(ds, spread_heads(q, masks)) * SCALE
            d[rows, lo : lo + T] = dq.astype(BF)
            d[rows, D + lo : D + lo + T] = dk.astype(BF)
            d[rows, 2 * D + lo : 2 * D + lo + T] = dv.astype(BF)

    save_d.start()
    acc[...] = jnp.zeros_like(acc)

    @pl.loop(0, 3)
    def _(s):
        cols = lanes(s * D, D)
        acc[...] += nt(d[:, cols], w[:, cols])


def mlp_backward(g, w, v, b, bring_b, d, acc):
    acc[...] = jnp.zeros_like(acc)
    bring_b.wait()

    @pl.loop(0, BLOCKS, step=2)
    def _(j0):
        blocks = []
        for jb in (j0, j0 + 1):
            cols = lanes(jb * STEP, STEP)
            da = nt(g, v[cols, :]).astype(BF).astype(F32)
            slope = jnp.concatenate(
                [
                    jnp.concatenate([b[t, jb * (STEP // T) + i] for i in range(STEP // T)], 1)
                    for t in range(PAIR)
                ],
                0,
            )
            blocks.append((cols, (da * slope.astype(F32)).astype(BF)))
        part = None
        for cols, du in blocks:
            d[:, cols] = du
            term = nt(du, w[:, cols])
            part = term if part is None else part + term
        acc[...] += part


def seed_rows(scales, c):
    row = lax.broadcasted_iota(jnp.int32, (T, 1), 0)
    parts = []
    for t in range(PAIR):
        base = (c * PAIR + t) * 8
        out = jnp.full((T, 1), scales[base], F32)
        for k, at in enumerate([POS] + [SMALL_AT + SMALL * i for i in range(3)]):
            out = jnp.where(row >= at, scales[base + 1 + k], out)
        parts.append(out)
    return jnp.concatenate(parts, 0)


def backward_kernel(info, slot, scales, vec, w, v, dsum_in, sums_in, p0, p1, p2, p3, came, *refs):
    gx, dsum, sums, *kept = refs[9:]
    xs, keep_a, keep_b, gs, keep_d, *outs = kept[:9]
    x_in, g_tile, a, b, d, acc, parts, sems = kept[9:]
    width = parts.shape[-1]
    section, used = info[0], info[1]
    c = slot[0] - (SECTIONS - 1 - section)

    def copy(source, target, k):
        return pltpu.make_async_copy(source, target, sems.at[k])

    bring_x, bring_a, bring_b = copy(xs.at[c], x_in, 0), copy(keep_a.at[c], a, 1), copy(keep_b.at[c], b, 2)
    save_g, save_d = copy(g_tile, gs.at[c], 3), copy(d, keep_d.at[c], 4)
    put = [copy(parts.at[k], outs[k].at[c], 5 + k) for k in range(SECTIONS)]

    @pl.when((c >= slot[1]) & (c < jnp.minimum(slot[2], used)))
    def _():
        @pl.when(section == SECTIONS - 1)
        def _():
            bring = [copy(p.at[c], parts.at[k], 5 + k) for k, p in enumerate((p3, p2, p1, p0))]
            for one in bring:
                one.start()
            bring_b.start()
            for one in bring:
                one.wait()
            seed = jnp.concatenate([parts[k] for k in range(SECTIONS)], -1).astype(F32)
            g_tile[...] = (seed * seed_rows(scales, c)).astype(BF)

        @pl.when(section != SECTIONS - 1)
        def _():
            bring_b.start()
            g_tile[...] = came[...]

        pl.when(section % 2 == 0)(bring_a.start)
        bring_x.start()
        save_g.start()

        @pl.when(c == 0)
        def _():
            dsum[...] = jnp.zeros_like(dsum)
            sums[...] = jnp.zeros_like(sums)

        g = g_tile[...]

        @pl.when(section % 2 == 0)
        def _():
            attention_backward(g, w, a, b, bring_a, bring_b, d, acc, save_d, dsum)

        @pl.when(section % 2 == 1)
        def _():
            mlp_backward(g, w, v, b, bring_b, d, acc)
            save_d.start()

        bring_x.wait()
        norm_backward(x_in[...].astype(F32), g.astype(F32), acc[...], vec, sums, gx)

        @pl.when(section == 0)
        def _():
            for k in range(SECTIONS):
                parts[k] = gx[:, k * width : (k + 1) * width]
                put[k].start()
            for k in range(SECTIONS):
                put[k].wait()

        save_g.wait()
        save_d.wait()


def run_backward(info, slot, scales, pieces, came, vec, w, v, dsum, sums, kept):
    count = len(kept)
    width = pieces[0].shape[-1]
    outs = pl.pallas_call(
        backward_kernel,
        out_shape=[shape((R, D), BF)] + [like(r) for r in (dsum, sums, *kept)],
        in_specs=[SM, SM, SM] + [VM] * 5 + [ANY] * 4 + [VM] + [ANY] * count,
        out_specs=[VM] * 3 + [ANY] * count,
        scratch_shapes=[
            pltpu.VMEM((R, D), BF),
            pltpu.VMEM((R, D), BF),
            pltpu.VMEM((R, FF), BF),
            pltpu.VMEM((PAIR, HEADS, T, T), BF),
            pltpu.VMEM((R, FF), BF),
            pltpu.VMEM((R, D), F32),
            pltpu.VMEM((SECTIONS, R, width), BF),
            pltpu.SemaphoreType.DMA((5 + SECTIONS,)),
        ],
        input_output_aliases={6: 1, 7: 2} | {13 + i: 3 + i for i in range(count)},
        compiler_params=pltpu.CompilerParams(vmem_limit_bytes=SMALL_LIMIT),
        cost_estimate=LITTLE,
        name="section_backward",
    )(
        info, slot, scales, vec, pin(w), pin(v), pin(dsum), pin(sums), *pieces, came,
        *[far(r) for r in kept],
    )
    return outs[0], outs[1], outs[2], list(outs[3:])


def make_room(dims):
    def body(*refs):
        pass

    return pl.pallas_call(
        body,
        out_shape=[pltpu.VMEM(d, k) if near else pltpu.HBM(d, k) for d, k, near in dims],
        out_specs=[VM if near else ANY for _, _, near in dims],
        compiler_params=pltpu.CompilerParams(vmem_limit_bytes=TINY_LIMIT),
        name="make_room",
    )()


def clear(ref, used, *at):
    @pl.loop(used, ref.shape[len(at)])
    def _(t):
        ref[(*at, t)] = jnp.zeros(ref.shape[-2:], BF)


def in_kernel(usual, info, keep_n, keep_a, keep_d, top, low, wide_sums, turned, n, a, d, tile, in_sems):
    chunks = n.shape[0]
    rows = chunks * R
    mlp, used = info[0] % 2, info[1]
    part = D // 2
    half = STEP // 2

    def bring(jb, first, count):
        cut = pl.ds(first, count)
        return pltpu.make_async_copy(
            keep_d.at[cut, :, pl.ds(jb * STEP, STEP)], d.at[jb, cut], in_sems.at[jb]
        )

    def others(work):
        for c in range(usual, chunks):
            pl.when(used > c)(functools.partial(work, c))

    bring_n = pltpu.make_async_copy(keep_n, n, in_sems.at[BLOCKS])
    bring_a = pltpu.make_async_copy(keep_a.at[:, :, pl.ds(3 * D, D)], a, in_sems.at[BLOCKS + 1])
    bring_n.start()
    for jb in range(BLOCKS):
        bring(jb, 0, usual).start()
    others(lambda c: [bring(jb, c, 1).start() for jb in range(BLOCKS)] and None)
    bring_a.start()
    bring_n.wait()
    clear(n, used)
    turned[0] = n[...].reshape(rows, D).T
    bring_a.wait()
    clear(a, used)

    @pl.when(mlp == 0)
    def _():
        turned[1] = a[...].reshape(rows, D).T

    @pl.when(mlp == 1)
    def _():
        turned[1] = turned[0]

    @pl.loop(0, BLOCKS)
    def _(jb):
        bring(jb, 0, usual).wait()
        others(lambda c: bring(jb, c, 1).wait())
        clear(d, used, jb)
        block = d[jb, :usual].reshape(usual * R, STEP)
        cols = lanes(jb * STEP, STEP)
        wide_sums[0:1, cols] = jnp.sum(block.astype(F32), 0, keepdims=True)

        def add_sum(c):
            wide_sums[0:1, cols] += jnp.sum(d[jb, c].astype(F32), 0, keepdims=True)

        others(add_sum)
        for k in range(2):
            late = (jb * 2 + k >= 3 * D // half).astype(jnp.int32)
            cut = slice(k * half, (k + 1) * half)
            tile[...] = nn(turned[late, :, : usual * R], block[:, cut])

            def add(c):
                tile[...] += nn(turned[late, :, c * R : (c + 1) * R], d[jb, c, :, cut])

            others(add)
            grad = tile[...].astype(BF)
            to = lanes(jb * STEP + k * half, half)
            top[:, to] = grad[:part]
            low[:, to] = grad[part:]


def in_grads(info, keep_n, keep_a, keep_d, usual):
    chunks = keep_n.shape[0]
    return pl.pallas_call(
        functools.partial(in_kernel, usual),
        out_shape=[pltpu.VMEM((D // 2, FF), BF)] * 2 + [shape((8, FF), F32)],
        in_specs=[SM] + [ANY] * 3,
        out_specs=[VM] * 3,
        scratch_shapes=[
            pltpu.VMEM((2, D, chunks * R), BF),
            pltpu.VMEM((chunks, R, D), BF),
            pltpu.VMEM((chunks, R, D), BF),
            pltpu.VMEM((BLOCKS, chunks, R, STEP), BF),
            pltpu.VMEM((D, STEP // 2), F32),
            pltpu.SemaphoreType.DMA((BLOCKS + 2,)),
        ],
        compiler_params=pltpu.CompilerParams(vmem_limit_bytes=LIMIT),
        cost_estimate=LITTLE,
        name="in_grads",
    )(info, *[far(r) for r in (keep_n, keep_a, keep_d)])


def down_kernel(usual, info, keep_a, gs, grad, a, g, tile, out, in_sems, out_sems):
    chunks = g.shape[0]
    mlp, used = info[0] % 2, info[1]

    def bring(jb, first, count):
        cut = pl.ds(first, count)
        return pltpu.make_async_copy(
            keep_a.at[cut, :, pl.ds(jb * STEP, STEP)], a.at[jb, cut], in_sems.at[jb]
        )

    def put(jb):
        return pltpu.make_async_copy(out.at[jb % 2], grad.at[pl.ds(jb * STEP, STEP), :], out_sems.at[jb % 2])

    def others(work):
        for c in range(usual, chunks):
            pl.when(used > c)(functools.partial(work, c))

    @pl.when(mlp == 1)
    def _():
        bring_g = pltpu.make_async_copy(gs, g, in_sems.at[BLOCKS])
        bring_g.start()
        for jb in range(BLOCKS):
            bring(jb, 0, usual).start()
        others(lambda c: [bring(jb, c, 1).start() for jb in range(BLOCKS)] and None)
        bring_g.wait()
        clear(g, used)
        flat_g = g[:usual].reshape(usual * R, D)

        @pl.loop(0, BLOCKS)
        def _(jb):
            bring(jb, 0, usual).wait()
            others(lambda c: bring(jb, c, 1).wait())
            clear(a, used, jb)

            @pl.when(jb >= 2)
            def _():
                put(jb - 2).wait()

            tile[...] = tn(a[jb, :usual].reshape(usual * R, STEP), flat_g)

            def add(c):
                tile[...] += tn(a[jb, c], g[c])

            others(add)
            out[jb % 2] = tile[...].astype(BF)
            put(jb).start()

        for jb in (BLOCKS - 2, BLOCKS - 1):
            put(jb).wait()


def down_grads(info, keep_a, gs, usual):
    chunks = gs.shape[0]
    dma = pltpu.SemaphoreType.DMA
    return pl.pallas_call(
        functools.partial(down_kernel, usual),
        out_shape=shape((FF, D), BF),
        in_specs=[SM] + [ANY] * 2,
        out_specs=ANY,
        scratch_shapes=[
            pltpu.VMEM((BLOCKS, chunks, R, STEP), BF),
            pltpu.VMEM((chunks, R, D), BF),
            pltpu.VMEM((STEP, D), F32),
            pltpu.VMEM((2, STEP, D), BF),
            dma((BLOCKS + 1,)),
            dma((2,)),
        ],
        compiler_params=pltpu.CompilerParams(vmem_limit_bytes=LIMIT),
        cost_estimate=LITTLE,
        name="down_grads",
    )(info, far(keep_a), far(gs))


def swapped(block, axis, bit):
    size = lax.axis_size(axis)
    return lax.ppermute(block, axis, [(i, i ^ bit) for i in range(size)])


def butterfly(block, axis):
    size = lax.axis_size(axis)
    if size & (size - 1):
        return lax.psum(block, axis)
    bit = 1
    while bit < size:
        block = block + swapped(block, axis, bit)
        bit *= 2
    return block


PARTS = 8


def pair_sum_kernel(mine, came, own, parcel, sems):
    rows = mine.shape[0] // PARTS
    moves = [
        pltpu.make_async_copy(came.at[pl.ds(k * rows, rows)], parcel.at[k], sems.at[k]) for k in range(PARTS)
    ]
    for move in moves:
        move.start()
    for move in moves:
        move.wait()

    @pl.loop(0, PARTS)
    def _(k):
        at = pl.ds(pl.multiple_of(k * rows, rows), rows)
        own[at, :] = (mine[at, :].astype(F32) + parcel[k].astype(F32)).astype(BF)


def pair_sum(mine, came):
    rows, cols = mine.shape
    return pl.pallas_call(
        pair_sum_kernel,
        out_shape=pltpu.VMEM(mine.shape, BF),
        in_specs=[VM, ANY],
        out_specs=VM,
        scratch_shapes=[pltpu.VMEM((PARTS, rows // PARTS, cols), BF), pltpu.SemaphoreType.DMA((PARTS,))],
        compiler_params=pltpu.CompilerParams(vmem_limit_bytes=TINY_LIMIT),
        cost_estimate=LITTLE,
        name="pair_sum",
    )(pin(mine), came)


def final_sum_kernel(count, blocks, came, other, *refs):
    owns, (out, parcel, wide, in_sems, out_sems) = refs[:count], refs[count:]
    rows = came.shape[0] // blocks
    each = blocks // count

    def bring(k):
        return pltpu.make_async_copy(other.at[pl.ds(k * rows, rows)], parcel.at[k], in_sems.at[k])

    def put(k):
        return pltpu.make_async_copy(wide.at[k % 2], out.at[pl.ds(k * rows, rows)], out_sems.at[k % 2])

    @pl.loop(0, blocks)
    def _(k):
        bring(k).start()

    for part, own in enumerate(owns):

        @pl.loop(0, each)
        def _(j):
            k = part * each + j
            bring(k).wait()

            @pl.when(k >= 2)
            def _():
                put(k - 2).wait()

            near = pl.ds(pl.multiple_of(j * rows, rows), rows)
            far_rows = pl.ds(pl.multiple_of(k * rows, rows), rows)
            value = own[near, :].astype(F32) + came[far_rows, :].astype(F32)
            wide[k % 2] = value + parcel[k].astype(F32)
            put(k).start()

    for k in range(blocks - 2, blocks):
        put(k).wait()


def final_sum(owns, came, other, blocks):
    rows, cols = came.shape
    return pl.pallas_call(
        functools.partial(final_sum_kernel, len(owns), blocks),
        out_shape=shape((rows, cols), F32),
        in_specs=[VM, ANY] + [VM] * len(owns),
        out_specs=ANY,
        scratch_shapes=[
            pltpu.VMEM((blocks, rows // blocks, cols), BF),
            pltpu.VMEM((2, rows // blocks, cols), F32),
            pltpu.SemaphoreType.DMA((blocks,)),
            pltpu.SemaphoreType.DMA((2,)),
        ],
        compiler_params=pltpu.CompilerParams(vmem_limit_bytes=10 << 20),
        cost_estimate=LITTLE,
        name="final_sum",
    )(pin(came), other, *[pin(x) for x in owns])


def line_kernel(stream, count, step, rank, came, *refs):
    tops, send = refs[:count], refs[count]
    chunk = step[0] - rank[0]
    at = stream * FF // 2

    def put(source, row, cuts):
        for k, (down_by, col) in enumerate(cuts):
            rows = pl.ds(pl.multiple_of(row + down_by, LINE), LINE)
            value = source[rows, col : col + D]

            @pl.when(rank[0] == 0)
            def _():
                send[k] = value

            @pl.when(rank[0] > 0)
            def _():
                send[k] = (value.astype(F32) + came[k].astype(F32)).astype(BF)

    side_by_side = ((0, at), (0, at + D))
    for half, source in enumerate(tops[:2]):
        first = half * IN_CHUNKS // 2

        @pl.when((chunk >= first) & (chunk < first + IN_CHUNKS // 2))
        def _():
            put(source, (chunk - first) * LINE, side_by_side)

    if count == 3:

        @pl.when((chunk >= IN_CHUNKS) & (chunk < CHUNKS))
        def _():
            put(tops[2], (chunk - IN_CHUNKS + stream * DOWN_CHUNKS) * 2 * LINE, ((0, 0), (LINE, 0)))


class LineSum:
    def __init__(self, place, core, length, stream):
        self.length, self.stream = length, stream
        self.rank = jnp.where(core == 0, place, length - 1 - place).reshape(1)
        self.came = jnp.zeros((2, LINE, D), BF)
        self.sends = CHUNKS + length - 2
        self.route = [(2 * z, 2 * z + 2) for z in range(length - 1)]
        self.route += [(2 * z + 3, 2 * z + 1) for z in range(length - 1)]
        self.kept = []

    def advance(self, step, owns):
        owns = owns[: 1 + (step >= IN_CHUNKS // 2) + (step >= IN_CHUNKS)]
        self.sent = pl.pallas_call(
            functools.partial(line_kernel, self.stream, len(owns)),
            out_shape=like(self.came),
            in_specs=[SM, SM] + [VM] * (1 + len(owns)),
            out_specs=VM,
            compiler_params=pltpu.CompilerParams(vmem_limit_bytes=TINY_LIMIT),
            cost_estimate=LITTLE,
            name="line_step",
        )(np.array([step], np.int32), self.rank, self.came, *[pin(x) for x in owns])
        self.came = lax.ppermute(self.sent, "dp", self.route)
        self.kept.append(self.came)


def collect_kernel(length, where, rank, *refs):
    kept, (out, zero, sems) = refs[:-3], refs[-3:]
    zero[...] = jnp.zeros_like(zero)

    def move(item, k, ref):
        row, col = where[item][1][k]
        to = out.at[pl.ds(row, LINE), pl.ds(col, D)]
        return pltpu.make_async_copy(ref, to, sems.at[item, k])

    for item, (index, _) in enumerate(where):
        for k in range(2):
            pl.when(rank[0] == 0)(move(item, k, zero).start)
            for r in range(1, length):
                pl.when(rank[0] == r)(move(item, k, kept[index[r - 1]].at[k]).start)
    for item in range(len(where)):
        for k in range(2):
            move(item, k, zero).wait()


def collect_rows(rank, streams, first, count, dims):
    length = streams[0].length
    kept, where = [], []
    for k, stream in enumerate(streams):
        for c in range(count):
            index = []
            for r in range(1, length):
                index.append(len(kept))
                kept.append(stream.kept[first + c + r - 1])
            if dims[1] == FF:
                spots = [(c * LINE, k * FF // 2), (c * LINE, k * FF // 2 + D)]
            else:
                spots = [((c + k * count) * 2 * LINE + half * LINE, 0) for half in range(2)]
            where.append((index, spots))
    return pl.pallas_call(
        functools.partial(collect_kernel, length, where),
        out_shape=pltpu.VMEM(dims, BF),
        in_specs=[SM] + [ANY] * len(kept),
        out_specs=VM,
        scratch_shapes=[pltpu.VMEM((LINE, D), BF), pltpu.SemaphoreType.DMA((len(where), 2))],
        compiler_params=pltpu.CompilerParams(vmem_limit_bytes=TINY_LIMIT),
        cost_estimate=LITTLE,
        name="collect_rows",
    )(rank, *kept)


def added(*parts):
    return sum(p.astype(F32) for p in parts)


def after(x, *first):
    return lax.optimization_barrier((x, *first))[0]


def flat_rows(x):
    return x.transpose(1, 0, 2).reshape(-1, x.shape[2])


def stacked_rows(x, crops):
    return x.reshape(POS, crops, -1).transpose(1, 0, 2)


def on_device(
    tokens,
    cotangent,
    in_weight,
    down_weight,
    norm_gain,
    norm_shift,
    out_bias,
    qv_bias,
    fc1_bias,
    rel_table,
    shift_regions,
    crop_global,
    micro_of,
):
    section = lax.axis_index("pipe")
    dp_index = lax.axis_index("dp")
    core, place = dp_index % 2, dp_index // 2
    dp_size = lax.axis_size("dp")
    mlp = section % 2
    block = section // 2
    crops = tokens.shape[0]
    chunks = (crops + 2 * PAIR - 1) // (2 * PAIR)
    last = SECTIONS - 1

    half = FF // 4
    sent = lax.dynamic_slice_in_dim(down_weight[0], core * half, half, 0)
    mine = lax.ppermute(sent, "pipe", [(s, s + 1) for s in range(0, SECTIONS, 2)])

    bigs_all = jnp.sum(crop_global)
    needed = jnp.maximum(
        (bigs_all + 2 * PAIR - 1) // (2 * PAIR), (crops - bigs_all + 3 * PAIR - 1) // (3 * PAIR)
    )
    info = after(jnp.stack([section, needed, core]).astype(jnp.int32), sent)
    packs = pack_rows(info, crop_global, flat_rows(tokens), flat_rows(cotangent), chunks)
    pieces = [packs[0]] + [
        lax.ppermute(packs[r], "pipe", [(SECTIONS - r, 0), (last - r, last)]) for r in range(1, SECTIONS)
    ]

    w = in_weight[0]

    vec = jnp.stack([norm_gain[section], norm_shift[section], out_bias[section]])
    qv = qv_bias[block]
    wide_attention = jnp.concatenate([qv[0], jnp.zeros((D,), F32), qv[1], jnp.zeros((D,), F32)])
    wide = jnp.where(mlp == 1, fc1_bias[block], wide_attention)[None]

    both, rolled = pair_index()
    regions = jnp.where(block == 1, shift_regions[rolled], 0)
    index = jnp.where(block == 1, both[1], both[0])
    index = jnp.where(regions[:, None] == regions[None, :], index, TABLE - 1)
    table = jnp.pad(
        rel_table[block].T, ((0, 32 - HEADS), (0, TABLE - SPAN)), constant_values=((0, 0), (0, NEGATIVE))
    )
    bias = spread_table(after(index, packs[0]), table)

    member = (micro_of == jnp.arange(MICRO, dtype=jnp.int32)[None, :]).astype(F32)
    crop_rows = jnp.where(crop_global == 1, POS, SMALL).astype(F32)
    counts = jnp.sum(member * crop_rows[:, None], 0)
    counts = jnp.concatenate([counts, needed.astype(F32).reshape(1)])
    count_rounds = [1 << k for k in range((dp_size - 1).bit_length())]
    before = np.tril(np.ones((crops, crops), np.int32), -1)
    bigs = jnp.sum(before * crop_global[None, :], 1)
    smalls = jnp.arange(crops, dtype=jnp.int32) - bigs
    entry = jnp.where(crop_global == 1, bigs // 2 * 8 + bigs % 2, smalls // 3 * 8 + 2 + smalls % 3)
    here = entry[:, None] == jnp.arange(chunks * PAIR * 8, dtype=jnp.int32)[None, :]

    width = tokens.shape[2]
    down_pipe = [(s, s + 1) for s in range(last)]
    up_pipe = [(s, s - 1) for s in range(1, SECTIONS)]

    dsum, sums, xs, keep_n, gs, keep_a, keep_d, keep_b, *outs = make_room(
        [((HEADS, T, T), F32, True), ((8, D), F32, True)]
        + [((chunks, R, D), BF, False)] * 3
        + [((chunks, R, FF), BF, False)] * 2
        + [((chunks, PAIR, HEADS, T, T), BF, False)]
        + [((chunks, R, width), BF, False)] * 4
    )
    usual = max(chunks - 1, 1)
    blank = jnp.zeros((R, D), BF)
    kept = [dsum, sums, xs, keep_n, gs, keep_a, keep_d, keep_b, *outs]

    def slot(at, first, stop):
        if isinstance(first, int):
            return np.array([first + at, first, stop], np.int32)
        return jnp.stack([first + at, first, stop]).astype(jnp.int32)

    def forward(i, first, stop, came, v, kept):
        dsum, sums, xs, keep_n, gs, keep_a, keep_d, keep_b, *outs = kept
        y, (xs, keep_n, keep_a, keep_b, *outs) = run_forward(
            info, slot(i, first, stop), pieces, came, vec, wide, w, v, bias,
            [xs, keep_n, keep_a, keep_b, *outs],
        )
        return y, [dsum, sums, xs, keep_n, gs, keep_a, keep_d, keep_b, *outs]

    def backward(j, first, stop, came, v, kept):
        dsum, sums, xs, keep_n, gs, keep_a, keep_d, keep_b, *outs = kept
        gx, dsum, sums, (xs, keep_a, keep_b, gs, keep_d, *outs) = run_backward(
            info, slot(j, first, stop), scales, pieces, came, vec, w, v,
            dsum, sums, [xs, keep_a, keep_b, gs, keep_d, *outs],
        )
        return gx, [dsum, sums, xs, keep_n, gs, keep_a, keep_d, keep_b, *outs]

    came_f = came_b = blank
    v = None
    for i in range(usual + 2 * last):
        if i < usual + last:
            y, kept = forward(i, 0, usual, came_f, v, kept)
            if i < usual + last - 1:
                came_f = lax.ppermute(y, "pipe", [(s, t) for s, t in down_pipe if 0 <= i - s < usual])
            if i < last:
                take = -(-len(count_rounds) // last)
                for bit in count_rounds[i * take : (i + 1) * take]:
                    count_other = swapped(after(counts, y), "dp", bit)
                    counts = jnp.concatenate(
                        [counts[:MICRO] + count_other[:MICRO], jnp.maximum(counts, count_other)[MICRO:]]
                    )
            if i == 0:
                mine = after(mine, counts)
                other = swapped(mine, "dp", 1)
                upper = jnp.where(core == 0, mine, other), jnp.where(core == 0, other, mine)
                v = jnp.concatenate([down_weight[0], *upper], 0)
        if i == last:
            most = counts[MICRO].astype(jnp.int32)
            counts = counts[:MICRO]
            scales = jnp.sum(member * (jnp.sum(counts) / (MICRO * counts))[None], 1)
            scales = jnp.sum(jnp.where(here, scales[:, None], 0.0), 0)
        if i >= last:
            gx, kept = backward(i - last, 0, usual, came_b, v, kept)
            if i < usual + 2 * last - 1:
                came_b = lax.ppermute(gx, "pipe", [(s, t) for s, t in up_pipe if 0 <= i - 2 * last + s < usual])

    def beyond(k, carry):
        came_f, came_b, kept = carry
        c, at = usual + k // (2 * SECTIONS), k % (2 * SECTIONS)
        y, kept = forward(at, c, c + 1, came_f, v, kept)
        came_f = lax.ppermute(y, "pipe", down_pipe)
        gx, kept = backward(at - SECTIONS, c, c + 1, came_b, v, kept)
        came_b = lax.ppermute(gx, "pipe", up_pipe)
        return came_f, came_b, kept

    more = jnp.maximum(most - usual, 0) * (2 * SECTIONS)
    kept = lax.fori_loop(0, more, beyond, (blank, blank, kept))[2]
    dsum, sums, xs, keep_n, gs, keep_a, keep_d, keep_b, *outs = kept
    v_grad = down_grads(info, keep_a, gs, usual)
    w_top, w_low, wide_sums = in_grads(info, after(keep_n, v_grad), keep_a, keep_d, usual)

    route = [
        (s * dp_size + i, s * dp_size + (i ^ 1)) for s in range(1, SECTIONS, 2) for i in range(dp_size)
    ]
    v_came = lax.ppermute(v_grad, ("pipe", "dp"), route)
    out_came = []
    at = FF // 2 + half * core
    parts = [lax.dynamic_slice_in_dim(after(x, w_top), at, half, 0) for x in (v_grad, v_came)]
    v_part = added(*parts).astype(BF)
    v_back = lax.ppermute(v_part, "pipe", [(s + 1, s) for s in range(0, SECTIONS, 2)])
    w_own = [pair_sum(w_top, swapped(w_top, "dp", 1)), None, None]

    length = dp_size // 2
    first, second = streams = [LineSum(place, core, length, k) for k in range(2)]
    ends = streams[0].sends
    ready = [[v_part]] + [[] for _ in range(ends + 8)]
    rounds = [("dp", 1 << k) for k in range((dp_size - 1).bit_length())] + [("pipe", 1), ("pipe", 2)]
    packed = waiting = None

    def turn(step, gap):
        nonlocal packed, waiting
        if waiting is not None:
            packed = packed + after(waiting, gap)
            waiting = None
            ready[step + 1].append(packed)
        if rounds:
            axis, bit = rounds.pop(0)
            if axis == "pipe" and bit == 1:
                packed = (jnp.arange(SECTIONS) == section).astype(F32)[:, None] * packed[None]
            waiting = swapped(after(packed, gap), axis, bit)

    for step in range(ends):
        first.came = after(first.came, *ready[step])
        first.advance(step, w_own)
        second.came = after(second.came, first.sent)
        second.advance(step, w_own)
        gap = second.sent
        ready[step + 1].append(gap)
        if step == 0:
            w_low = after(w_low, gap)
            w_own[1] = pair_sum(w_low, swapped(w_low, "dp", 1))
            rel_grad = fold_table(index, after(dsum, gap))
            narrow = jnp.where(
                mlp == 1,
                wide_sums[0],
                jnp.concatenate(
                    [wide_sums[0, :D], wide_sums[0, 2 * D : 3 * D], jnp.zeros((2 * D,), F32)]
                ),
            )
            packed = jnp.concatenate([sums[:3].reshape(-1), narrow, rel_grad[:, :SPAN].reshape(-1)])
            ready[1].append(packed)
        else:
            turn(step, gap)
        if step == IN_CHUNKS - 1:
            v_other = swapped(after(v_back, gap), "dp", 1)
            mine, other = after(v_back, first.came), after(v_other, first.came)
            v_high = jnp.concatenate(
                [jnp.where(core == 0, mine, other), jnp.where(core == 0, other, mine)], 0
            )
            v_low = added(v_grad[: FF // 2], v_came[: FF // 2]).astype(BF)
            w_own[2] = jnp.where(mlp == 1, v_low, v_high)
        if 1 < step < 2 + last:
            r = step - 1
            out_came.append(lax.ppermute(after(outs[r], gap), "pipe", [(last, r - 1), (0, r)]))
            ready[step + 3].append(out_came[-1])
        if step == ends - DOWN_CHUNKS:
            w_came = collect_rows(after(first.rank, gap), streams, 0, IN_CHUNKS, (D, FF))
            w_other = swapped(w_came, "dp", 1)
            ready[step + 1].append(w_came)
    while rounds or waiting is not None:
        turn(ends, second.sent)
    rows_flat, grads_flat = unpack_rows(info, after(crop_global, second.sent), outs[0], out_came)
    in_grad = final_sum(w_own[:2], after(w_came, rows_flat), w_other, 8)
    d_came = collect_rows(after(first.rank, in_grad), streams, IN_CHUNKS, DOWN_CHUNKS, (FF // 2, D))
    d_other = swapped(d_came, "dp", 1)
    down_grad = final_sum(w_own[2:], d_came, d_other, 8)
    output_rows, tokens_grad = stacked_rows(rows_flat, crops), stacked_rows(grads_flat, crops)

    gain_grad = packed[:, :D]
    shift_grad = packed[:, D : 2 * D]
    outbias_grad = packed[:, 2 * D : 3 * D]
    qv_grad = packed[0::2, 3 * D : 5 * D].reshape(2, 2, D)
    first_grad = packed[1::2, 3 * D : 3 * D + FF]
    rel_out = packed[0::2, 3 * D + FF :].reshape(2, HEADS, SPAN).transpose(0, 2, 1)

    return (
        output_rows,
        tokens_grad,
        in_grad[None],
        down_grad[None],
        gain_grad,
        shift_grad,
        outbias_grad,
        qv_grad,
        first_grad,
        rel_out,
    )


def solution(mesh):
    return jax.shard_map(
        on_device,
        mesh=mesh,
        in_specs=(
            P("dp", None, "pipe"),
            P("dp", None, "pipe"),
            P("pipe", None, None),
            P("pipe", None, None),
            P(),
            P(),
            P(),
            P(),
            P(),
            P(),
            P(),
            P("dp"),
            P("dp", None),
        ),
        out_specs=(
            P("dp", None, "pipe"),
            P("dp", None, "pipe"),
            P("pipe", None, None),
            P("pipe", None, None),
            P(),
            P(),
            P(),
            P(),
            P(),
            P(),
        ),
        check_vma=False,
    )
```

```python
import functools

import jax
import jax.numpy as jnp
import numpy as np
from jax import lax
from jax.experimental import pallas as pl
from jax.experimental.pallas import tpu as pltpu
from jax.sharding import PartitionSpec as P

HEADS = 24
HEAD = 32
FF = 3072
D = 768
WIN = 7
SMALL_SIDE = 3
SECTIONS = 4
MICRO = 4
POS = 49
SPAN = 169
SMALL = SMALL_SIDE * SMALL_SIDE

T = 128
PAIR = 2
R = PAIR * T
SMALL_AT = 2 * POS
GROUP = 4
TABLE = 256
IN_CHUNKS = 4
DOWN_CHUNKS = 2
CHUNKS = IN_CHUNKS + DOWN_CHUNKS
LINE = D // IN_CHUNKS

EPSILON = 1e-05
NEGATIVE = -1e30
SQRT_HALF = 0.7071067811865476
INV_SQRT_TAU = 0.3989422804014327
SCALE = HEAD**-0.5
BF = jnp.bfloat16
F32 = jnp.float32
VM = pl.BlockSpec(memory_space=pltpu.VMEM)
SM = pl.BlockSpec(memory_space=pltpu.SMEM)
LIMIT = 17 << 20
SMALL_LIMIT = 13 << 20
TINY_LIMIT = 8 << 20


LITTLE = pl.CostEstimate(flops=0, transcendentals=0, bytes_accessed=1024)


def pin(x):
    return pltpu.with_memory_space_constraint(x, pltpu.VMEM)


def like(x):
    return jax.ShapeDtypeStruct(x.shape, x.dtype)


def shape(dims, kind):
    return jax.ShapeDtypeStruct(dims, kind)


def nn(a, b):
    return lax.dot_general(a, b, (((1,), (0,)), ((), ())), preferred_element_type=F32)


def nt(a, b):
    return lax.dot_general(a, b, (((1,), (1,)), ((), ())), preferred_element_type=F32)


def tn(a, b):
    return lax.dot_general(a, b, (((0,), (0,)), ((), ())), preferred_element_type=F32)


def tile_layout():
    slot = np.full((T,), -1, np.int32)
    place = np.zeros((T,), np.int32)
    for big in range(2):
        slot[big * POS : (big + 1) * POS] = big
        place[big * POS : (big + 1) * POS] = np.arange(POS)
    small = np.array([r * WIN + c for r in range(SMALL_SIDE) for c in range(SMALL_SIDE)], np.int32)
    for k in range(3):
        at = SMALL_AT + SMALL * k
        slot[at : at + SMALL] = 2 + k
        place[at : at + SMALL] = small
    return slot, place


def pair_index():
    slot, place = tile_layout()
    row, col = place // WIN, place % WIN
    half = WIN // 2
    out, where = [], []
    for block in range(2):
        r, c = (row, col) if block == 0 else ((row - half) % WIN, (col - half) % WIN)
        index = (r[:, None] - r[None, :] + WIN - 1) * (2 * WIN - 1) + c[:, None] - c[None, :] + WIN - 1
        same = (slot[:, None] == slot[None, :]) & (slot[:, None] >= 0)
        out.append(np.where(same, index, TABLE - 1).astype(np.int32))
        where.append((r * WIN + c).astype(np.int32))
    return np.stack(out), where[1]


def crop_bases(flags, crops):
    bigs, smalls, found = jnp.int32(0), jnp.int32(0), []
    for c in range(crops):
        flag = flags[c]
        third = (smalls * 11) >> 5
        big_at = (bigs >> 1) * T + (bigs & 1) * POS
        small_at = third * T + SMALL_AT + SMALL * (smalls - 3 * third)
        found.append((flag, jnp.where(flag == 1, big_at, small_at)))
        bigs = bigs + flag
        smalls = smalls + (1 - flag)
    return found


def landing(flags, crops, axis):
    rows = POS * crops
    dims = (rows, 1) if axis == 0 else (1, rows)
    at = lax.broadcasted_iota(jnp.int32, dims, axis)
    place = at // crops
    crop = at - place * crops
    row = place // WIN
    col = place - row * WIN
    inside = (row < SMALL_SIDE) & (col < SMALL_SIDE)
    small = jnp.where(inside, row * SMALL_SIDE + col, -T * crops)
    out = jnp.full(dims, -1, jnp.int32)
    for c, (flag, base) in enumerate(crop_bases(flags, crops)):
        out = jnp.where(crop == c, base + jnp.where(flag == 1, place, small), out)
    return out


def pack_kernel(crops, info, flags, tokens, cotangent, *outs):
    section = info[0]
    target = lax.broadcasted_iota(jnp.int32, (R, POS * crops), 0)
    lands = landing(flags, crops, 1)

    @pl.loop(0, info[1])
    def _(t):
        picks = (target + t * R == lands).astype(F32).astype(BF)
        packed = [nn(picks, rows[...]).astype(BF) for rows in (tokens, cotangent)]
        for r, out in enumerate(outs):
            is_last = section == SECTIONS - 1 - r

            @pl.when(is_last)
            def _():
                out[t] = packed[1]

            @pl.when(jnp.logical_not(is_last))
            def _():
                out[t] = packed[0]


def pack_rows(info, flags, tokens, cotangent, chunks):
    rows, width = tokens.shape
    crops = rows // POS
    return pl.pallas_call(
        functools.partial(pack_kernel, crops),
        out_shape=[shape((chunks, R, width), BF)] * SECTIONS,
        in_specs=[SM, SM, VM, VM],
        out_specs=[VM] * SECTIONS,
        compiler_params=pltpu.CompilerParams(vmem_limit_bytes=TINY_LIMIT),
        cost_estimate=LITTLE,
        name="pack_rows",
    )(info, flags, tokens, cotangent)


def unpack_kernel(crops, info, flags, own, came1, came2, came3, rows_out, grad_out):
    section = info[0]
    lands = landing(flags, crops, 0)
    total = own.shape[0] * R
    target = lax.broadcasted_iota(jnp.int32, (POS * crops, total), 1)
    picks = (target == lands).astype(F32).astype(BF)
    came = (own, came1, came2, came3)
    used = lax.broadcasted_iota(jnp.int32, (total, own.shape[2]), 0) < info[1] * R

    def rows_of(ref):
        block = ref[...].reshape(total, -1).astype(F32)
        return jnp.where(used, block, 0.0).astype(BF)

    for s in range(SECTIONS):

        @pl.when(section == s)
        def _():
            rows_out[...] = nn(picks, rows_of(came[(s + 1) % SECTIONS])).astype(BF)
            grad_out[...] = nn(picks, rows_of(came[s]))


def unpack_rows(info, flags, own, came):
    width = own.shape[2]
    crops = flags.shape[0]
    return pl.pallas_call(
        functools.partial(unpack_kernel, crops),
        out_shape=[shape((POS * crops, width), BF), shape((POS * crops, width), F32)],
        in_specs=[SM, SM] + [VM] * 4,
        out_specs=[VM, VM],
        compiler_params=pltpu.CompilerParams(vmem_limit_bytes=TINY_LIMIT),
        cost_estimate=LITTLE,
        name="unpack_rows",
    )(info, flags, own, *came)


ROWS_AT_ONCE = 8


def onehot_rows(index, it):
    rows = index[pl.ds(it * ROWS_AT_ONCE, ROWS_AT_ONCE), :]
    entry = lax.broadcasted_iota(jnp.int32, (TABLE, T), 0)
    parts = [(entry == rows[r : r + 1, :]).astype(F32).astype(BF) for r in range(ROWS_AT_ONCE)]
    return jnp.concatenate(parts, 1)


def split3(x):
    top = x.astype(BF)
    rest = x - top.astype(F32)
    middle = rest.astype(BF)
    return top, middle, (rest - middle.astype(F32)).astype(BF)


def spread_kernel(index, table, out):
    parts = split3(table[...])

    @pl.loop(0, T // ROWS_AT_ONCE)
    def _(it):
        picks = onehot_rows(index, it)
        values = nn(parts[0], picks) + nn(parts[1], picks) + nn(parts[2], picks)
        for r in range(ROWS_AT_ONCE):
            out[:, it * ROWS_AT_ONCE + r, :] = values[:HEADS, r * T : (r + 1) * T]


def spread_table(index, table):
    return pl.pallas_call(
        spread_kernel,
        out_shape=shape((HEADS, T, T), F32),
        in_specs=[VM, VM],
        out_specs=VM,
        compiler_params=pltpu.CompilerParams(vmem_limit_bytes=TINY_LIMIT),
        cost_estimate=LITTLE,
        name="spread_table",
    )(index, table)


def fold_kernel(index, sums, out):
    out[...] = jnp.zeros_like(out)

    @pl.loop(0, T // ROWS_AT_ONCE)
    def _(it):
        picks = onehot_rows(index, it)
        rows = jnp.concatenate([sums[:, it * ROWS_AT_ONCE + r, :] for r in range(ROWS_AT_ONCE)], 1)
        top = rows.astype(BF)
        rest = (rows - top.astype(F32)).astype(BF)
        out[...] += nt(top, picks) + nt(rest, picks)


def fold_table(index, sums):
    return pl.pallas_call(
        fold_kernel,
        out_shape=shape((HEADS, TABLE), F32),
        in_specs=[VM, VM],
        out_specs=VM,
        compiler_params=pltpu.CompilerParams(vmem_limit_bytes=TINY_LIMIT),
        cost_estimate=LITTLE,
        name="fold_table",
    )(index, pin(sums))


def row_norm(x):
    mean = jnp.sum(x, -1, keepdims=True) * (1.0 / D)
    centered = x - mean
    var = jnp.sum(centered * centered, -1, keepdims=True) * (1.0 / D)
    inv = lax.rsqrt(var + EPSILON)
    return centered * inv, inv


def head_masks():
    lane = lax.broadcasted_iota(jnp.int32, (T, T), 1)
    return [(lane >= HEAD * h) & (lane < HEAD * (h + 1)) for h in range(GROUP)]


def spread_heads(block, masks):
    zero = jnp.zeros_like(block)
    return jnp.concatenate([jnp.where(m, block, zero) for m in masks], 0)


def gather_heads(stacked, masks):
    total = stacked[0:T]
    for h in range(1, GROUP):
        total = jnp.where(masks[h], stacked[h * T : (h + 1) * T], total)
    return total


def lanes(at, size=T):
    return pl.ds(pl.multiple_of(at, T), size)


STEP = 512
BLOCKS = FF // STEP


def attention_forward(x, n, vec, wide, w, bias, a, b, save_a, save_b, y):

    @pl.loop(0, 3)
    def _(s):
        cols = lanes(s * D, D)
        a[:, cols] = (nn(n, w[:, cols]) + wide[0:1, cols]).astype(BF)

    save_a[0].start()
    masks = head_masks()

    @pl.loop(0, PAIR)
    def _(t):
        rows = pl.ds(pl.multiple_of(t * T, T), T)
        for grp in range(HEADS // GROUP):
            lo = grp * T
            heads = slice(grp * GROUP, (grp + 1) * GROUP)
            q, k, v = (a[rows, lo + s * D : lo + s * D + T] for s in range(3))
            s = nt(spread_heads(q, masks), k) * SCALE + bias[heads].reshape(GROUP * T, T)
            e = jnp.exp(s - jnp.max(s, -1, keepdims=True))
            p = (e * (1.0 / jnp.sum(e, -1, keepdims=True))).astype(BF)
            b[t, heads] = p.reshape(GROUP, T, T)
            a[rows, 3 * D + lo : 3 * D + lo + T] = gather_heads(nn(p, v), masks).astype(BF)

    save_a[1].start()
    save_b.start()
    branch = nn(a[:, 3 * D :], w[:, 3 * D :]) + vec[2:3, :]
    y[...] = (x + branch).astype(BF)


ERF_SLOPE = 0.3275911 * SQRT_HALF
ERF_TERMS = (1.061405429, -1.453152027, 1.421413741, -0.284496736, 0.254829592)


def normal_parts(u):
    bell = jnp.exp(-0.5 * u * u)
    base = 1.0 + ERF_SLOPE * jnp.abs(u)
    t = pl.reciprocal(base, approx=True)
    t = t * (2.0 - base * t)
    poly = 0.5 * ERF_TERMS[0]
    for term in ERF_TERMS[1:]:
        poly = poly * t + 0.5 * term
    tail = poly * t * bell
    return jnp.where(u >= 0, 1.0 - tail, tail), u * (bell * INV_SQRT_TAU)


def mlp_forward(x, n, vec, wide, w, v, a, b, acc):
    acc[...] = x + vec[2:3, :]

    @pl.loop(0, BLOCKS, step=2)
    def _(j0):
        blocks = []
        for jb in (j0, j0 + 1):
            cols = lanes(jb * STEP, STEP)
            u = nn(n, w[:, cols]) + wide[0:1, cols]
            cdf, rise = normal_parts(u)
            blocks.append((jb, cols, (u * cdf).astype(BF), (cdf + rise).astype(BF)))
        part = None
        for jb, cols, act, slope in blocks:
            a[:, cols] = act
            for t in range(PAIR):
                for i in range(STEP // T):
                    b[t, jb * (STEP // T) + i] = slope[t * T : (t + 1) * T, i * T : (i + 1) * T]
            term = nn(act, v[cols, :])
            part = term if part is None else part + term
        acc[...] += part


def forward_kernel(both, info, slot, vec, wide, bias, w, *refs):
    v = refs[0] if both else None
    p0, p1, p2, p3, came = refs[both : both + 5]
    y, *kept = refs[both + 13 :]
    xs, keep_n, keep_a, keep_b, *outs = kept[:8]
    x_in, n, a, b, acc, parts, sems = kept[8:]
    width = parts.shape[-1]
    section, used = info[0], info[1]
    c = slot[0] - section

    def copy(source, target, k):
        return pltpu.make_async_copy(source, target, sems.at[k])

    save_x, save_n = copy(x_in, xs.at[c], 0), copy(n, keep_n.at[c], 1)
    save_b = copy(b, keep_b.at[c], 3)
    early = [copy(a.at[:, cut], keep_a.at[c, :, cut], 2) for cut in (pl.ds(0, 3 * D), pl.ds(3 * D, D))]
    put = [copy(parts.at[d], outs[(d + 1) % SECTIONS].at[c], 4 + d) for d in range(SECTIONS)]

    @pl.when((c >= slot[1]) & (c < jnp.minimum(slot[2], used)))
    def _():
        @pl.when(section == 0)
        def _():
            bring = [copy(p.at[c], parts.at[d], 4 + d) for d, p in enumerate((p0, p3, p2, p1))]
            for one in bring:
                one.start()
            for one in bring:
                one.wait()
            x_in[...] = jnp.concatenate([parts[d] for d in range(SECTIONS)], -1)

        @pl.when(section != 0)
        def _():
            x_in[...] = came[...]

        save_x.start()
        x = x_in[...].astype(F32)
        raw, _ = row_norm(x)
        normed = (raw * vec[0:1, :] + vec[1:2, :]).astype(BF)
        n[...] = normed
        save_n.start()

        @pl.when(section % 2 == 0)
        def _():
            attention_forward(x, normed, vec, wide, w, bias, a, b, early, save_b, y)

        if both:

            @pl.when(section % 2 == 1)
            def _():
                mlp_forward(x, normed, vec, wide, w, v, a, b, acc)
                for one in early:
                    one.start()
                save_b.start()
                y[...] = acc[...].astype(BF)

        @pl.when(both & (section == SECTIONS - 1))
        def _():
            for d in range(SECTIONS):
                parts[d] = y[:, d * width : (d + 1) * width]
                put[d].start()
            for d in range(SECTIONS):
                put[d].wait()

        save_x.wait()
        save_n.wait()
        for one in early:
            one.wait()
        save_b.wait()


ANY = pl.BlockSpec(memory_space=pl.ANY)


def far(x):
    return pltpu.with_memory_space_constraint(x, pltpu.HBM)


def run_forward(info, slot, pieces, came, vec, wide, w, v, bias, kept):
    count = len(kept)
    width = pieces[0].shape[-1]
    both = v is not None
    weights = [pin(w), pin(v)] if both else [pin(w)]
    outs = pl.pallas_call(
        functools.partial(forward_kernel, both),
        out_shape=[shape((R, D), BF)] + [like(r) for r in kept],
        in_specs=[SM, SM] + [VM] * (4 + both) + [ANY] * 4 + [VM] + [ANY] * count,
        out_specs=[VM] + [ANY] * count,
        scratch_shapes=[
            pltpu.VMEM((R, D), BF),
            pltpu.VMEM((R, D), BF),
            pltpu.VMEM((R, FF), BF),
            pltpu.VMEM((PAIR, HEADS, T, T), BF),
            pltpu.VMEM((R, D), F32),
            pltpu.VMEM((SECTIONS, R, width), BF),
            pltpu.SemaphoreType.DMA((4 + SECTIONS,)),
        ],
        input_output_aliases={11 + both + i: 1 + i for i in range(count)},
        compiler_params=pltpu.CompilerParams(vmem_limit_bytes=SMALL_LIMIT),
        cost_estimate=LITTLE,
        name="section_forward",
    )(info, slot, vec, wide, pin(bias), *weights, *pieces, came, *[far(r) for r in kept])
    return outs[0], list(outs[1:])


def norm_backward(x, g, dn, vec, sums, gx):
    raw, inv = row_norm(x)
    sums[0:1, :] += jnp.sum(dn * raw, 0, keepdims=True)
    sums[1:2, :] += jnp.sum(dn, 0, keepdims=True)
    sums[2:3, :] += jnp.sum(g, 0, keepdims=True)
    s = dn * vec[0:1, :]
    m1 = jnp.sum(s, -1, keepdims=True) * (1.0 / D)
    m2 = jnp.sum(s * raw, -1, keepdims=True) * (1.0 / D)
    gx[...] = (g + inv * (s - m1 - raw * m2)).astype(BF)


def attention_backward(g, w, a, b, bring_a, bring_b, d, acc, save_d, dsum):
    masks = head_masks()
    d[:, 3 * D :] = g
    d[:, 0:D] = nt(g, w[:, 3 * D :]).astype(BF)
    bring_a.wait()
    bring_b.wait()

    @pl.loop(0, PAIR)
    def _(t):
        rows = pl.ds(pl.multiple_of(t * T, T), T)
        for grp in range(HEADS // GROUP):
            lo = grp * T
            heads = slice(grp * GROUP, (grp + 1) * GROUP)
            q, k, v = (a[rows, lo + s * D : lo + s * D + T] for s in range(3))
            p = b[t, heads].reshape(GROUP * T, T)
            do_heads = spread_heads(d[rows, lo : lo + T], masks)
            dv = tn(p, do_heads)
            pf = p.astype(F32)
            pdp = pf * nt(do_heads, v)
            ds = (pdp - pf * jnp.sum(pdp, -1, keepdims=True)).astype(BF)
            dsum[heads] += ds.astype(F32).reshape(GROUP, T, T)
            dq = gather_heads(nn(ds, k), masks) * SCALE
            dk = tn(ds, spread_heads(q, masks)) * SCALE
            d[rows, lo : lo + T] = dq.astype(BF)
            d[rows, D + lo : D + lo + T] = dk.astype(BF)
            d[rows, 2 * D + lo : 2 * D + lo + T] = dv.astype(BF)

    save_d.start()
    acc[...] = jnp.zeros_like(acc)

    @pl.loop(0, 3)
    def _(s):
        cols = lanes(s * D, D)
        acc[...] += nt(d[:, cols], w[:, cols])


def mlp_backward(g, w, v, b, bring_b, d, acc):
    acc[...] = jnp.zeros_like(acc)
    bring_b.wait()

    @pl.loop(0, BLOCKS, step=2)
    def _(j0):
        blocks = []
        for jb in (j0, j0 + 1):
            cols = lanes(jb * STEP, STEP)
            da = nt(g, v[cols, :]).astype(BF).astype(F32)
            slope = jnp.concatenate(
                [
                    jnp.concatenate([b[t, jb * (STEP // T) + i] for i in range(STEP // T)], 1)
                    for t in range(PAIR)
                ],
                0,
            )
            blocks.append((cols, (da * slope.astype(F32)).astype(BF)))
        part = None
        for cols, du in blocks:
            d[:, cols] = du
            term = nt(du, w[:, cols])
            part = term if part is None else part + term
        acc[...] += part


def seed_rows(scales, c):
    row = lax.broadcasted_iota(jnp.int32, (T, 1), 0)
    parts = []
    for t in range(PAIR):
        base = (c * PAIR + t) * 8
        out = jnp.full((T, 1), scales[base], F32)
        for k, at in enumerate([POS] + [SMALL_AT + SMALL * i for i in range(3)]):
            out = jnp.where(row >= at, scales[base + 1 + k], out)
        parts.append(out)
    return jnp.concatenate(parts, 0)


def backward_kernel(info, slot, scales, vec, w, v, dsum_in, sums_in, p0, p1, p2, p3, came, *refs):
    gx, dsum, sums, *kept = refs[9:]
    xs, keep_a, keep_b, gs, keep_d, *outs = kept[:9]
    x_in, g_tile, a, b, d, acc, parts, sems = kept[9:]
    width = parts.shape[-1]
    section, used = info[0], info[1]
    c = slot[0] - (SECTIONS - 1 - section)

    def copy(source, target, k):
        return pltpu.make_async_copy(source, target, sems.at[k])

    bring_x, bring_a, bring_b = copy(xs.at[c], x_in, 0), copy(keep_a.at[c], a, 1), copy(keep_b.at[c], b, 2)
    save_g, save_d = copy(g_tile, gs.at[c], 3), copy(d, keep_d.at[c], 4)
    put = [copy(parts.at[k], outs[k].at[c], 5 + k) for k in range(SECTIONS)]

    @pl.when((c >= slot[1]) & (c < jnp.minimum(slot[2], used)))
    def _():
        @pl.when(section == SECTIONS - 1)
        def _():
            bring = [copy(p.at[c], parts.at[k], 5 + k) for k, p in enumerate((p3, p2, p1, p0))]
            for one in bring:
                one.start()
            bring_b.start()
            for one in bring:
                one.wait()
            seed = jnp.concatenate([parts[k] for k in range(SECTIONS)], -1).astype(F32)
            g_tile[...] = (seed * seed_rows(scales, c)).astype(BF)

        @pl.when(section != SECTIONS - 1)
        def _():
            bring_b.start()
            g_tile[...] = came[...]

        pl.when(section % 2 == 0)(bring_a.start)
        bring_x.start()
        save_g.start()

        @pl.when(c == 0)
        def _():
            dsum[...] = jnp.zeros_like(dsum)
            sums[...] = jnp.zeros_like(sums)

        g = g_tile[...]

        @pl.when(section % 2 == 0)
        def _():
            attention_backward(g, w, a, b, bring_a, bring_b, d, acc, save_d, dsum)

        @pl.when(section % 2 == 1)
        def _():
            mlp_backward(g, w, v, b, bring_b, d, acc)
            save_d.start()

        bring_x.wait()
        norm_backward(x_in[...].astype(F32), g.astype(F32), acc[...], vec, sums, gx)

        @pl.when(section == 0)
        def _():
            for k in range(SECTIONS):
                parts[k] = gx[:, k * width : (k + 1) * width]
                put[k].start()
            for k in range(SECTIONS):
                put[k].wait()

        save_g.wait()
        save_d.wait()


def run_backward(info, slot, scales, pieces, came, vec, w, v, dsum, sums, kept):
    count = len(kept)
    width = pieces[0].shape[-1]
    outs = pl.pallas_call(
        backward_kernel,
        out_shape=[shape((R, D), BF)] + [like(r) for r in (dsum, sums, *kept)],
        in_specs=[SM, SM, SM] + [VM] * 5 + [ANY] * 4 + [VM] + [ANY] * count,
        out_specs=[VM] * 3 + [ANY] * count,
        scratch_shapes=[
            pltpu.VMEM((R, D), BF),
            pltpu.VMEM((R, D), BF),
            pltpu.VMEM((R, FF), BF),
            pltpu.VMEM((PAIR, HEADS, T, T), BF),
            pltpu.VMEM((R, FF), BF),
            pltpu.VMEM((R, D), F32),
            pltpu.VMEM((SECTIONS, R, width), BF),
            pltpu.SemaphoreType.DMA((5 + SECTIONS,)),
        ],
        input_output_aliases={6: 1, 7: 2} | {13 + i: 3 + i for i in range(count)},
        compiler_params=pltpu.CompilerParams(vmem_limit_bytes=SMALL_LIMIT),
        cost_estimate=LITTLE,
        name="section_backward",
    )(
        info, slot, scales, vec, pin(w), pin(v), pin(dsum), pin(sums), *pieces, came,
        *[far(r) for r in kept],
    )
    return outs[0], outs[1], outs[2], list(outs[3:])


def make_room(dims):
    def body(*refs):
        pass

    return pl.pallas_call(
        body,
        out_shape=[pltpu.VMEM(d, k) if near else pltpu.HBM(d, k) for d, k, near in dims],
        out_specs=[VM if near else ANY for _, _, near in dims],
        compiler_params=pltpu.CompilerParams(vmem_limit_bytes=TINY_LIMIT),
        name="make_room",
    )()


def clear(ref, used, *at):
    @pl.loop(used, ref.shape[len(at)])
    def _(t):
        ref[(*at, t)] = jnp.zeros(ref.shape[-2:], BF)


def in_kernel(usual, info, keep_n, keep_a, keep_d, top, low, wide_sums, turned, n, a, d, tile, in_sems):
    chunks = n.shape[0]
    rows = chunks * R
    mlp, used = info[0] % 2, info[1]
    part = D // 2
    half = STEP // 2

    def bring(jb, first, count):
        cut = pl.ds(first, count)
        return pltpu.make_async_copy(
            keep_d.at[cut, :, pl.ds(jb * STEP, STEP)], d.at[jb, cut], in_sems.at[jb]
        )

    def others(work):
        for c in range(usual, chunks):
            pl.when(used > c)(functools.partial(work, c))

    bring_n = pltpu.make_async_copy(keep_n, n, in_sems.at[BLOCKS])
    bring_a = pltpu.make_async_copy(keep_a.at[:, :, pl.ds(3 * D, D)], a, in_sems.at[BLOCKS + 1])
    bring_n.start()
    for jb in range(BLOCKS):
        bring(jb, 0, usual).start()
    others(lambda c: [bring(jb, c, 1).start() for jb in range(BLOCKS)] and None)
    bring_a.start()
    bring_n.wait()
    clear(n, used)
    turned[0] = n[...].reshape(rows, D).T
    bring_a.wait()
    clear(a, used)

    @pl.when(mlp == 0)
    def _():
        turned[1] = a[...].reshape(rows, D).T

    @pl.when(mlp == 1)
    def _():
        turned[1] = turned[0]

    @pl.loop(0, BLOCKS)
    def _(jb):
        bring(jb, 0, usual).wait()
        others(lambda c: bring(jb, c, 1).wait())
        clear(d, used, jb)
        block = d[jb, :usual].reshape(usual * R, STEP)
        cols = lanes(jb * STEP, STEP)
        wide_sums[0:1, cols] = jnp.sum(block.astype(F32), 0, keepdims=True)

        def add_sum(c):
            wide_sums[0:1, cols] += jnp.sum(d[jb, c].astype(F32), 0, keepdims=True)

        others(add_sum)
        for k in range(2):
            late = (jb * 2 + k >= 3 * D // half).astype(jnp.int32)
            cut = slice(k * half, (k + 1) * half)
            tile[...] = nn(turned[late, :, : usual * R], block[:, cut])

            def add(c):
                tile[...] += nn(turned[late, :, c * R : (c + 1) * R], d[jb, c, :, cut])

            others(add)
            grad = tile[...].astype(BF)
            to = lanes(jb * STEP + k * half, half)
            top[:, to] = grad[:part]
            low[:, to] = grad[part:]


def in_grads(info, keep_n, keep_a, keep_d, usual):
    chunks = keep_n.shape[0]
    return pl.pallas_call(
        functools.partial(in_kernel, usual),
        out_shape=[pltpu.VMEM((D // 2, FF), BF)] * 2 + [shape((8, FF), F32)],
        in_specs=[SM] + [ANY] * 3,
        out_specs=[VM] * 3,
        scratch_shapes=[
            pltpu.VMEM((2, D, chunks * R), BF),
            pltpu.VMEM((chunks, R, D), BF),
            pltpu.VMEM((chunks, R, D), BF),
            pltpu.VMEM((BLOCKS, chunks, R, STEP), BF),
            pltpu.VMEM((D, STEP // 2), F32),
            pltpu.SemaphoreType.DMA((BLOCKS + 2,)),
        ],
        compiler_params=pltpu.CompilerParams(vmem_limit_bytes=LIMIT),
        cost_estimate=LITTLE,
        name="in_grads",
    )(info, *[far(r) for r in (keep_n, keep_a, keep_d)])


def down_kernel(usual, info, keep_a, gs, grad, a, g, tile, out, in_sems, out_sems):
    chunks = g.shape[0]
    mlp, used = info[0] % 2, info[1]

    def bring(jb, first, count):
        cut = pl.ds(first, count)
        return pltpu.make_async_copy(
            keep_a.at[cut, :, pl.ds(jb * STEP, STEP)], a.at[jb, cut], in_sems.at[jb]
        )

    def put(jb):
        return pltpu.make_async_copy(out.at[jb % 2], grad.at[pl.ds(jb * STEP, STEP), :], out_sems.at[jb % 2])

    def others(work):
        for c in range(usual, chunks):
            pl.when(used > c)(functools.partial(work, c))

    @pl.when(mlp == 1)
    def _():
        bring_g = pltpu.make_async_copy(gs, g, in_sems.at[BLOCKS])
        bring_g.start()
        for jb in range(BLOCKS):
            bring(jb, 0, usual).start()
        others(lambda c: [bring(jb, c, 1).start() for jb in range(BLOCKS)] and None)
        bring_g.wait()
        clear(g, used)
        flat_g = g[:usual].reshape(usual * R, D)

        @pl.loop(0, BLOCKS)
        def _(jb):
            bring(jb, 0, usual).wait()
            others(lambda c: bring(jb, c, 1).wait())
            clear(a, used, jb)

            @pl.when(jb >= 2)
            def _():
                put(jb - 2).wait()

            tile[...] = tn(a[jb, :usual].reshape(usual * R, STEP), flat_g)

            def add(c):
                tile[...] += tn(a[jb, c], g[c])

            others(add)
            out[jb % 2] = tile[...].astype(BF)
            put(jb).start()

        for jb in (BLOCKS - 2, BLOCKS - 1):
            put(jb).wait()


def down_grads(info, keep_a, gs, usual):
    chunks = gs.shape[0]
    dma = pltpu.SemaphoreType.DMA
    return pl.pallas_call(
        functools.partial(down_kernel, usual),
        out_shape=shape((FF, D), BF),
        in_specs=[SM] + [ANY] * 2,
        out_specs=ANY,
        scratch_shapes=[
            pltpu.VMEM((BLOCKS, chunks, R, STEP), BF),
            pltpu.VMEM((chunks, R, D), BF),
            pltpu.VMEM((STEP, D), F32),
            pltpu.VMEM((2, STEP, D), BF),
            dma((BLOCKS + 1,)),
            dma((2,)),
        ],
        compiler_params=pltpu.CompilerParams(vmem_limit_bytes=LIMIT),
        cost_estimate=LITTLE,
        name="down_grads",
    )(info, far(keep_a), far(gs))


def swapped(block, axis, bit):
    size = lax.axis_size(axis)
    return lax.ppermute(block, axis, [(i, i ^ bit) for i in range(size)])


def butterfly(block, axis):
    size = lax.axis_size(axis)
    if size & (size - 1):
        return lax.psum(block, axis)
    bit = 1
    while bit < size:
        block = block + swapped(block, axis, bit)
        bit *= 2
    return block


PARTS = 8


def pair_sum_kernel(mine, came, own, parcel, sems):
    rows = mine.shape[0] // PARTS
    moves = [
        pltpu.make_async_copy(came.at[pl.ds(k * rows, rows)], parcel.at[k], sems.at[k]) for k in range(PARTS)
    ]
    for move in moves:
        move.start()
    for move in moves:
        move.wait()

    @pl.loop(0, PARTS)
    def _(k):
        at = pl.ds(pl.multiple_of(k * rows, rows), rows)
        own[at, :] = (mine[at, :].astype(F32) + parcel[k].astype(F32)).astype(BF)


def pair_sum(mine, came):
    rows, cols = mine.shape
    return pl.pallas_call(
        pair_sum_kernel,
        out_shape=pltpu.VMEM(mine.shape, BF),
        in_specs=[VM, ANY],
        out_specs=VM,
        scratch_shapes=[pltpu.VMEM((PARTS, rows // PARTS, cols), BF), pltpu.SemaphoreType.DMA((PARTS,))],
        compiler_params=pltpu.CompilerParams(vmem_limit_bytes=TINY_LIMIT),
        cost_estimate=LITTLE,
        name="pair_sum",
    )(pin(mine), came)


def final_sum_kernel(count, blocks, came, other, *refs):
    owns, (out, parcel, wide, in_sems, out_sems) = refs[:count], refs[count:]
    rows = came.shape[0] // blocks
    each = blocks // count

    def bring(k):
        return pltpu.make_async_copy(other.at[pl.ds(k * rows, rows)], parcel.at[k], in_sems.at[k])

    def put(k):
        return pltpu.make_async_copy(wide.at[k % 2], out.at[pl.ds(k * rows, rows)], out_sems.at[k % 2])

    @pl.loop(0, blocks)
    def _(k):
        bring(k).start()

    for part, own in enumerate(owns):

        @pl.loop(0, each)
        def _(j):
            k = part * each + j
            bring(k).wait()

            @pl.when(k >= 2)
            def _():
                put(k - 2).wait()

            near = pl.ds(pl.multiple_of(j * rows, rows), rows)
            far_rows = pl.ds(pl.multiple_of(k * rows, rows), rows)
            value = own[near, :].astype(F32) + came[far_rows, :].astype(F32)
            wide[k % 2] = value + parcel[k].astype(F32)
            put(k).start()

    for k in range(blocks - 2, blocks):
        put(k).wait()


def final_sum(owns, came, other, blocks):
    rows, cols = came.shape
    return pl.pallas_call(
        functools.partial(final_sum_kernel, len(owns), blocks),
        out_shape=shape((rows, cols), F32),
        in_specs=[VM, ANY] + [VM] * len(owns),
        out_specs=ANY,
        scratch_shapes=[
            pltpu.VMEM((blocks, rows // blocks, cols), BF),
            pltpu.VMEM((2, rows // blocks, cols), F32),
            pltpu.SemaphoreType.DMA((blocks,)),
            pltpu.SemaphoreType.DMA((2,)),
        ],
        compiler_params=pltpu.CompilerParams(vmem_limit_bytes=10 << 20),
        cost_estimate=LITTLE,
        name="final_sum",
    )(pin(came), other, *[pin(x) for x in owns])


def line_kernel(stream, count, step, rank, came, *refs):
    tops, send = refs[:count], refs[count]
    chunk = step[0] - rank[0]
    at = stream * FF // 2

    def put(source, row, cuts):
        for k, (down_by, col) in enumerate(cuts):
            rows = pl.ds(pl.multiple_of(row + down_by, LINE), LINE)
            value = source[rows, col : col + D]

            @pl.when(rank[0] == 0)
            def _():
                send[k] = value

            @pl.when(rank[0] > 0)
            def _():
                send[k] = (value.astype(F32) + came[k].astype(F32)).astype(BF)

    side_by_side = ((0, at), (0, at + D))
    for half, source in enumerate(tops[:2]):
        first = half * IN_CHUNKS // 2

        @pl.when((chunk >= first) & (chunk < first + IN_CHUNKS // 2))
        def _():
            put(source, (chunk - first) * LINE, side_by_side)

    if count == 3:

        @pl.when((chunk >= IN_CHUNKS) & (chunk < CHUNKS))
        def _():
            put(tops[2], (chunk - IN_CHUNKS + stream * DOWN_CHUNKS) * 2 * LINE, ((0, 0), (LINE, 0)))


class LineSum:
    def __init__(self, place, core, length, stream):
        self.length, self.stream = length, stream
        self.rank = jnp.where(core == 0, place, length - 1 - place).reshape(1)
        self.came = jnp.zeros((2, LINE, D), BF)
        self.sends = CHUNKS + length - 2
        self.route = [(2 * z, 2 * z + 2) for z in range(length - 1)]
        self.route += [(2 * z + 3, 2 * z + 1) for z in range(length - 1)]
        self.kept = []

    def advance(self, step, owns):
        owns = owns[: 1 + (step >= IN_CHUNKS // 2) + (step >= IN_CHUNKS)]
        self.sent = pl.pallas_call(
            functools.partial(line_kernel, self.stream, len(owns)),
            out_shape=like(self.came),
            in_specs=[SM, SM] + [VM] * (1 + len(owns)),
            out_specs=VM,
            compiler_params=pltpu.CompilerParams(vmem_limit_bytes=TINY_LIMIT),
            cost_estimate=LITTLE,
            name="line_step",
        )(np.array([step], np.int32), self.rank, self.came, *[pin(x) for x in owns])
        self.came = lax.ppermute(self.sent, "dp", self.route)
        self.kept.append(self.came)


def collect_kernel(length, where, rank, *refs):
    kept, (out, zero, sems) = refs[:-3], refs[-3:]
    zero[...] = jnp.zeros_like(zero)

    def move(item, k, ref):
        row, col = where[item][1][k]
        to = out.at[pl.ds(row, LINE), pl.ds(col, D)]
        return pltpu.make_async_copy(ref, to, sems.at[item, k])

    for item, (index, _) in enumerate(where):
        for k in range(2):
            pl.when(rank[0] == 0)(move(item, k, zero).start)
            for r in range(1, length):
                pl.when(rank[0] == r)(move(item, k, kept[index[r - 1]].at[k]).start)
    for item in range(len(where)):
        for k in range(2):
            move(item, k, zero).wait()


def collect_rows(rank, streams, first, count, dims):
    length = streams[0].length
    kept, where = [], []
    for k, stream in enumerate(streams):
        for c in range(count):
            index = []
            for r in range(1, length):
                index.append(len(kept))
                kept.append(stream.kept[first + c + r - 1])
            if dims[1] == FF:
                spots = [(c * LINE, k * FF // 2), (c * LINE, k * FF // 2 + D)]
            else:
                spots = [((c + k * count) * 2 * LINE + half * LINE, 0) for half in range(2)]
            where.append((index, spots))
    return pl.pallas_call(
        functools.partial(collect_kernel, length, where),
        out_shape=pltpu.VMEM(dims, BF),
        in_specs=[SM] + [ANY] * len(kept),
        out_specs=VM,
        scratch_shapes=[pltpu.VMEM((LINE, D), BF), pltpu.SemaphoreType.DMA((len(where), 2))],
        compiler_params=pltpu.CompilerParams(vmem_limit_bytes=TINY_LIMIT),
        cost_estimate=LITTLE,
        name="collect_rows",
    )(rank, *kept)


def added(*parts):
    return sum(p.astype(F32) for p in parts)


def after(x, *first):
    return lax.optimization_barrier((x, *first))[0]


def flat_rows(x):
    return x.transpose(1, 0, 2).reshape(-1, x.shape[2])


def stacked_rows(x, crops):
    return x.reshape(POS, crops, -1).transpose(1, 0, 2)


def on_device(
    tokens,
    cotangent,
    in_weight,
    down_weight,
    norm_gain,
    norm_shift,
    out_bias,
    qv_bias,
    fc1_bias,
    rel_table,
    shift_regions,
    crop_global,
    micro_of,
):
    section = lax.axis_index("pipe")
    dp_index = lax.axis_index("dp")
    core, place = dp_index % 2, dp_index // 2
    dp_size = lax.axis_size("dp")
    mlp = section % 2
    block = section // 2
    crops = tokens.shape[0]
    chunks = (crops + 2 * PAIR - 1) // (2 * PAIR)
    last = SECTIONS - 1

    half = FF // 4
    sent = lax.dynamic_slice_in_dim(down_weight[0], core * half, half, 0)
    mine = lax.ppermute(sent, "pipe", [(s, s + 1) for s in range(0, SECTIONS, 2)])

    bigs_all = jnp.sum(crop_global)
    needed = jnp.maximum(
        (bigs_all + 2 * PAIR - 1) // (2 * PAIR), (crops - bigs_all + 3 * PAIR - 1) // (3 * PAIR)
    )
    info = after(jnp.stack([section, needed, core]).astype(jnp.int32), sent)
    packs = pack_rows(info, crop_global, flat_rows(tokens), flat_rows(cotangent), chunks)
    pieces = [packs[0]] + [
        lax.ppermute(packs[r], "pipe", [(SECTIONS - r, 0), (last - r, last)]) for r in range(1, SECTIONS)
    ]

    w = in_weight[0]

    vec = jnp.stack([norm_gain[section], norm_shift[section], out_bias[section]])
    qv = qv_bias[block]
    wide_attention = jnp.concatenate([qv[0], jnp.zeros((D,), F32), qv[1], jnp.zeros((D,), F32)])
    wide = jnp.where(mlp == 1, fc1_bias[block], wide_attention)[None]

    both, rolled = pair_index()
    regions = jnp.where(block == 1, shift_regions[rolled], 0)
    index = jnp.where(block == 1, both[1], both[0])
    index = jnp.where(regions[:, None] == regions[None, :], index, TABLE - 1)
    table = jnp.pad(
        rel_table[block].T, ((0, 32 - HEADS), (0, TABLE - SPAN)), constant_values=((0, 0), (0, NEGATIVE))
    )
    bias = spread_table(after(index, packs[0]), table)

    member = (micro_of == jnp.arange(MICRO, dtype=jnp.int32)[None, :]).astype(F32)
    crop_rows = jnp.where(crop_global == 1, POS, SMALL).astype(F32)
    counts = jnp.sum(member * crop_rows[:, None], 0)
    counts = jnp.concatenate([counts, needed.astype(F32).reshape(1)])
    count_rounds = [1 << k for k in range((dp_size - 1).bit_length())]
    before = np.tril(np.ones((crops, crops), np.int32), -1)
    bigs = jnp.sum(before * crop_global[None, :], 1)
    smalls = jnp.arange(crops, dtype=jnp.int32) - bigs
    entry = jnp.where(crop_global == 1, bigs // 2 * 8 + bigs % 2, smalls // 3 * 8 + 2 + smalls % 3)
    here = entry[:, None] == jnp.arange(chunks * PAIR * 8, dtype=jnp.int32)[None, :]

    width = tokens.shape[2]
    down_pipe = [(s, s + 1) for s in range(last)]
    up_pipe = [(s, s - 1) for s in range(1, SECTIONS)]

    dsum, sums, xs, keep_n, gs, keep_a, keep_d, keep_b, *outs = make_room(
        [((HEADS, T, T), F32, True), ((8, D), F32, True)]
        + [((chunks, R, D), BF, False)] * 3
        + [((chunks, R, FF), BF, False)] * 2
        + [((chunks, PAIR, HEADS, T, T), BF, False)]
        + [((chunks, R, width), BF, False)] * 4
    )
    usual = max(chunks - 1, 1)
    blank = jnp.zeros((R, D), BF)
    kept = [dsum, sums, xs, keep_n, gs, keep_a, keep_d, keep_b, *outs]

    def slot(at, first, stop):
        if isinstance(first, int):
            return np.array([first + at, first, stop], np.int32)
        return jnp.stack([first + at, first, stop]).astype(jnp.int32)

    def forward(i, first, stop, came, v, kept):
        dsum, sums, xs, keep_n, gs, keep_a, keep_d, keep_b, *outs = kept
        y, (xs, keep_n, keep_a, keep_b, *outs) = run_forward(
            info, slot(i, first, stop), pieces, came, vec, wide, w, v, bias,
            [xs, keep_n, keep_a, keep_b, *outs],
        )
        return y, [dsum, sums, xs, keep_n, gs, keep_a, keep_d, keep_b, *outs]

    def backward(j, first, stop, came, v, kept):
        dsum, sums, xs, keep_n, gs, keep_a, keep_d, keep_b, *outs = kept
        gx, dsum, sums, (xs, keep_a, keep_b, gs, keep_d, *outs) = run_backward(
            info, slot(j, first, stop), scales, pieces, came, vec, w, v,
            dsum, sums, [xs, keep_a, keep_b, gs, keep_d, *outs],
        )
        return gx, [dsum, sums, xs, keep_n, gs, keep_a, keep_d, keep_b, *outs]

    def count_round(counts, bit):
        other = swapped(counts, "dp", bit)
        return jnp.concatenate([counts[:MICRO] + other[:MICRO], jnp.maximum(counts, other)[MICRO:]])

    counts = count_round(counts, count_rounds[0])
    came_f, came_b = after(blank, counts), blank
    v = None
    for i in range(usual + 2 * last):
        if i < usual + last:
            y, kept = forward(i, 0, usual, came_f, v, kept)
            if i < usual + last - 1:
                came_f = lax.ppermute(y, "pipe", [(s, t) for s, t in down_pipe if 0 <= i - s < usual])
            if 0 < i < last:
                take = -(-len(count_rounds[1:]) // (last - 1))
                for bit in count_rounds[1:][(i - 1) * take : i * take]:
                    counts = count_round(after(counts, y), bit)
            if i == 0:
                mine = after(mine, y)
                other = swapped(mine, "dp", 1)
                upper = jnp.where(core == 0, mine, other), jnp.where(core == 0, other, mine)
                v = jnp.concatenate([down_weight[0], *upper], 0)
        if i == last:
            most = counts[MICRO].astype(jnp.int32)
            counts = counts[:MICRO]
            scales = jnp.sum(member * (jnp.sum(counts) / (MICRO * counts))[None], 1)
            scales = jnp.sum(jnp.where(here, scales[:, None], 0.0), 0)
        if i >= last:
            gx, kept = backward(i - last, 0, usual, came_b, v, kept)
            if i < usual + 2 * last - 1:
                came_b = lax.ppermute(gx, "pipe", [(s, t) for s, t in up_pipe if 0 <= i - 2 * last + s < usual])

    def beyond(k, carry):
        came_f, came_b, kept = carry
        c, at = usual + k // (2 * SECTIONS), k % (2 * SECTIONS)
        y, kept = forward(at, c, c + 1, came_f, v, kept)
        came_f = lax.ppermute(y, "pipe", down_pipe)
        gx, kept = backward(at - SECTIONS, c, c + 1, came_b, v, kept)
        came_b = lax.ppermute(gx, "pipe", up_pipe)
        return came_f, came_b, kept

    more = jnp.maximum(most - usual, 0) * (2 * SECTIONS)
    kept = lax.fori_loop(0, more, beyond, (blank, blank, kept))[2]
    dsum, sums, xs, keep_n, gs, keep_a, keep_d, keep_b, *outs = kept
    v_grad = down_grads(info, keep_a, gs, usual)
    w_top, w_low, wide_sums = in_grads(info, after(keep_n, v_grad), keep_a, keep_d, usual)

    route = [
        (s * dp_size + i, s * dp_size + (i ^ 1)) for s in range(1, SECTIONS, 2) for i in range(dp_size)
    ]
    v_came = lax.ppermute(v_grad, ("pipe", "dp"), route)
    out_came = []
    at = FF // 2 + half * core
    parts = [lax.dynamic_slice_in_dim(after(x, w_top), at, half, 0) for x in (v_grad, v_came)]
    v_part = added(*parts).astype(BF)
    v_back = lax.ppermute(v_part, "pipe", [(s + 1, s) for s in range(0, SECTIONS, 2)])
    w_own = [pair_sum(w_top, swapped(w_top, "dp", 1)), None, None]

    length = dp_size // 2
    first, second = streams = [LineSum(place, core, length, k) for k in range(2)]
    ends = streams[0].sends
    ready = [[]] + [[] for _ in range(ends + 8)]
    rounds = [("dp", 1 << k) for k in range((dp_size - 1).bit_length())] + [("pipe", 1), ("pipe", 2)]
    packed = waiting = None

    def turn(step, gap):
        nonlocal packed, waiting
        if waiting is not None:
            packed = packed + after(waiting, gap)
            waiting = None
            ready[step + 1].append(packed)
        if rounds:
            axis, bit = rounds.pop(0)
            if axis == "pipe" and bit == 1:
                packed = (jnp.arange(SECTIONS) == section).astype(F32)[:, None] * packed[None]
            waiting = swapped(after(packed, gap), axis, bit)

    for step in range(ends):
        first.came = after(first.came, *ready[step])
        first.advance(step, w_own)
        second.came = after(second.came, first.sent)
        second.advance(step, w_own)
        gap = second.sent
        ready[step + 1].append(gap)
        if step == 0:
            w_low = after(w_low, gap)
            w_own[1] = pair_sum(w_low, swapped(w_low, "dp", 1))
            rel_grad = fold_table(index, after(dsum, gap))
            narrow = jnp.where(
                mlp == 1,
                wide_sums[0],
                jnp.concatenate(
                    [wide_sums[0, :D], wide_sums[0, 2 * D : 3 * D], jnp.zeros((2 * D,), F32)]
                ),
            )
            packed = jnp.concatenate([sums[:3].reshape(-1), narrow, rel_grad[:, :SPAN].reshape(-1)])
            ready[1].append(packed)
        else:
            turn(step, gap)
        if step == IN_CHUNKS - 1:
            v_other = swapped(after(v_back, gap), "dp", 1)
            mine, other = after(v_back, first.came), after(v_other, first.came)
            v_high = jnp.concatenate(
                [jnp.where(core == 0, mine, other), jnp.where(core == 0, other, mine)], 0
            )
            v_low = added(v_grad[: FF // 2], v_came[: FF // 2]).astype(BF)
            w_own[2] = jnp.where(mlp == 1, v_low, v_high)
        if 1 < step < 2 + last:
            r = step - 1
            out_came.append(lax.ppermute(after(outs[r], gap), "pipe", [(last, r - 1), (0, r)]))
            ready[step + 3].append(out_came[-1])
        if step == ends - DOWN_CHUNKS:
            w_came = collect_rows(after(first.rank, gap), streams, 0, IN_CHUNKS, (D, FF))
            w_other = swapped(w_came, "dp", 1)
            ready[step + 1].append(w_came)
    while rounds or waiting is not None:
        turn(ends, second.sent)
    rows_flat, grads_flat = unpack_rows(info, after(crop_global, second.sent), outs[0], out_came)
    in_grad = final_sum(w_own[:2], after(w_came, rows_flat), w_other, 8)
    d_came = collect_rows(after(first.rank, in_grad), streams, IN_CHUNKS, DOWN_CHUNKS, (FF // 2, D))
    d_other = swapped(d_came, "dp", 1)
    down_grad = final_sum(w_own[2:], d_came, d_other, 8)
    output_rows, tokens_grad = stacked_rows(rows_flat, crops), stacked_rows(grads_flat, crops)

    gain_grad = packed[:, :D]
    shift_grad = packed[:, D : 2 * D]
    outbias_grad = packed[:, 2 * D : 3 * D]
    qv_grad = packed[0::2, 3 * D : 5 * D].reshape(2, 2, D)
    first_grad = packed[1::2, 3 * D : 3 * D + FF]
    rel_out = packed[0::2, 3 * D + FF :].reshape(2, HEADS, SPAN).transpose(0, 2, 1)

    return (
        output_rows,
        tokens_grad,
        in_grad[None],
        down_grad[None],
        gain_grad,
        shift_grad,
        outbias_grad,
        qv_grad,
        first_grad,
        rel_out,
    )


def solution(mesh):
    return jax.shard_map(
        on_device,
        mesh=mesh,
        in_specs=(
            P("dp", None, "pipe"),
            P("dp", None, "pipe"),
            P("pipe", None, None),
            P("pipe", None, None),
            P(),
            P(),
            P(),
            P(),
            P(),
            P(),
            P(),
            P("dp"),
            P("dp", None),
        ),
        out_specs=(
            P("dp", None, "pipe"),
            P("dp", None, "pipe"),
            P("pipe", None, None),
            P("pipe", None, None),
            P(),
            P(),
            P(),
            P(),
            P(),
            P(),
        ),
        check_vma=False,
    )
```

```python
import functools

import jax
import jax.numpy as jnp
import numpy as np
from jax import lax
from jax.experimental import pallas as pl
from jax.experimental.pallas import tpu as pltpu
from jax.sharding import PartitionSpec as P

HEADS = 24
HEAD = 32
FF = 3072
D = 768
WIN = 7
SMALL_SIDE = 3
SECTIONS = 4
MICRO = 4
POS = 49
SPAN = 169
SMALL = SMALL_SIDE * SMALL_SIDE

T = 128
PAIR = 2
R = PAIR * T
SMALL_AT = 2 * POS
GROUP = 4
TABLE = 256
IN_CHUNKS = 4
DOWN_CHUNKS = 2
CHUNKS = IN_CHUNKS + DOWN_CHUNKS
LINE = D // IN_CHUNKS

EPSILON = 1e-05
NEGATIVE = -1e30
SQRT_HALF = 0.7071067811865476
INV_SQRT_TAU = 0.3989422804014327
SCALE = HEAD**-0.5
BF = jnp.bfloat16
F32 = jnp.float32
VM = pl.BlockSpec(memory_space=pltpu.VMEM)
SM = pl.BlockSpec(memory_space=pltpu.SMEM)
LIMIT = 17 << 20
SMALL_LIMIT = 13 << 20
TINY_LIMIT = 8 << 20


LITTLE = pl.CostEstimate(flops=0, transcendentals=0, bytes_accessed=1024)


def pin(x):
    return pltpu.with_memory_space_constraint(x, pltpu.VMEM)


def like(x):
    return jax.ShapeDtypeStruct(x.shape, x.dtype)


def shape(dims, kind):
    return jax.ShapeDtypeStruct(dims, kind)


def nn(a, b):
    return lax.dot_general(a, b, (((1,), (0,)), ((), ())), preferred_element_type=F32)


def nt(a, b):
    return lax.dot_general(a, b, (((1,), (1,)), ((), ())), preferred_element_type=F32)


def tn(a, b):
    return lax.dot_general(a, b, (((0,), (0,)), ((), ())), preferred_element_type=F32)


def tile_layout():
    slot = np.full((T,), -1, np.int32)
    place = np.zeros((T,), np.int32)
    for big in range(2):
        slot[big * POS : (big + 1) * POS] = big
        place[big * POS : (big + 1) * POS] = np.arange(POS)
    small = np.array([r * WIN + c for r in range(SMALL_SIDE) for c in range(SMALL_SIDE)], np.int32)
    for k in range(3):
        at = SMALL_AT + SMALL * k
        slot[at : at + SMALL] = 2 + k
        place[at : at + SMALL] = small
    return slot, place


def pair_index():
    slot, place = tile_layout()
    row, col = place // WIN, place % WIN
    half = WIN // 2
    out, where = [], []
    for block in range(2):
        r, c = (row, col) if block == 0 else ((row - half) % WIN, (col - half) % WIN)
        index = (r[:, None] - r[None, :] + WIN - 1) * (2 * WIN - 1) + c[:, None] - c[None, :] + WIN - 1
        same = (slot[:, None] == slot[None, :]) & (slot[:, None] >= 0)
        out.append(np.where(same, index, TABLE - 1).astype(np.int32))
        where.append((r * WIN + c).astype(np.int32))
    return np.stack(out), where[1]


def crop_bases(flags, crops):
    bigs, smalls, found = jnp.int32(0), jnp.int32(0), []
    for c in range(crops):
        flag = flags[c]
        third = (smalls * 11) >> 5
        big_at = (bigs >> 1) * T + (bigs & 1) * POS
        small_at = third * T + SMALL_AT + SMALL * (smalls - 3 * third)
        found.append((flag, jnp.where(flag == 1, big_at, small_at)))
        bigs = bigs + flag
        smalls = smalls + (1 - flag)
    return found


def landing(flags, crops, axis):
    rows = POS * crops
    dims = (rows, 1) if axis == 0 else (1, rows)
    at = lax.broadcasted_iota(jnp.int32, dims, axis)
    place = at // crops
    crop = at - place * crops
    row = place // WIN
    col = place - row * WIN
    inside = (row < SMALL_SIDE) & (col < SMALL_SIDE)
    small = jnp.where(inside, row * SMALL_SIDE + col, -T * crops)
    out = jnp.full(dims, -1, jnp.int32)
    for c, (flag, base) in enumerate(crop_bases(flags, crops)):
        out = jnp.where(crop == c, base + jnp.where(flag == 1, place, small), out)
    return out


def pack_kernel(crops, info, flags, tokens, cotangent, *outs):
    section = info[0]
    target = lax.broadcasted_iota(jnp.int32, (R, POS * crops), 0)
    lands = landing(flags, crops, 1)

    @pl.loop(0, info[1])
    def _(t):
        picks = (target + t * R == lands).astype(F32).astype(BF)
        packed = [nn(picks, rows[...]).astype(BF) for rows in (tokens, cotangent)]
        for r, out in enumerate(outs):
            is_last = section == SECTIONS - 1 - r

            @pl.when(is_last)
            def _():
                out[t] = packed[1]

            @pl.when(jnp.logical_not(is_last))
            def _():
                out[t] = packed[0]


def pack_rows(info, flags, tokens, cotangent, chunks):
    rows, width = tokens.shape
    crops = rows // POS
    return pl.pallas_call(
        functools.partial(pack_kernel, crops),
        out_shape=[shape((chunks, R, width), BF)] * SECTIONS,
        in_specs=[SM, SM, VM, VM],
        out_specs=[VM] * SECTIONS,
        compiler_params=pltpu.CompilerParams(vmem_limit_bytes=TINY_LIMIT),
        cost_estimate=LITTLE,
        name="pack_rows",
    )(info, flags, tokens, cotangent)


def unpack_kernel(crops, info, flags, own, came1, came2, came3, rows_out, grad_out):
    section = info[0]
    lands = landing(flags, crops, 0)
    total = own.shape[0] * R
    target = lax.broadcasted_iota(jnp.int32, (POS * crops, total), 1)
    picks = (target == lands).astype(F32).astype(BF)
    came = (own, came1, came2, came3)
    used = lax.broadcasted_iota(jnp.int32, (total, own.shape[2]), 0) < info[1] * R

    def rows_of(ref):
        block = ref[...].reshape(total, -1).astype(F32)
        return jnp.where(used, block, 0.0).astype(BF)

    for s in range(SECTIONS):

        @pl.when(section == s)
        def _():
            rows_out[...] = nn(picks, rows_of(came[(s + 1) % SECTIONS])).astype(BF)
            grad_out[...] = nn(picks, rows_of(came[s]))


def unpack_rows(info, flags, own, came):
    width = own.shape[2]
    crops = flags.shape[0]
    return pl.pallas_call(
        functools.partial(unpack_kernel, crops),
        out_shape=[shape((POS * crops, width), BF), shape((POS * crops, width), F32)],
        in_specs=[SM, SM] + [VM] * 4,
        out_specs=[VM, VM],
        compiler_params=pltpu.CompilerParams(vmem_limit_bytes=TINY_LIMIT),
        cost_estimate=LITTLE,
        name="unpack_rows",
    )(info, flags, own, *came)


ROWS_AT_ONCE = 8


def onehot_rows(index, it):
    rows = index[pl.ds(it * ROWS_AT_ONCE, ROWS_AT_ONCE), :]
    entry = lax.broadcasted_iota(jnp.int32, (TABLE, T), 0)
    parts = [(entry == rows[r : r + 1, :]).astype(F32).astype(BF) for r in range(ROWS_AT_ONCE)]
    return jnp.concatenate(parts, 1)


def split3(x):
    top = x.astype(BF)
    rest = x - top.astype(F32)
    middle = rest.astype(BF)
    return top, middle, (rest - middle.astype(F32)).astype(BF)


def spread_kernel(index, table, out):
    parts = split3(table[...])

    @pl.loop(0, T // ROWS_AT_ONCE)
    def _(it):
        picks = onehot_rows(index, it)
        values = nn(parts[0], picks) + nn(parts[1], picks) + nn(parts[2], picks)
        for r in range(ROWS_AT_ONCE):
            out[:, it * ROWS_AT_ONCE + r, :] = values[:HEADS, r * T : (r + 1) * T]


def spread_table(index, table):
    return pl.pallas_call(
        spread_kernel,
        out_shape=shape((HEADS, T, T), F32),
        in_specs=[VM, VM],
        out_specs=VM,
        compiler_params=pltpu.CompilerParams(vmem_limit_bytes=TINY_LIMIT),
        cost_estimate=LITTLE,
        name="spread_table",
    )(index, table)


def fold_kernel(index, sums, out):
    out[...] = jnp.zeros_like(out)

    @pl.loop(0, T // ROWS_AT_ONCE)
    def _(it):
        picks = onehot_rows(index, it)
        rows = jnp.concatenate([sums[:, it * ROWS_AT_ONCE + r, :] for r in range(ROWS_AT_ONCE)], 1)
        top = rows.astype(BF)
        rest = (rows - top.astype(F32)).astype(BF)
        out[...] += nt(top, picks) + nt(rest, picks)


def fold_table(index, sums):
    return pl.pallas_call(
        fold_kernel,
        out_shape=shape((HEADS, TABLE), F32),
        in_specs=[VM, VM],
        out_specs=VM,
        compiler_params=pltpu.CompilerParams(vmem_limit_bytes=TINY_LIMIT),
        cost_estimate=LITTLE,
        name="fold_table",
    )(index, pin(sums))


def row_norm(x):
    mean = jnp.sum(x, -1, keepdims=True) * (1.0 / D)
    centered = x - mean
    var = jnp.sum(centered * centered, -1, keepdims=True) * (1.0 / D)
    inv = lax.rsqrt(var + EPSILON)
    return centered * inv, inv


def head_masks():
    lane = lax.broadcasted_iota(jnp.int32, (T, T), 1)
    return [(lane >= HEAD * h) & (lane < HEAD * (h + 1)) for h in range(GROUP)]


def spread_heads(block, masks):
    zero = jnp.zeros_like(block)
    return jnp.concatenate([jnp.where(m, block, zero) for m in masks], 0)


def gather_heads(stacked, masks):
    total = stacked[0:T]
    for h in range(1, GROUP):
        total = jnp.where(masks[h], stacked[h * T : (h + 1) * T], total)
    return total


def lanes(at, size=T):
    return pl.ds(pl.multiple_of(at, T), size)


STEP = 512
BLOCKS = FF // STEP


def attention_forward(x, n, vec, wide, w, bias, a, b, save_a, save_b, y):

    @pl.loop(0, 3)
    def _(s):
        cols = lanes(s * D, D)
        a[:, cols] = (nn(n, w[:, cols]) + wide[0:1, cols]).astype(BF)

    save_a[0].start()
    masks = head_masks()

    @pl.loop(0, PAIR)
    def _(t):
        rows = pl.ds(pl.multiple_of(t * T, T), T)
        for grp in range(HEADS // GROUP):
            lo = grp * T
            heads = slice(grp * GROUP, (grp + 1) * GROUP)
            q, k, v = (a[rows, lo + s * D : lo + s * D + T] for s in range(3))
            s = nt(spread_heads(q, masks), k) * SCALE + bias[heads].reshape(GROUP * T, T)
            e = jnp.exp(s - jnp.max(s, -1, keepdims=True))
            p = (e * (1.0 / jnp.sum(e, -1, keepdims=True))).astype(BF)
            b[t, heads] = p.reshape(GROUP, T, T)
            a[rows, 3 * D + lo : 3 * D + lo + T] = gather_heads(nn(p, v), masks).astype(BF)

    save_a[1].start()
    save_b.start()
    branch = nn(a[:, 3 * D :], w[:, 3 * D :]) + vec[2:3, :]
    y[...] = (x + branch).astype(BF)


ERF_SLOPE = 0.3275911 * SQRT_HALF
ERF_TERMS = (1.061405429, -1.453152027, 1.421413741, -0.284496736, 0.254829592)


def normal_parts(u):
    bell = jnp.exp(-0.5 * u * u)
    base = 1.0 + ERF_SLOPE * jnp.abs(u)
    t = pl.reciprocal(base, approx=True)
    t = t * (2.0 - base * t)
    poly = 0.5 * ERF_TERMS[0]
    for term in ERF_TERMS[1:]:
        poly = poly * t + 0.5 * term
    tail = poly * t * bell
    return jnp.where(u >= 0, 1.0 - tail, tail), u * (bell * INV_SQRT_TAU)


def mlp_forward(x, n, vec, wide, w, v, a, b, acc):
    acc[...] = x + vec[2:3, :]

    @pl.loop(0, BLOCKS, step=2)
    def _(j0):
        blocks = []
        for jb in (j0, j0 + 1):
            cols = lanes(jb * STEP, STEP)
            u = nn(n, w[:, cols]) + wide[0:1, cols]
            cdf, rise = normal_parts(u)
            blocks.append((jb, cols, (u * cdf).astype(BF), (cdf + rise).astype(BF)))
        part = None
        for jb, cols, act, slope in blocks:
            a[:, cols] = act
            for t in range(PAIR):
                for i in range(STEP // T):
                    b[t, jb * (STEP // T) + i] = slope[t * T : (t + 1) * T, i * T : (i + 1) * T]
            term = nn(act, v[cols, :])
            part = term if part is None else part + term
        acc[...] += part


def forward_kernel(both, info, slot, vec, wide, bias, w, *refs):
    v = refs[0] if both else None
    p0, p1, p2, p3, came = refs[both : both + 5]
    y, *kept = refs[both + 13 :]
    xs, keep_n, keep_a, keep_b, *outs = kept[:8]
    x_in, n, a, b, acc, parts, sems = kept[8:]
    width = parts.shape[-1]
    section, used = info[0], info[1]
    c = slot[0] - section

    def copy(source, target, k):
        return pltpu.make_async_copy(source, target, sems.at[k])

    save_x, save_n = copy(x_in, xs.at[c], 0), copy(n, keep_n.at[c], 1)
    save_b = copy(b, keep_b.at[c], 3)
    early = [copy(a.at[:, cut], keep_a.at[c, :, cut], 2) for cut in (pl.ds(0, 3 * D), pl.ds(3 * D, D))]
    put = [copy(parts.at[d], outs[(d + 1) % SECTIONS].at[c], 4 + d) for d in range(SECTIONS)]

    @pl.when((c >= slot[1]) & (c < jnp.minimum(slot[2], used)))
    def _():
        @pl.when(section == 0)
        def _():
            bring = [copy(p.at[c], parts.at[d], 4 + d) for d, p in enumerate((p0, p3, p2, p1))]
            for one in bring:
                one.start()
            for one in bring:
                one.wait()
            x_in[...] = jnp.concatenate([parts[d] for d in range(SECTIONS)], -1)

        @pl.when(section != 0)
        def _():
            x_in[...] = came[...]

        save_x.start()
        x = x_in[...].astype(F32)
        raw, _ = row_norm(x)
        normed = (raw * vec[0:1, :] + vec[1:2, :]).astype(BF)
        n[...] = normed
        save_n.start()

        @pl.when(section % 2 == 0)
        def _():
            attention_forward(x, normed, vec, wide, w, bias, a, b, early, save_b, y)

        if both:

            @pl.when(section % 2 == 1)
            def _():
                mlp_forward(x, normed, vec, wide, w, v, a, b, acc)
                for one in early:
                    one.start()
                save_b.start()
                y[...] = acc[...].astype(BF)

        @pl.when(both & (section == SECTIONS - 1))
        def _():
            for d in range(SECTIONS):
                parts[d] = y[:, d * width : (d + 1) * width]
                put[d].start()
            for d in range(SECTIONS):
                put[d].wait()

        save_x.wait()
        save_n.wait()
        for one in early:
            one.wait()
        save_b.wait()


ANY = pl.BlockSpec(memory_space=pl.ANY)


def far(x):
    return pltpu.with_memory_space_constraint(x, pltpu.HBM)


def run_forward(info, slot, pieces, came, vec, wide, w, v, bias, kept):
    count = len(kept)
    width = pieces[0].shape[-1]
    both = v is not None
    weights = [pin(w), pin(v)] if both else [pin(w)]
    outs = pl.pallas_call(
        functools.partial(forward_kernel, both),
        out_shape=[shape((R, D), BF)] + [like(r) for r in kept],
        in_specs=[SM, SM] + [VM] * (4 + both) + [ANY] * 4 + [VM] + [ANY] * count,
        out_specs=[VM] + [ANY] * count,
        scratch_shapes=[
            pltpu.VMEM((R, D), BF),
            pltpu.VMEM((R, D), BF),
            pltpu.VMEM((R, FF), BF),
            pltpu.VMEM((PAIR, HEADS, T, T), BF),
            pltpu.VMEM((R, D), F32),
            pltpu.VMEM((SECTIONS, R, width), BF),
            pltpu.SemaphoreType.DMA((4 + SECTIONS,)),
        ],
        input_output_aliases={11 + both + i: 1 + i for i in range(count)},
        compiler_params=pltpu.CompilerParams(vmem_limit_bytes=SMALL_LIMIT),
        cost_estimate=LITTLE,
        name="section_forward",
    )(info, slot, vec, wide, pin(bias), *weights, *pieces, came, *[far(r) for r in kept])
    return outs[0], list(outs[1:])


def norm_backward(x, g, dn, vec, sums, gx):
    raw, inv = row_norm(x)
    sums[0:1, :] += jnp.sum(dn * raw, 0, keepdims=True)
    sums[1:2, :] += jnp.sum(dn, 0, keepdims=True)
    sums[2:3, :] += jnp.sum(g, 0, keepdims=True)
    s = dn * vec[0:1, :]
    m1 = jnp.sum(s, -1, keepdims=True) * (1.0 / D)
    m2 = jnp.sum(s * raw, -1, keepdims=True) * (1.0 / D)
    gx[...] = (g + inv * (s - m1 - raw * m2)).astype(BF)


def attention_backward(g, w, a, b, bring_a, bring_b, d, acc, save_d, dsum):
    masks = head_masks()
    d[:, 3 * D :] = g
    d[:, 0:D] = nt(g, w[:, 3 * D :]).astype(BF)
    bring_a.wait()
    bring_b.wait()

    @pl.loop(0, PAIR)
    def _(t):
        rows = pl.ds(pl.multiple_of(t * T, T), T)
        for grp in range(HEADS // GROUP):
            lo = grp * T
            heads = slice(grp * GROUP, (grp + 1) * GROUP)
            q, k, v = (a[rows, lo + s * D : lo + s * D + T] for s in range(3))
            p = b[t, heads].reshape(GROUP * T, T)
            do_heads = spread_heads(d[rows, lo : lo + T], masks)
            dv = tn(p, do_heads)
            pf = p.astype(F32)
            pdp = pf * nt(do_heads, v)
            ds = (pdp - pf * jnp.sum(pdp, -1, keepdims=True)).astype(BF)
            dsum[heads] += ds.astype(F32).reshape(GROUP, T, T)
            dq = gather_heads(nn(ds, k), masks) * SCALE
            dk = tn(ds, spread_heads(q, masks)) * SCALE
            d[rows, lo : lo + T] = dq.astype(BF)
            d[rows, D + lo : D + lo + T] = dk.astype(BF)
            d[rows, 2 * D + lo : 2 * D + lo + T] = dv.astype(BF)

    save_d.start()
    acc[...] = jnp.zeros_like(acc)

    @pl.loop(0, 3)
    def _(s):
        cols = lanes(s * D, D)
        acc[...] += nt(d[:, cols], w[:, cols])


def mlp_backward(g, w, v, b, bring_b, d, acc):
    acc[...] = jnp.zeros_like(acc)
    bring_b.wait()

    @pl.loop(0, BLOCKS, step=2)
    def _(j0):
        blocks = []
        for jb in (j0, j0 + 1):
            cols = lanes(jb * STEP, STEP)
            da = nt(g, v[cols, :]).astype(BF).astype(F32)
            slope = jnp.concatenate(
                [
                    jnp.concatenate([b[t, jb * (STEP // T) + i] for i in range(STEP // T)], 1)
                    for t in range(PAIR)
                ],
                0,
            )
            blocks.append((cols, (da * slope.astype(F32)).astype(BF)))
        part = None
        for cols, du in blocks:
            d[:, cols] = du
            term = nt(du, w[:, cols])
            part = term if part is None else part + term
        acc[...] += part


def seed_rows(scales, c):
    row = lax.broadcasted_iota(jnp.int32, (T, 1), 0)
    parts = []
    for t in range(PAIR):
        base = (c * PAIR + t) * 8
        out = jnp.full((T, 1), scales[base], F32)
        for k, at in enumerate([POS] + [SMALL_AT + SMALL * i for i in range(3)]):
            out = jnp.where(row >= at, scales[base + 1 + k], out)
        parts.append(out)
    return jnp.concatenate(parts, 0)


def backward_kernel(info, slot, scales, vec, w, v, dsum_in, sums_in, p0, p1, p2, p3, came, *refs):
    gx, dsum, sums, *kept = refs[9:]
    xs, keep_a, keep_b, gs, keep_d, *outs = kept[:9]
    x_in, g_tile, a, b, d, acc, parts, sems = kept[9:]
    width = parts.shape[-1]
    section, used = info[0], info[1]
    c = slot[0] - (SECTIONS - 1 - section)

    def copy(source, target, k):
        return pltpu.make_async_copy(source, target, sems.at[k])

    bring_x, bring_a, bring_b = copy(xs.at[c], x_in, 0), copy(keep_a.at[c], a, 1), copy(keep_b.at[c], b, 2)
    save_g, save_d = copy(g_tile, gs.at[c], 3), copy(d, keep_d.at[c], 4)
    put = [copy(parts.at[k], outs[k].at[c], 5 + k) for k in range(SECTIONS)]

    @pl.when((c >= slot[1]) & (c < jnp.minimum(slot[2], used)))
    def _():
        @pl.when(section == SECTIONS - 1)
        def _():
            bring = [copy(p.at[c], parts.at[k], 5 + k) for k, p in enumerate((p3, p2, p1, p0))]
            for one in bring:
                one.start()
            bring_b.start()
            for one in bring:
                one.wait()
            seed = jnp.concatenate([parts[k] for k in range(SECTIONS)], -1).astype(F32)
            g_tile[...] = (seed * seed_rows(scales, c)).astype(BF)

        @pl.when(section != SECTIONS - 1)
        def _():
            bring_b.start()
            g_tile[...] = came[...]

        pl.when(section % 2 == 0)(bring_a.start)
        bring_x.start()
        save_g.start()

        @pl.when(c == 0)
        def _():
            dsum[...] = jnp.zeros_like(dsum)
            sums[...] = jnp.zeros_like(sums)

        g = g_tile[...]

        @pl.when(section % 2 == 0)
        def _():
            attention_backward(g, w, a, b, bring_a, bring_b, d, acc, save_d, dsum)

        @pl.when(section % 2 == 1)
        def _():
            mlp_backward(g, w, v, b, bring_b, d, acc)
            save_d.start()

        bring_x.wait()
        norm_backward(x_in[...].astype(F32), g.astype(F32), acc[...], vec, sums, gx)

        @pl.when(section == 0)
        def _():
            for k in range(SECTIONS):
                parts[k] = gx[:, k * width : (k + 1) * width]
                put[k].start()
            for k in range(SECTIONS):
                put[k].wait()

        save_g.wait()
        save_d.wait()


def run_backward(info, slot, scales, pieces, came, vec, w, v, dsum, sums, kept):
    count = len(kept)
    width = pieces[0].shape[-1]
    outs = pl.pallas_call(
        backward_kernel,
        out_shape=[shape((R, D), BF)] + [like(r) for r in (dsum, sums, *kept)],
        in_specs=[SM, SM, SM] + [VM] * 5 + [ANY] * 4 + [VM] + [ANY] * count,
        out_specs=[VM] * 3 + [ANY] * count,
        scratch_shapes=[
            pltpu.VMEM((R, D), BF),
            pltpu.VMEM((R, D), BF),
            pltpu.VMEM((R, FF), BF),
            pltpu.VMEM((PAIR, HEADS, T, T), BF),
            pltpu.VMEM((R, FF), BF),
            pltpu.VMEM((R, D), F32),
            pltpu.VMEM((SECTIONS, R, width), BF),
            pltpu.SemaphoreType.DMA((5 + SECTIONS,)),
        ],
        input_output_aliases={6: 1, 7: 2} | {13 + i: 3 + i for i in range(count)},
        compiler_params=pltpu.CompilerParams(vmem_limit_bytes=SMALL_LIMIT),
        cost_estimate=LITTLE,
        name="section_backward",
    )(
        info, slot, scales, vec, pin(w), pin(v), pin(dsum), pin(sums), *pieces, came,
        *[far(r) for r in kept],
    )
    return outs[0], outs[1], outs[2], list(outs[3:])


def make_room(dims):
    def body(*refs):
        pass

    return pl.pallas_call(
        body,
        out_shape=[pltpu.VMEM(d, k) if near else pltpu.HBM(d, k) for d, k, near in dims],
        out_specs=[VM if near else ANY for _, _, near in dims],
        compiler_params=pltpu.CompilerParams(vmem_limit_bytes=TINY_LIMIT),
        name="make_room",
    )()


def clear(ref, used, *at):
    @pl.loop(used, ref.shape[len(at)])
    def _(t):
        ref[(*at, t)] = jnp.zeros(ref.shape[-2:], BF)


def in_kernel(usual, info, keep_n, keep_a, keep_d, top, low, wide_sums, turned, n, a, d, tile, in_sems):
    chunks = n.shape[0]
    rows = chunks * R
    mlp, used = info[0] % 2, info[1]
    part = D // 2
    half = STEP // 2

    def bring(jb, first, count):
        cut = pl.ds(first, count)
        return pltpu.make_async_copy(
            keep_d.at[cut, :, pl.ds(jb * STEP, STEP)], d.at[jb, cut], in_sems.at[jb]
        )

    def others(work):
        for c in range(usual, chunks):
            pl.when(used > c)(functools.partial(work, c))

    bring_n = pltpu.make_async_copy(keep_n, n, in_sems.at[BLOCKS])
    bring_a = pltpu.make_async_copy(keep_a.at[:, :, pl.ds(3 * D, D)], a, in_sems.at[BLOCKS + 1])
    bring_n.start()
    for jb in range(BLOCKS):
        bring(jb, 0, usual).start()
    others(lambda c: [bring(jb, c, 1).start() for jb in range(BLOCKS)] and None)
    bring_a.start()
    bring_n.wait()
    clear(n, used)
    turned[0] = n[...].reshape(rows, D).T
    bring_a.wait()
    clear(a, used)

    @pl.when(mlp == 0)
    def _():
        turned[1] = a[...].reshape(rows, D).T

    @pl.when(mlp == 1)
    def _():
        turned[1] = turned[0]

    @pl.loop(0, BLOCKS)
    def _(jb):
        bring(jb, 0, usual).wait()
        others(lambda c: bring(jb, c, 1).wait())
        clear(d, used, jb)
        block = d[jb, :usual].reshape(usual * R, STEP)
        cols = lanes(jb * STEP, STEP)
        wide_sums[0:1, cols] = jnp.sum(block.astype(F32), 0, keepdims=True)

        def add_sum(c):
            wide_sums[0:1, cols] += jnp.sum(d[jb, c].astype(F32), 0, keepdims=True)

        others(add_sum)
        for k in range(2):
            late = (jb * 2 + k >= 3 * D // half).astype(jnp.int32)
            cut = slice(k * half, (k + 1) * half)
            tile[...] = nn(turned[late, :, : usual * R], block[:, cut])

            def add(c):
                tile[...] += nn(turned[late, :, c * R : (c + 1) * R], d[jb, c, :, cut])

            others(add)
            grad = tile[...].astype(BF)
            to = lanes(jb * STEP + k * half, half)
            top[:, to] = grad[:part]
            low[:, to] = grad[part:]


def in_grads(info, keep_n, keep_a, keep_d, usual):
    chunks = keep_n.shape[0]
    return pl.pallas_call(
        functools.partial(in_kernel, usual),
        out_shape=[pltpu.VMEM((D // 2, FF), BF)] * 2 + [shape((8, FF), F32)],
        in_specs=[SM] + [ANY] * 3,
        out_specs=[VM] * 3,
        scratch_shapes=[
            pltpu.VMEM((2, D, chunks * R), BF),
            pltpu.VMEM((chunks, R, D), BF),
            pltpu.VMEM((chunks, R, D), BF),
            pltpu.VMEM((BLOCKS, chunks, R, STEP), BF),
            pltpu.VMEM((D, STEP // 2), F32),
            pltpu.SemaphoreType.DMA((BLOCKS + 2,)),
        ],
        compiler_params=pltpu.CompilerParams(vmem_limit_bytes=LIMIT),
        cost_estimate=LITTLE,
        name="in_grads",
    )(info, *[far(r) for r in (keep_n, keep_a, keep_d)])


def down_kernel(usual, info, keep_a, gs, grad, a, g, tile, out, in_sems, out_sems):
    chunks = g.shape[0]
    mlp, used = info[0] % 2, info[1]

    def bring(jb, first, count):
        cut = pl.ds(first, count)
        return pltpu.make_async_copy(
            keep_a.at[cut, :, pl.ds(jb * STEP, STEP)], a.at[jb, cut], in_sems.at[jb]
        )

    def put(jb):
        return pltpu.make_async_copy(out.at[jb % 2], grad.at[pl.ds(jb * STEP, STEP), :], out_sems.at[jb % 2])

    def others(work):
        for c in range(usual, chunks):
            pl.when(used > c)(functools.partial(work, c))

    @pl.when(mlp == 1)
    def _():
        bring_g = pltpu.make_async_copy(gs, g, in_sems.at[BLOCKS])
        bring_g.start()
        for jb in range(BLOCKS):
            bring(jb, 0, usual).start()
        others(lambda c: [bring(jb, c, 1).start() for jb in range(BLOCKS)] and None)
        bring_g.wait()
        clear(g, used)
        flat_g = g[:usual].reshape(usual * R, D)

        @pl.loop(0, BLOCKS)
        def _(jb):
            bring(jb, 0, usual).wait()
            others(lambda c: bring(jb, c, 1).wait())
            clear(a, used, jb)

            @pl.when(jb >= 2)
            def _():
                put(jb - 2).wait()

            tile[...] = tn(a[jb, :usual].reshape(usual * R, STEP), flat_g)

            def add(c):
                tile[...] += tn(a[jb, c], g[c])

            others(add)
            out[jb % 2] = tile[...].astype(BF)
            put(jb).start()

        for jb in (BLOCKS - 2, BLOCKS - 1):
            put(jb).wait()


def down_grads(info, keep_a, gs, usual):
    chunks = gs.shape[0]
    dma = pltpu.SemaphoreType.DMA
    return pl.pallas_call(
        functools.partial(down_kernel, usual),
        out_shape=shape((FF, D), BF),
        in_specs=[SM] + [ANY] * 2,
        out_specs=ANY,
        scratch_shapes=[
            pltpu.VMEM((BLOCKS, chunks, R, STEP), BF),
            pltpu.VMEM((chunks, R, D), BF),
            pltpu.VMEM((STEP, D), F32),
            pltpu.VMEM((2, STEP, D), BF),
            dma((BLOCKS + 1,)),
            dma((2,)),
        ],
        compiler_params=pltpu.CompilerParams(vmem_limit_bytes=LIMIT),
        cost_estimate=LITTLE,
        name="down_grads",
    )(info, far(keep_a), far(gs))


def swapped(block, axis, bit):
    size = lax.axis_size(axis)
    return lax.ppermute(block, axis, [(i, i ^ bit) for i in range(size)])


def butterfly(block, axis):
    size = lax.axis_size(axis)
    if size & (size - 1):
        return lax.psum(block, axis)
    bit = 1
    while bit < size:
        block = block + swapped(block, axis, bit)
        bit *= 2
    return block


PARTS = 8


def pair_sum_kernel(mine, came, own, parcel, sems):
    rows = mine.shape[0] // PARTS
    moves = [
        pltpu.make_async_copy(came.at[pl.ds(k * rows, rows)], parcel.at[k], sems.at[k]) for k in range(PARTS)
    ]
    for move in moves:
        move.start()
    for move in moves:
        move.wait()

    @pl.loop(0, PARTS)
    def _(k):
        at = pl.ds(pl.multiple_of(k * rows, rows), rows)
        own[at, :] = (mine[at, :].astype(F32) + parcel[k].astype(F32)).astype(BF)


def pair_sum(mine, came):
    rows, cols = mine.shape
    return pl.pallas_call(
        pair_sum_kernel,
        out_shape=pltpu.VMEM(mine.shape, BF),
        in_specs=[VM, ANY],
        out_specs=VM,
        scratch_shapes=[pltpu.VMEM((PARTS, rows // PARTS, cols), BF), pltpu.SemaphoreType.DMA((PARTS,))],
        compiler_params=pltpu.CompilerParams(vmem_limit_bytes=TINY_LIMIT),
        cost_estimate=LITTLE,
        name="pair_sum",
    )(pin(mine), came)


def final_sum_kernel(count, blocks, came, other, *refs):
    owns, (out, parcel, wide, in_sems, out_sems) = refs[:count], refs[count:]
    rows = came.shape[0] // blocks
    each = blocks // count

    def bring(k):
        return pltpu.make_async_copy(other.at[pl.ds(k * rows, rows)], parcel.at[k], in_sems.at[k])

    def put(k):
        return pltpu.make_async_copy(wide.at[k % 2], out.at[pl.ds(k * rows, rows)], out_sems.at[k % 2])

    @pl.loop(0, blocks)
    def _(k):
        bring(k).start()

    for part, own in enumerate(owns):

        @pl.loop(0, each)
        def _(j):
            k = part * each + j
            bring(k).wait()

            @pl.when(k >= 2)
            def _():
                put(k - 2).wait()

            near = pl.ds(pl.multiple_of(j * rows, rows), rows)
            far_rows = pl.ds(pl.multiple_of(k * rows, rows), rows)
            value = own[near, :].astype(F32) + came[far_rows, :].astype(F32)
            wide[k % 2] = value + parcel[k].astype(F32)
            put(k).start()

    for k in range(blocks - 2, blocks):
        put(k).wait()


def final_sum(owns, came, other, blocks):
    rows, cols = came.shape
    return pl.pallas_call(
        functools.partial(final_sum_kernel, len(owns), blocks),
        out_shape=shape((rows, cols), F32),
        in_specs=[VM, ANY] + [VM] * len(owns),
        out_specs=ANY,
        scratch_shapes=[
            pltpu.VMEM((blocks, rows // blocks, cols), BF),
            pltpu.VMEM((2, rows // blocks, cols), F32),
            pltpu.SemaphoreType.DMA((blocks,)),
            pltpu.SemaphoreType.DMA((2,)),
        ],
        compiler_params=pltpu.CompilerParams(vmem_limit_bytes=10 << 20),
        cost_estimate=LITTLE,
        name="final_sum",
    )(pin(came), other, *[pin(x) for x in owns])


def line_kernel(stream, count, step, rank, came, *refs):
    tops, send = refs[:count], refs[count]
    chunk = step[0] - rank[0]
    at = stream * FF // 2

    def put(source, row, cuts):
        for k, (down_by, col) in enumerate(cuts):
            rows = pl.ds(pl.multiple_of(row + down_by, LINE), LINE)
            value = source[rows, col : col + D]

            @pl.when(rank[0] == 0)
            def _():
                send[k] = value

            @pl.when(rank[0] > 0)
            def _():
                send[k] = (value.astype(F32) + came[k].astype(F32)).astype(BF)

    side_by_side = ((0, at), (0, at + D))
    for half, source in enumerate(tops[:2]):
        first = half * IN_CHUNKS // 2

        @pl.when((chunk >= first) & (chunk < first + IN_CHUNKS // 2))
        def _():
            put(source, (chunk - first) * LINE, side_by_side)

    if count == 3:

        @pl.when((chunk >= IN_CHUNKS) & (chunk < CHUNKS))
        def _():
            put(tops[2], (chunk - IN_CHUNKS + stream * DOWN_CHUNKS) * 2 * LINE, ((0, 0), (LINE, 0)))


class LineSum:
    def __init__(self, place, core, length, stream):
        self.length, self.stream = length, stream
        self.rank = jnp.where(core == 0, place, length - 1 - place).reshape(1)
        self.came = jnp.zeros((2, LINE, D), BF)
        self.sends = CHUNKS + length - 2
        self.route = [(2 * z, 2 * z + 2) for z in range(length - 1)]
        self.route += [(2 * z + 3, 2 * z + 1) for z in range(length - 1)]
        self.kept = []

    def advance(self, step, owns):
        owns = owns[: 1 + (step >= IN_CHUNKS // 2) + (step >= IN_CHUNKS)]
        self.sent = pl.pallas_call(
            functools.partial(line_kernel, self.stream, len(owns)),
            out_shape=like(self.came),
            in_specs=[SM, SM] + [VM] * (1 + len(owns)),
            out_specs=VM,
            compiler_params=pltpu.CompilerParams(vmem_limit_bytes=TINY_LIMIT),
            cost_estimate=LITTLE,
            name="line_step",
        )(np.array([step], np.int32), self.rank, self.came, *[pin(x) for x in owns])
        self.came = lax.ppermute(self.sent, "dp", self.route)
        self.kept.append(self.came)


def collect_kernel(length, where, rank, *refs):
    kept, (out, zero, sems) = refs[:-3], refs[-3:]
    zero[...] = jnp.zeros_like(zero)

    def move(item, k, ref):
        row, col = where[item][1][k]
        to = out.at[pl.ds(row, LINE), pl.ds(col, D)]
        return pltpu.make_async_copy(ref, to, sems.at[item, k])

    for item, (index, _) in enumerate(where):
        for k in range(2):
            pl.when(rank[0] == 0)(move(item, k, zero).start)
            for r in range(1, length):
                pl.when(rank[0] == r)(move(item, k, kept[index[r - 1]].at[k]).start)
    for item in range(len(where)):
        for k in range(2):
            move(item, k, zero).wait()


def collect_rows(rank, streams, first, count, dims):
    length = streams[0].length
    kept, where = [], []
    for k, stream in enumerate(streams):
        for c in range(count):
            index = []
            for r in range(1, length):
                index.append(len(kept))
                kept.append(stream.kept[first + c + r - 1])
            if dims[1] == FF:
                spots = [(c * LINE, k * FF // 2), (c * LINE, k * FF // 2 + D)]
            else:
                spots = [((c + k * count) * 2 * LINE + half * LINE, 0) for half in range(2)]
            where.append((index, spots))
    return pl.pallas_call(
        functools.partial(collect_kernel, length, where),
        out_shape=pltpu.VMEM(dims, BF),
        in_specs=[SM] + [ANY] * len(kept),
        out_specs=VM,
        scratch_shapes=[pltpu.VMEM((LINE, D), BF), pltpu.SemaphoreType.DMA((len(where), 2))],
        compiler_params=pltpu.CompilerParams(vmem_limit_bytes=TINY_LIMIT),
        cost_estimate=LITTLE,
        name="collect_rows",
    )(rank, *kept)


def added(*parts):
    return sum(p.astype(F32) for p in parts)


def after(x, *first):
    return lax.optimization_barrier((x, *first))[0]


def flat_rows(x):
    return x.transpose(1, 0, 2).reshape(-1, x.shape[2])


def stacked_rows(x, crops):
    return x.reshape(POS, crops, -1).transpose(1, 0, 2)


def on_device(
    tokens,
    cotangent,
    in_weight,
    down_weight,
    norm_gain,
    norm_shift,
    out_bias,
    qv_bias,
    fc1_bias,
    rel_table,
    shift_regions,
    crop_global,
    micro_of,
):
    section = lax.axis_index("pipe")
    dp_index = lax.axis_index("dp")
    core, place = dp_index % 2, dp_index // 2
    dp_size = lax.axis_size("dp")
    mlp = section % 2
    block = section // 2
    crops = tokens.shape[0]
    chunks = (crops + 2 * PAIR - 1) // (2 * PAIR)
    last = SECTIONS - 1

    half = FF // 4
    sent = lax.dynamic_slice_in_dim(down_weight[0], core * half, half, 0)
    mine = lax.ppermute(sent, "pipe", [(s, s + 1) for s in range(0, SECTIONS, 2)])

    bigs_all = jnp.sum(crop_global)
    needed = jnp.maximum(
        (bigs_all + 2 * PAIR - 1) // (2 * PAIR), (crops - bigs_all + 3 * PAIR - 1) // (3 * PAIR)
    )
    info = after(jnp.stack([section, needed, core]).astype(jnp.int32), sent)
    packs = pack_rows(info, crop_global, flat_rows(tokens), flat_rows(cotangent), chunks)
    pieces = [packs[0]] + [
        lax.ppermute(packs[r], "pipe", [(SECTIONS - r, 0), (last - r, last)]) for r in range(1, SECTIONS)
    ]

    w = in_weight[0]

    vec = jnp.stack([norm_gain[section], norm_shift[section], out_bias[section]])
    qv = qv_bias[block]
    wide_attention = jnp.concatenate([qv[0], jnp.zeros((D,), F32), qv[1], jnp.zeros((D,), F32)])
    wide = jnp.where(mlp == 1, fc1_bias[block], wide_attention)[None]

    both, rolled = pair_index()
    regions = jnp.where(block == 1, shift_regions[rolled], 0)
    index = jnp.where(block == 1, both[1], both[0])
    index = jnp.where(regions[:, None] == regions[None, :], index, TABLE - 1)
    table = jnp.pad(
        rel_table[block].T, ((0, 32 - HEADS), (0, TABLE - SPAN)), constant_values=((0, 0), (0, NEGATIVE))
    )
    bias = spread_table(after(index, packs[0]), table)

    member = (micro_of == jnp.arange(MICRO, dtype=jnp.int32)[None, :]).astype(F32)
    crop_rows = jnp.where(crop_global == 1, POS, SMALL).astype(F32)
    counts = jnp.sum(member * crop_rows[:, None], 0)
    counts = jnp.concatenate([counts, needed.astype(F32).reshape(1)])
    count_rounds = [1 << k for k in range((dp_size - 1).bit_length())]
    before = np.tril(np.ones((crops, crops), np.int32), -1)
    bigs = jnp.sum(before * crop_global[None, :], 1)
    smalls = jnp.arange(crops, dtype=jnp.int32) - bigs
    entry = jnp.where(crop_global == 1, bigs // 2 * 8 + bigs % 2, smalls // 3 * 8 + 2 + smalls % 3)
    here = entry[:, None] == jnp.arange(chunks * PAIR * 8, dtype=jnp.int32)[None, :]

    width = tokens.shape[2]
    down_pipe = [(s, s + 1) for s in range(last)]
    up_pipe = [(s, s - 1) for s in range(1, SECTIONS)]

    dsum, sums, xs, keep_n, gs, keep_a, keep_d, keep_b, *outs = make_room(
        [((HEADS, T, T), F32, True), ((8, D), F32, True)]
        + [((chunks, R, D), BF, False)] * 3
        + [((chunks, R, FF), BF, False)] * 2
        + [((chunks, PAIR, HEADS, T, T), BF, False)]
        + [((chunks, R, width), BF, False)] * 4
    )
    usual = max(chunks - 1, 1)
    blank = jnp.zeros((R, D), BF)
    kept = [dsum, sums, xs, keep_n, gs, keep_a, keep_d, keep_b, *outs]

    def slot(at, first, stop):
        if isinstance(first, int):
            return np.array([first + at, first, stop], np.int32)
        return jnp.stack([first + at, first, stop]).astype(jnp.int32)

    def forward(i, first, stop, came, v, kept):
        dsum, sums, xs, keep_n, gs, keep_a, keep_d, keep_b, *outs = kept
        y, (xs, keep_n, keep_a, keep_b, *outs) = run_forward(
            info, slot(i, first, stop), pieces, came, vec, wide, w, v, bias,
            [xs, keep_n, keep_a, keep_b, *outs],
        )
        return y, [dsum, sums, xs, keep_n, gs, keep_a, keep_d, keep_b, *outs]

    def backward(j, first, stop, came, v, kept):
        dsum, sums, xs, keep_n, gs, keep_a, keep_d, keep_b, *outs = kept
        gx, dsum, sums, (xs, keep_a, keep_b, gs, keep_d, *outs) = run_backward(
            info, slot(j, first, stop), scales, pieces, came, vec, w, v,
            dsum, sums, [xs, keep_a, keep_b, gs, keep_d, *outs],
        )
        return gx, [dsum, sums, xs, keep_n, gs, keep_a, keep_d, keep_b, *outs]

    def count_round(counts, bit):
        other = swapped(counts, "dp", bit)
        return jnp.concatenate([counts[:MICRO] + other[:MICRO], jnp.maximum(counts, other)[MICRO:]])

    counts = count_round(counts, count_rounds[0])
    came_f, came_b = after(blank, counts), blank
    v = None
    for i in range(usual + 2 * last):
        if i < usual + last:
            y, kept = forward(i, 0, usual, came_f, v, kept)
            if i < usual + last - 1:
                came_f = lax.ppermute(y, "pipe", [(s, t) for s, t in down_pipe if 0 <= i - s < usual])
            if 0 < i < last:
                take = -(-len(count_rounds[1:]) // (last - 1))
                for bit in count_rounds[1:][(i - 1) * take : i * take]:
                    counts = count_round(after(counts, y), bit)
            if i == 0:
                mine = after(mine, y)
                other = swapped(mine, "dp", 1)
                upper = jnp.where(core == 0, mine, other), jnp.where(core == 0, other, mine)
                v = jnp.concatenate([down_weight[0], *upper], 0)
        if i == last:
            most = counts[MICRO].astype(jnp.int32)
            counts = counts[:MICRO]
            scales = jnp.sum(member * (jnp.sum(counts) / (MICRO * counts))[None], 1)
            scales = jnp.sum(jnp.where(here, scales[:, None], 0.0), 0)
        if i >= last:
            gx, kept = backward(i - last, 0, usual, came_b, v, kept)
            if i < usual + 2 * last - 1:
                came_b = lax.ppermute(gx, "pipe", [(s, t) for s, t in up_pipe if 0 <= i - 2 * last + s < usual])

    turns = 2 * last + 1

    def beyond(k, carry):
        came_f, came_b, kept = carry
        c, at = usual + k // turns, k % turns
        y, kept = forward(at, c, c + 1, came_f, v, kept)
        came_f = lax.ppermute(y, "pipe", down_pipe)
        gx, kept = backward(at - last, c, c + 1, came_b, v, kept)
        came_b = lax.ppermute(gx, "pipe", up_pipe)
        return came_f, came_b, kept

    more = jnp.maximum(most - usual, 0) * turns
    kept = lax.fori_loop(0, more, beyond, (blank, blank, kept))[2]
    dsum, sums, xs, keep_n, gs, keep_a, keep_d, keep_b, *outs = kept
    v_grad = down_grads(info, keep_a, gs, usual)
    w_top, w_low, wide_sums = in_grads(info, after(keep_n, v_grad), keep_a, keep_d, usual)

    route = [
        (s * dp_size + i, s * dp_size + (i ^ 1)) for s in range(1, SECTIONS, 2) for i in range(dp_size)
    ]
    v_came = lax.ppermute(v_grad, ("pipe", "dp"), route)
    out_came = []
    at = FF // 2 + half * core
    parts = [lax.dynamic_slice_in_dim(after(x, w_top), at, half, 0) for x in (v_grad, v_came)]
    v_part = added(*parts).astype(BF)
    v_back = lax.ppermute(v_part, "pipe", [(s + 1, s) for s in range(0, SECTIONS, 2)])
    w_own = [pair_sum(w_top, swapped(w_top, "dp", 1)), None, None]

    length = dp_size // 2
    first, second = streams = [LineSum(place, core, length, k) for k in range(2)]
    ends = streams[0].sends
    ready = [[]] + [[] for _ in range(ends + 8)]
    rounds = [("dp", 1 << k) for k in range((dp_size - 1).bit_length())] + [("pipe", 1), ("pipe", 2)]
    packed = waiting = None

    def turn(step, gap):
        nonlocal packed, waiting
        if waiting is not None:
            packed = packed + after(waiting, gap)
            waiting = None
            ready[step + 1].append(packed)
        if rounds:
            axis, bit = rounds.pop(0)
            if axis == "pipe" and bit == 1:
                packed = (jnp.arange(SECTIONS) == section).astype(F32)[:, None] * packed[None]
            waiting = swapped(after(packed, gap), axis, bit)

    for step in range(ends):
        first.came = after(first.came, *ready[step])
        first.advance(step, w_own)
        second.came = after(second.came, first.sent)
        second.advance(step, w_own)
        gap = second.sent
        ready[step + 1].append(gap)
        if step == 0:
            w_low = after(w_low, gap)
            w_own[1] = pair_sum(w_low, swapped(w_low, "dp", 1))
            rel_grad = fold_table(index, after(dsum, gap))
            narrow = jnp.where(
                mlp == 1,
                wide_sums[0],
                jnp.concatenate(
                    [wide_sums[0, :D], wide_sums[0, 2 * D : 3 * D], jnp.zeros((2 * D,), F32)]
                ),
            )
            packed = jnp.concatenate([sums[:3].reshape(-1), narrow, rel_grad[:, :SPAN].reshape(-1)])
            ready[1].append(packed)
        else:
            turn(step, gap)
        if step == IN_CHUNKS - 1:
            v_other = swapped(after(v_back, gap), "dp", 1)
            mine, other = after(v_back, first.came), after(v_other, first.came)
            v_high = jnp.concatenate(
                [jnp.where(core == 0, mine, other), jnp.where(core == 0, other, mine)], 0
            )
            v_low = added(v_grad[: FF // 2], v_came[: FF // 2]).astype(BF)
            w_own[2] = jnp.where(mlp == 1, v_low, v_high)
        if 1 < step < 2 + last:
            r = step - 1
            out_came.append(lax.ppermute(after(outs[r], gap), "pipe", [(last, r - 1), (0, r)]))
            ready[step + 3].append(out_came[-1])
        if step == ends - DOWN_CHUNKS:
            w_came = collect_rows(after(first.rank, gap), streams, 0, IN_CHUNKS, (D, FF))
            w_other = swapped(w_came, "dp", 1)
            ready[step + 1].append(w_came)
    while rounds or waiting is not None:
        turn(ends, second.sent)
    rows_flat, grads_flat = unpack_rows(info, after(crop_global, second.sent), outs[0], out_came)
    in_grad = final_sum(w_own[:2], after(w_came, rows_flat), w_other, 8)
    d_came = collect_rows(after(first.rank, in_grad), streams, IN_CHUNKS, DOWN_CHUNKS, (FF // 2, D))
    d_other = swapped(d_came, "dp", 1)
    down_grad = final_sum(w_own[2:], d_came, d_other, 8)
    output_rows, tokens_grad = stacked_rows(rows_flat, crops), stacked_rows(grads_flat, crops)

    gain_grad = packed[:, :D]
    shift_grad = packed[:, D : 2 * D]
    outbias_grad = packed[:, 2 * D : 3 * D]
    qv_grad = packed[0::2, 3 * D : 5 * D].reshape(2, 2, D)
    first_grad = packed[1::2, 3 * D : 3 * D + FF]
    rel_out = packed[0::2, 3 * D + FF :].reshape(2, HEADS, SPAN).transpose(0, 2, 1)

    return (
        output_rows,
        tokens_grad,
        in_grad[None],
        down_grad[None],
        gain_grad,
        shift_grad,
        outbias_grad,
        qv_grad,
        first_grad,
        rel_out,
    )


def solution(mesh):
    return jax.shard_map(
        on_device,
        mesh=mesh,
        in_specs=(
            P("dp", None, "pipe"),
            P("dp", None, "pipe"),
            P("pipe", None, None),
            P("pipe", None, None),
            P(),
            P(),
            P(),
            P(),
            P(),
            P(),
            P(),
            P("dp"),
            P("dp", None),
        ),
        out_specs=(
            P("dp", None, "pipe"),
            P("dp", None, "pipe"),
            P("pipe", None, None),
            P("pipe", None, None),
            P(),
            P(),
            P(),
            P(),
            P(),
            P(),
        ),
        check_vma=False,
    )
```

```python
import functools

import jax
import jax.numpy as jnp
import numpy as np
from jax import lax
from jax.experimental import pallas as pl
from jax.experimental.pallas import tpu as pltpu
from jax.sharding import PartitionSpec as P

HEADS = 24
HEAD = 32
FF = 3072
D = 768
WIN = 7
SMALL_SIDE = 3
SECTIONS = 4
MICRO = 4
POS = 49
SPAN = 169
SMALL = SMALL_SIDE * SMALL_SIDE

T = 128
PAIR = 2
R = PAIR * T
SMALL_AT = 2 * POS
GROUP = 4
TABLE = 256
IN_CHUNKS = 4
DOWN_CHUNKS = 2
CHUNKS = IN_CHUNKS + DOWN_CHUNKS
LINE = D // IN_CHUNKS

EPSILON = 1e-05
NEGATIVE = -1e30
SQRT_HALF = 0.7071067811865476
INV_SQRT_TAU = 0.3989422804014327
SCALE = HEAD**-0.5
BF = jnp.bfloat16
F32 = jnp.float32
VM = pl.BlockSpec(memory_space=pltpu.VMEM)
SM = pl.BlockSpec(memory_space=pltpu.SMEM)
LIMIT = 17 << 20
SMALL_LIMIT = 13 << 20
TINY_LIMIT = 8 << 20


LITTLE = pl.CostEstimate(flops=0, transcendentals=0, bytes_accessed=1024)


def pin(x):
    return pltpu.with_memory_space_constraint(x, pltpu.VMEM)


def like(x):
    return jax.ShapeDtypeStruct(x.shape, x.dtype)


def shape(dims, kind):
    return jax.ShapeDtypeStruct(dims, kind)


def nn(a, b):
    return lax.dot_general(a, b, (((1,), (0,)), ((), ())), preferred_element_type=F32)


def nt(a, b):
    return lax.dot_general(a, b, (((1,), (1,)), ((), ())), preferred_element_type=F32)


def tn(a, b):
    return lax.dot_general(a, b, (((0,), (0,)), ((), ())), preferred_element_type=F32)


def tile_layout():
    slot = np.full((T,), -1, np.int32)
    place = np.zeros((T,), np.int32)
    for big in range(2):
        slot[big * POS : (big + 1) * POS] = big
        place[big * POS : (big + 1) * POS] = np.arange(POS)
    small = np.array([r * WIN + c for r in range(SMALL_SIDE) for c in range(SMALL_SIDE)], np.int32)
    for k in range(3):
        at = SMALL_AT + SMALL * k
        slot[at : at + SMALL] = 2 + k
        place[at : at + SMALL] = small
    return slot, place


def pair_index():
    slot, place = tile_layout()
    row, col = place // WIN, place % WIN
    half = WIN // 2
    out, where = [], []
    for block in range(2):
        r, c = (row, col) if block == 0 else ((row - half) % WIN, (col - half) % WIN)
        index = (r[:, None] - r[None, :] + WIN - 1) * (2 * WIN - 1) + c[:, None] - c[None, :] + WIN - 1
        same = (slot[:, None] == slot[None, :]) & (slot[:, None] >= 0)
        out.append(np.where(same, index, TABLE - 1).astype(np.int32))
        where.append((r * WIN + c).astype(np.int32))
    return np.stack(out), where[1]


def crop_bases(flags, crops):
    bigs, smalls, found = jnp.int32(0), jnp.int32(0), []
    for c in range(crops):
        flag = flags[c]
        third = (smalls * 11) >> 5
        big_at = (bigs >> 1) * T + (bigs & 1) * POS
        small_at = third * T + SMALL_AT + SMALL * (smalls - 3 * third)
        found.append((flag, jnp.where(flag == 1, big_at, small_at)))
        bigs = bigs + flag
        smalls = smalls + (1 - flag)
    return found


def landing(flags, crops, axis):
    rows = POS * crops
    dims = (rows, 1) if axis == 0 else (1, rows)
    at = lax.broadcasted_iota(jnp.int32, dims, axis)
    place = at // crops
    crop = at - place * crops
    row = place // WIN
    col = place - row * WIN
    inside = (row < SMALL_SIDE) & (col < SMALL_SIDE)
    small = jnp.where(inside, row * SMALL_SIDE + col, -T * crops)
    out = jnp.full(dims, -1, jnp.int32)
    for c, (flag, base) in enumerate(crop_bases(flags, crops)):
        out = jnp.where(crop == c, base + jnp.where(flag == 1, place, small), out)
    return out


def pack_kernel(crops, info, flags, tokens, cotangent, *outs):
    section = info[0]
    target = lax.broadcasted_iota(jnp.int32, (R, POS * crops), 0)
    lands = landing(flags, crops, 1)

    @pl.loop(0, info[1])
    def _(t):
        picks = (target + t * R == lands).astype(F32).astype(BF)
        packed = [nn(picks, rows[...]).astype(BF) for rows in (tokens, cotangent)]
        for r, out in enumerate(outs):
            is_last = section == SECTIONS - 1 - r

            @pl.when(is_last)
            def _():
                out[t] = packed[1]

            @pl.when(jnp.logical_not(is_last))
            def _():
                out[t] = packed[0]


def pack_rows(info, flags, tokens, cotangent, chunks):
    rows, width = tokens.shape
    crops = rows // POS
    return pl.pallas_call(
        functools.partial(pack_kernel, crops),
        out_shape=[shape((chunks, R, width), BF)] * SECTIONS,
        in_specs=[SM, SM, VM, VM],
        out_specs=[VM] * SECTIONS,
        compiler_params=pltpu.CompilerParams(vmem_limit_bytes=TINY_LIMIT),
        cost_estimate=LITTLE,
        name="pack_rows",
    )(info, flags, tokens, cotangent)


def unpack_kernel(crops, info, flags, own, came1, came2, came3, rows_out, grad_out):
    section = info[0]
    lands = landing(flags, crops, 0)
    total = own.shape[0] * R
    target = lax.broadcasted_iota(jnp.int32, (POS * crops, total), 1)
    picks = (target == lands).astype(F32).astype(BF)
    came = (own, came1, came2, came3)
    used = lax.broadcasted_iota(jnp.int32, (total, own.shape[2]), 0) < info[1] * R

    def rows_of(ref):
        block = ref[...].reshape(total, -1).astype(F32)
        return jnp.where(used, block, 0.0).astype(BF)

    for s in range(SECTIONS):

        @pl.when(section == s)
        def _():
            rows_out[...] = nn(picks, rows_of(came[(s + 1) % SECTIONS])).astype(BF)
            grad_out[...] = nn(picks, rows_of(came[s]))


def unpack_rows(info, flags, own, came):
    width = own.shape[2]
    crops = flags.shape[0]
    return pl.pallas_call(
        functools.partial(unpack_kernel, crops),
        out_shape=[shape((POS * crops, width), BF), shape((POS * crops, width), F32)],
        in_specs=[SM, SM] + [VM] * 4,
        out_specs=[VM, VM],
        compiler_params=pltpu.CompilerParams(vmem_limit_bytes=TINY_LIMIT),
        cost_estimate=LITTLE,
        name="unpack_rows",
    )(info, flags, own, *came)


ROWS_AT_ONCE = 8


def onehot_rows(index, it):
    rows = index[pl.ds(it * ROWS_AT_ONCE, ROWS_AT_ONCE), :]
    entry = lax.broadcasted_iota(jnp.int32, (TABLE, T), 0)
    parts = [(entry == rows[r : r + 1, :]).astype(F32).astype(BF) for r in range(ROWS_AT_ONCE)]
    return jnp.concatenate(parts, 1)


def split3(x):
    top = x.astype(BF)
    rest = x - top.astype(F32)
    middle = rest.astype(BF)
    return top, middle, (rest - middle.astype(F32)).astype(BF)


def spread_kernel(index, table, out):
    parts = split3(table[...])

    @pl.loop(0, T // ROWS_AT_ONCE)
    def _(it):
        picks = onehot_rows(index, it)
        values = nn(parts[0], picks) + nn(parts[1], picks) + nn(parts[2], picks)
        for r in range(ROWS_AT_ONCE):
            out[:, it * ROWS_AT_ONCE + r, :] = values[:HEADS, r * T : (r + 1) * T]


def spread_table(index, table):
    return pl.pallas_call(
        spread_kernel,
        out_shape=shape((HEADS, T, T), F32),
        in_specs=[VM, VM],
        out_specs=VM,
        compiler_params=pltpu.CompilerParams(vmem_limit_bytes=TINY_LIMIT),
        cost_estimate=LITTLE,
        name="spread_table",
    )(index, table)


def fold_kernel(index, sums, out):
    out[...] = jnp.zeros_like(out)

    @pl.loop(0, T // ROWS_AT_ONCE)
    def _(it):
        picks = onehot_rows(index, it)
        rows = jnp.concatenate([sums[:, it * ROWS_AT_ONCE + r, :] for r in range(ROWS_AT_ONCE)], 1)
        top = rows.astype(BF)
        rest = (rows - top.astype(F32)).astype(BF)
        out[...] += nt(top, picks) + nt(rest, picks)


def fold_table(index, sums):
    return pl.pallas_call(
        fold_kernel,
        out_shape=shape((HEADS, TABLE), F32),
        in_specs=[VM, VM],
        out_specs=VM,
        compiler_params=pltpu.CompilerParams(vmem_limit_bytes=TINY_LIMIT),
        cost_estimate=LITTLE,
        name="fold_table",
    )(index, pin(sums))


def row_norm(x):
    mean = jnp.sum(x, -1, keepdims=True) * (1.0 / D)
    centered = x - mean
    var = jnp.sum(centered * centered, -1, keepdims=True) * (1.0 / D)
    inv = lax.rsqrt(var + EPSILON)
    return centered * inv, inv


def head_masks():
    lane = lax.broadcasted_iota(jnp.int32, (T, T), 1)
    return [(lane >= HEAD * h) & (lane < HEAD * (h + 1)) for h in range(GROUP)]


def spread_heads(block, masks):
    zero = jnp.zeros_like(block)
    return jnp.concatenate([jnp.where(m, block, zero) for m in masks], 0)


def gather_heads(stacked, masks):
    total = stacked[0:T]
    for h in range(1, GROUP):
        total = jnp.where(masks[h], stacked[h * T : (h + 1) * T], total)
    return total


def lanes(at, size=T):
    return pl.ds(pl.multiple_of(at, T), size)


STEP = 512
BLOCKS = FF // STEP


def attention_forward(x, n, vec, wide, w, bias, a, b, save_a, save_b, y):

    @pl.loop(0, 3)
    def _(s):
        cols = lanes(s * D, D)
        a[:, cols] = (nn(n, w[:, cols]) + wide[0:1, cols]).astype(BF)

    save_a[0].start()
    masks = head_masks()

    @pl.loop(0, PAIR)
    def _(t):
        rows = pl.ds(pl.multiple_of(t * T, T), T)
        for grp in range(HEADS // GROUP):
            lo = grp * T
            heads = slice(grp * GROUP, (grp + 1) * GROUP)
            q, k, v = (a[rows, lo + s * D : lo + s * D + T] for s in range(3))
            s = nt(spread_heads(q, masks), k) * SCALE + bias[heads].reshape(GROUP * T, T)
            e = jnp.exp(s - jnp.max(s, -1, keepdims=True))
            p = (e * (1.0 / jnp.sum(e, -1, keepdims=True))).astype(BF)
            b[t, heads] = p.reshape(GROUP, T, T)
            a[rows, 3 * D + lo : 3 * D + lo + T] = gather_heads(nn(p, v), masks).astype(BF)

    save_a[1].start()
    save_b.start()
    branch = nn(a[:, 3 * D :], w[:, 3 * D :]) + vec[2:3, :]
    y[...] = (x + branch).astype(BF)


ERF_SLOPE = 0.3275911 * SQRT_HALF
ERF_TERMS = (1.061405429, -1.453152027, 1.421413741, -0.284496736, 0.254829592)


def normal_parts(u):
    bell = jnp.exp(-0.5 * u * u)
    base = 1.0 + ERF_SLOPE * jnp.abs(u)
    t = pl.reciprocal(base, approx=True)
    t = t * (2.0 - base * t)
    poly = 0.5 * ERF_TERMS[0]
    for term in ERF_TERMS[1:]:
        poly = poly * t + 0.5 * term
    tail = poly * t * bell
    return jnp.where(u >= 0, 1.0 - tail, tail), u * (bell * INV_SQRT_TAU)


def mlp_forward(x, n, vec, wide, w, v, a, b, acc):
    acc[...] = x + vec[2:3, :]

    @pl.loop(0, BLOCKS, step=2)
    def _(j0):
        blocks = []
        for jb in (j0, j0 + 1):
            cols = lanes(jb * STEP, STEP)
            u = nn(n, w[:, cols]) + wide[0:1, cols]
            cdf, rise = normal_parts(u)
            blocks.append((jb, cols, (u * cdf).astype(BF), (cdf + rise).astype(BF)))
        part = None
        for jb, cols, act, slope in blocks:
            a[:, cols] = act
            for t in range(PAIR):
                for i in range(STEP // T):
                    b[t, jb * (STEP // T) + i] = slope[t * T : (t + 1) * T, i * T : (i + 1) * T]
            term = nn(act, v[cols, :])
            part = term if part is None else part + term
        acc[...] += part


def forward_kernel(both, info, slot, vec, wide, bias, w, *refs):
    v = refs[0] if both else None
    p0, p1, p2, p3, came = refs[both : both + 5]
    y, *kept = refs[both + 13 :]
    xs, keep_n, keep_a, keep_b, *outs = kept[:8]
    x_in, n, a, b, acc, parts, sems = kept[8:]
    width = parts.shape[-1]
    section, used = info[0], info[1]
    c = slot[0] - section

    def copy(source, target, k):
        return pltpu.make_async_copy(source, target, sems.at[k])

    save_x, save_n = copy(x_in, xs.at[c], 0), copy(n, keep_n.at[c], 1)
    save_b = copy(b, keep_b.at[c], 3)
    early = [copy(a.at[:, cut], keep_a.at[c, :, cut], 2) for cut in (pl.ds(0, 3 * D), pl.ds(3 * D, D))]
    put = [copy(parts.at[d], outs[(d + 1) % SECTIONS].at[c], 4 + d) for d in range(SECTIONS)]

    @pl.when((c >= slot[1]) & (c < jnp.minimum(slot[2], used)))
    def _():
        @pl.when(section == 0)
        def _():
            bring = [copy(p.at[c], parts.at[d], 4 + d) for d, p in enumerate((p0, p3, p2, p1))]
            for one in bring:
                one.start()
            for one in bring:
                one.wait()
            x_in[...] = jnp.concatenate([parts[d] for d in range(SECTIONS)], -1)

        @pl.when(section != 0)
        def _():
            x_in[...] = came[...]

        save_x.start()
        x = x_in[...].astype(F32)
        raw, _ = row_norm(x)
        normed = (raw * vec[0:1, :] + vec[1:2, :]).astype(BF)
        n[...] = normed
        save_n.start()

        @pl.when(section % 2 == 0)
        def _():
            attention_forward(x, normed, vec, wide, w, bias, a, b, early, save_b, y)

        if both:

            @pl.when(section % 2 == 1)
            def _():
                mlp_forward(x, normed, vec, wide, w, v, a, b, acc)
                for one in early:
                    one.start()
                save_b.start()
                y[...] = acc[...].astype(BF)

        @pl.when(both & (section == SECTIONS - 1))
        def _():
            for d in range(SECTIONS):
                parts[d] = y[:, d * width : (d + 1) * width]
                put[d].start()
            for d in range(SECTIONS):
                put[d].wait()

        save_x.wait()
        save_n.wait()
        for one in early:
            one.wait()
        save_b.wait()


ANY = pl.BlockSpec(memory_space=pl.ANY)


def far(x):
    return pltpu.with_memory_space_constraint(x, pltpu.HBM)


def run_forward(info, slot, pieces, came, vec, wide, w, v, bias, kept):
    count = len(kept)
    width = pieces[0].shape[-1]
    both = v is not None
    weights = [pin(w), pin(v)] if both else [pin(w)]
    outs = pl.pallas_call(
        functools.partial(forward_kernel, both),
        out_shape=[shape((R, D), BF)] + [like(r) for r in kept],
        in_specs=[SM, SM] + [VM] * (4 + both) + [ANY] * 4 + [VM] + [ANY] * count,
        out_specs=[VM] + [ANY] * count,
        scratch_shapes=[
            pltpu.VMEM((R, D), BF),
            pltpu.VMEM((R, D), BF),
            pltpu.VMEM((R, FF), BF),
            pltpu.VMEM((PAIR, HEADS, T, T), BF),
            pltpu.VMEM((R, D), F32),
            pltpu.VMEM((SECTIONS, R, width), BF),
            pltpu.SemaphoreType.DMA((4 + SECTIONS,)),
        ],
        input_output_aliases={11 + both + i: 1 + i for i in range(count)},
        compiler_params=pltpu.CompilerParams(vmem_limit_bytes=SMALL_LIMIT),
        cost_estimate=LITTLE,
        name="section_forward",
    )(info, slot, vec, wide, pin(bias), *weights, *pieces, came, *[far(r) for r in kept])
    return outs[0], list(outs[1:])


def norm_backward(x, g, dn, vec, sums, gx):
    raw, inv = row_norm(x)
    sums[0:1, :] += jnp.sum(dn * raw, 0, keepdims=True)
    sums[1:2, :] += jnp.sum(dn, 0, keepdims=True)
    sums[2:3, :] += jnp.sum(g, 0, keepdims=True)
    s = dn * vec[0:1, :]
    m1 = jnp.sum(s, -1, keepdims=True) * (1.0 / D)
    m2 = jnp.sum(s * raw, -1, keepdims=True) * (1.0 / D)
    gx[...] = (g + inv * (s - m1 - raw * m2)).astype(BF)


def attention_backward(g, w, a, b, bring_a, bring_b, d, acc, save_d, dsum):
    masks = head_masks()
    d[:, 3 * D :] = g
    d[:, 0:D] = nt(g, w[:, 3 * D :]).astype(BF)
    bring_a.wait()
    bring_b.wait()

    @pl.loop(0, PAIR)
    def _(t):
        rows = pl.ds(pl.multiple_of(t * T, T), T)
        for grp in range(HEADS // GROUP):
            lo = grp * T
            heads = slice(grp * GROUP, (grp + 1) * GROUP)
            q, k, v = (a[rows, lo + s * D : lo + s * D + T] for s in range(3))
            p = b[t, heads].reshape(GROUP * T, T)
            do_heads = spread_heads(d[rows, lo : lo + T], masks)
            dv = tn(p, do_heads)
            pf = p.astype(F32)
            pdp = pf * nt(do_heads, v)
            ds = (pdp - pf * jnp.sum(pdp, -1, keepdims=True)).astype(BF)
            dsum[heads] += ds.astype(F32).reshape(GROUP, T, T)
            dq = gather_heads(nn(ds, k), masks) * SCALE
            dk = tn(ds, spread_heads(q, masks)) * SCALE
            d[rows, lo : lo + T] = dq.astype(BF)
            d[rows, D + lo : D + lo + T] = dk.astype(BF)
            d[rows, 2 * D + lo : 2 * D + lo + T] = dv.astype(BF)

    save_d.start()
    acc[...] = jnp.zeros_like(acc)

    @pl.loop(0, 3)
    def _(s):
        cols = lanes(s * D, D)
        acc[...] += nt(d[:, cols], w[:, cols])


def mlp_backward(g, w, v, b, bring_b, d, acc):
    acc[...] = jnp.zeros_like(acc)
    bring_b.wait()

    @pl.loop(0, BLOCKS, step=2)
    def _(j0):
        blocks = []
        for jb in (j0, j0 + 1):
            cols = lanes(jb * STEP, STEP)
            da = nt(g, v[cols, :]).astype(BF).astype(F32)
            slope = jnp.concatenate(
                [
                    jnp.concatenate([b[t, jb * (STEP // T) + i] for i in range(STEP // T)], 1)
                    for t in range(PAIR)
                ],
                0,
            )
            blocks.append((cols, (da * slope.astype(F32)).astype(BF)))
        part = None
        for cols, du in blocks:
            d[:, cols] = du
            term = nt(du, w[:, cols])
            part = term if part is None else part + term
        acc[...] += part


def seed_rows(scales, c):
    row = lax.broadcasted_iota(jnp.int32, (T, 1), 0)
    parts = []
    for t in range(PAIR):
        base = (c * PAIR + t) * 8
        out = jnp.full((T, 1), scales[base], F32)
        for k, at in enumerate([POS] + [SMALL_AT + SMALL * i for i in range(3)]):
            out = jnp.where(row >= at, scales[base + 1 + k], out)
        parts.append(out)
    return jnp.concatenate(parts, 0)


def backward_kernel(info, slot, scales, vec, w, v, dsum_in, sums_in, p0, p1, p2, p3, came, *refs):
    gx, dsum, sums, *kept = refs[9:]
    xs, keep_a, keep_b, gs, keep_d, *outs = kept[:9]
    x_in, g_tile, a, b, d, acc, parts, sems = kept[9:]
    width = parts.shape[-1]
    section, used = info[0], info[1]
    c = slot[0] - (SECTIONS - 1 - section)

    def copy(source, target, k):
        return pltpu.make_async_copy(source, target, sems.at[k])

    bring_x, bring_a, bring_b = copy(xs.at[c], x_in, 0), copy(keep_a.at[c], a, 1), copy(keep_b.at[c], b, 2)
    save_g, save_d = copy(g_tile, gs.at[c], 3), copy(d, keep_d.at[c], 4)
    put = [copy(parts.at[k], outs[k].at[c], 5 + k) for k in range(SECTIONS)]

    @pl.when((c >= slot[1]) & (c < jnp.minimum(slot[2], used)))
    def _():
        @pl.when(section == SECTIONS - 1)
        def _():
            bring = [copy(p.at[c], parts.at[k], 5 + k) for k, p in enumerate((p3, p2, p1, p0))]
            for one in bring:
                one.start()
            bring_b.start()
            for one in bring:
                one.wait()
            seed = jnp.concatenate([parts[k] for k in range(SECTIONS)], -1).astype(F32)
            g_tile[...] = (seed * seed_rows(scales, c)).astype(BF)

        @pl.when(section != SECTIONS - 1)
        def _():
            bring_b.start()
            g_tile[...] = came[...]

        pl.when(section % 2 == 0)(bring_a.start)
        bring_x.start()
        save_g.start()

        @pl.when(c == 0)
        def _():
            dsum[...] = jnp.zeros_like(dsum)
            sums[...] = jnp.zeros_like(sums)

        g = g_tile[...]

        @pl.when(section % 2 == 0)
        def _():
            attention_backward(g, w, a, b, bring_a, bring_b, d, acc, save_d, dsum)

        @pl.when(section % 2 == 1)
        def _():
            mlp_backward(g, w, v, b, bring_b, d, acc)
            save_d.start()

        bring_x.wait()
        norm_backward(x_in[...].astype(F32), g.astype(F32), acc[...], vec, sums, gx)

        @pl.when(section == 0)
        def _():
            for k in range(SECTIONS):
                parts[k] = gx[:, k * width : (k + 1) * width]
                put[k].start()
            for k in range(SECTIONS):
                put[k].wait()

        save_g.wait()
        save_d.wait()


def run_backward(info, slot, scales, pieces, came, vec, w, v, dsum, sums, kept):
    count = len(kept)
    width = pieces[0].shape[-1]
    outs = pl.pallas_call(
        backward_kernel,
        out_shape=[shape((R, D), BF)] + [like(r) for r in (dsum, sums, *kept)],
        in_specs=[SM, SM, SM] + [VM] * 5 + [ANY] * 4 + [VM] + [ANY] * count,
        out_specs=[VM] * 3 + [ANY] * count,
        scratch_shapes=[
            pltpu.VMEM((R, D), BF),
            pltpu.VMEM((R, D), BF),
            pltpu.VMEM((R, FF), BF),
            pltpu.VMEM((PAIR, HEADS, T, T), BF),
            pltpu.VMEM((R, FF), BF),
            pltpu.VMEM((R, D), F32),
            pltpu.VMEM((SECTIONS, R, width), BF),
            pltpu.SemaphoreType.DMA((5 + SECTIONS,)),
        ],
        input_output_aliases={6: 1, 7: 2} | {13 + i: 3 + i for i in range(count)},
        compiler_params=pltpu.CompilerParams(vmem_limit_bytes=SMALL_LIMIT),
        cost_estimate=LITTLE,
        name="section_backward",
    )(
        info, slot, scales, vec, pin(w), pin(v), pin(dsum), pin(sums), *pieces, came,
        *[far(r) for r in kept],
    )
    return outs[0], outs[1], outs[2], list(outs[3:])


def make_room(dims):
    def body(*refs):
        pass

    return pl.pallas_call(
        body,
        out_shape=[pltpu.VMEM(d, k) if near else pltpu.HBM(d, k) for d, k, near in dims],
        out_specs=[VM if near else ANY for _, _, near in dims],
        compiler_params=pltpu.CompilerParams(vmem_limit_bytes=TINY_LIMIT),
        name="make_room",
    )()


def clear(ref, used, *at):
    @pl.loop(used, ref.shape[len(at)])
    def _(t):
        ref[(*at, t)] = jnp.zeros(ref.shape[-2:], BF)


def in_kernel(usual, info, keep_n, keep_a, keep_d, top, low, wide_sums, turned, n, a, d, tile, in_sems):
    chunks = n.shape[0]
    rows = chunks * R
    mlp, used = info[0] % 2, info[1]
    part = D // 2
    half = STEP // 2

    def bring(jb, first, count):
        cut = pl.ds(first, count)
        return pltpu.make_async_copy(
            keep_d.at[cut, :, pl.ds(jb * STEP, STEP)], d.at[jb, cut], in_sems.at[jb]
        )

    def others(work):
        for c in range(usual, chunks):
            pl.when(used > c)(functools.partial(work, c))

    bring_n = pltpu.make_async_copy(keep_n, n, in_sems.at[BLOCKS])
    bring_a = pltpu.make_async_copy(keep_a.at[:, :, pl.ds(3 * D, D)], a, in_sems.at[BLOCKS + 1])
    bring_n.start()
    for jb in range(BLOCKS):
        bring(jb, 0, usual).start()
    others(lambda c: [bring(jb, c, 1).start() for jb in range(BLOCKS)] and None)
    bring_a.start()
    bring_n.wait()
    clear(n, used)

    def turn(k, ref):
        turned[k, :, : usual * R] = ref[:usual].reshape(usual * R, D).T

        def other(c):
            turned[k, :, c * R : (c + 1) * R] = ref[c].T

        others(other)

    turn(0, n)
    bring_a.wait()
    clear(a, used)

    @pl.when(mlp == 0)
    def _():
        turn(1, a)

    @pl.when(mlp == 1)
    def _():
        turned[1] = turned[0]

    @pl.loop(0, BLOCKS)
    def _(jb):
        bring(jb, 0, usual).wait()
        others(lambda c: bring(jb, c, 1).wait())
        clear(d, used, jb)
        block = d[jb, :usual].reshape(usual * R, STEP)
        cols = lanes(jb * STEP, STEP)
        wide_sums[0:1, cols] = jnp.sum(block.astype(F32), 0, keepdims=True)

        def add_sum(c):
            wide_sums[0:1, cols] += jnp.sum(d[jb, c].astype(F32), 0, keepdims=True)

        others(add_sum)
        for k in range(2):
            late = (jb * 2 + k >= 3 * D // half).astype(jnp.int32)
            cut = slice(k * half, (k + 1) * half)
            tile[...] = nn(turned[late, :, : usual * R], block[:, cut])

            def add(c):
                tile[...] += nn(turned[late, :, c * R : (c + 1) * R], d[jb, c, :, cut])

            others(add)
            grad = tile[...].astype(BF)
            to = lanes(jb * STEP + k * half, half)
            top[:, to] = grad[:part]
            low[:, to] = grad[part:]


def in_grads(info, keep_n, keep_a, keep_d, usual):
    chunks = keep_n.shape[0]
    return pl.pallas_call(
        functools.partial(in_kernel, usual),
        out_shape=[pltpu.VMEM((D // 2, FF), BF)] * 2 + [shape((8, FF), F32)],
        in_specs=[SM] + [ANY] * 3,
        out_specs=[VM] * 3,
        scratch_shapes=[
            pltpu.VMEM((2, D, chunks * R), BF),
            pltpu.VMEM((chunks, R, D), BF),
            pltpu.VMEM((chunks, R, D), BF),
            pltpu.VMEM((BLOCKS, chunks, R, STEP), BF),
            pltpu.VMEM((D, STEP // 2), F32),
            pltpu.SemaphoreType.DMA((BLOCKS + 2,)),
        ],
        compiler_params=pltpu.CompilerParams(vmem_limit_bytes=LIMIT),
        cost_estimate=LITTLE,
        name="in_grads",
    )(info, *[far(r) for r in (keep_n, keep_a, keep_d)])


def down_kernel(usual, info, keep_a, gs, grad, a, g, tile, out, in_sems, out_sems):
    chunks = g.shape[0]
    mlp, used = info[0] % 2, info[1]

    def bring(jb, first, count):
        cut = pl.ds(first, count)
        return pltpu.make_async_copy(
            keep_a.at[cut, :, pl.ds(jb * STEP, STEP)], a.at[jb, cut], in_sems.at[jb]
        )

    def put(jb):
        return pltpu.make_async_copy(out.at[jb % 2], grad.at[pl.ds(jb * STEP, STEP), :], out_sems.at[jb % 2])

    def others(work):
        for c in range(usual, chunks):
            pl.when(used > c)(functools.partial(work, c))

    @pl.when(mlp == 1)
    def _():
        bring_g = pltpu.make_async_copy(gs, g, in_sems.at[BLOCKS])
        bring_g.start()
        for jb in range(BLOCKS):
            bring(jb, 0, usual).start()
        others(lambda c: [bring(jb, c, 1).start() for jb in range(BLOCKS)] and None)
        bring_g.wait()
        clear(g, used)
        flat_g = g[:usual].reshape(usual * R, D)

        @pl.loop(0, BLOCKS)
        def _(jb):
            bring(jb, 0, usual).wait()
            others(lambda c: bring(jb, c, 1).wait())
            clear(a, used, jb)

            @pl.when(jb >= 2)
            def _():
                put(jb - 2).wait()

            tile[...] = tn(a[jb, :usual].reshape(usual * R, STEP), flat_g)

            def add(c):
                tile[...] += tn(a[jb, c], g[c])

            others(add)
            out[jb % 2] = tile[...].astype(BF)
            put(jb).start()

        for jb in (BLOCKS - 2, BLOCKS - 1):
            put(jb).wait()


def down_grads(info, keep_a, gs, usual):
    chunks = gs.shape[0]
    dma = pltpu.SemaphoreType.DMA
    return pl.pallas_call(
        functools.partial(down_kernel, usual),
        out_shape=shape((FF, D), BF),
        in_specs=[SM] + [ANY] * 2,
        out_specs=ANY,
        scratch_shapes=[
            pltpu.VMEM((BLOCKS, chunks, R, STEP), BF),
            pltpu.VMEM((chunks, R, D), BF),
            pltpu.VMEM((STEP, D), F32),
            pltpu.VMEM((2, STEP, D), BF),
            dma((BLOCKS + 1,)),
            dma((2,)),
        ],
        compiler_params=pltpu.CompilerParams(vmem_limit_bytes=LIMIT),
        cost_estimate=LITTLE,
        name="down_grads",
    )(info, far(keep_a), far(gs))


def swapped(block, axis, bit):
    size = lax.axis_size(axis)
    return lax.ppermute(block, axis, [(i, i ^ bit) for i in range(size)])


def butterfly(block, axis):
    size = lax.axis_size(axis)
    if size & (size - 1):
        return lax.psum(block, axis)
    bit = 1
    while bit < size:
        block = block + swapped(block, axis, bit)
        bit *= 2
    return block


PARTS = 8


def pair_sum_kernel(mine, came, own, parcel, sems):
    rows = mine.shape[0] // PARTS
    moves = [
        pltpu.make_async_copy(came.at[pl.ds(k * rows, rows)], parcel.at[k], sems.at[k]) for k in range(PARTS)
    ]
    for move in moves:
        move.start()
    for move in moves:
        move.wait()

    @pl.loop(0, PARTS)
    def _(k):
        at = pl.ds(pl.multiple_of(k * rows, rows), rows)
        own[at, :] = (mine[at, :].astype(F32) + parcel[k].astype(F32)).astype(BF)


def pair_sum(mine, came):
    rows, cols = mine.shape
    return pl.pallas_call(
        pair_sum_kernel,
        out_shape=pltpu.VMEM(mine.shape, BF),
        in_specs=[VM, ANY],
        out_specs=VM,
        scratch_shapes=[pltpu.VMEM((PARTS, rows // PARTS, cols), BF), pltpu.SemaphoreType.DMA((PARTS,))],
        compiler_params=pltpu.CompilerParams(vmem_limit_bytes=TINY_LIMIT),
        cost_estimate=LITTLE,
        name="pair_sum",
    )(pin(mine), came)


def final_sum_kernel(count, blocks, came, other, *refs):
    owns, (out, parcel, wide, in_sems, out_sems) = refs[:count], refs[count:]
    rows = came.shape[0] // blocks
    each = blocks // count

    def bring(k):
        return pltpu.make_async_copy(other.at[pl.ds(k * rows, rows)], parcel.at[k], in_sems.at[k])

    def put(k):
        return pltpu.make_async_copy(wide.at[k % 2], out.at[pl.ds(k * rows, rows)], out_sems.at[k % 2])

    @pl.loop(0, blocks)
    def _(k):
        bring(k).start()

    for part, own in enumerate(owns):

        @pl.loop(0, each)
        def _(j):
            k = part * each + j
            bring(k).wait()

            @pl.when(k >= 2)
            def _():
                put(k - 2).wait()

            near = pl.ds(pl.multiple_of(j * rows, rows), rows)
            far_rows = pl.ds(pl.multiple_of(k * rows, rows), rows)
            value = own[near, :].astype(F32) + came[far_rows, :].astype(F32)
            wide[k % 2] = value + parcel[k].astype(F32)
            put(k).start()

    for k in range(blocks - 2, blocks):
        put(k).wait()


def final_sum(owns, came, other, blocks):
    rows, cols = came.shape
    return pl.pallas_call(
        functools.partial(final_sum_kernel, len(owns), blocks),
        out_shape=shape((rows, cols), F32),
        in_specs=[VM, ANY] + [VM] * len(owns),
        out_specs=ANY,
        scratch_shapes=[
            pltpu.VMEM((blocks, rows // blocks, cols), BF),
            pltpu.VMEM((2, rows // blocks, cols), F32),
            pltpu.SemaphoreType.DMA((blocks,)),
            pltpu.SemaphoreType.DMA((2,)),
        ],
        compiler_params=pltpu.CompilerParams(vmem_limit_bytes=10 << 20),
        cost_estimate=LITTLE,
        name="final_sum",
    )(pin(came), other, *[pin(x) for x in owns])


def line_kernel(stream, count, step, rank, came, *refs):
    tops, send = refs[:count], refs[count]
    chunk = step[0] - rank[0]
    at = stream * FF // 2

    def put(source, row, cuts):
        for k, (down_by, col) in enumerate(cuts):
            rows = pl.ds(pl.multiple_of(row + down_by, LINE), LINE)
            value = source[rows, col : col + D]

            @pl.when(rank[0] == 0)
            def _():
                send[k] = value

            @pl.when(rank[0] > 0)
            def _():
                send[k] = (value.astype(F32) + came[k].astype(F32)).astype(BF)

    side_by_side = ((0, at), (0, at + D))
    for half, source in enumerate(tops[:2]):
        first = half * IN_CHUNKS // 2

        @pl.when((chunk >= first) & (chunk < first + IN_CHUNKS // 2))
        def _():
            put(source, (chunk - first) * LINE, side_by_side)

    if count == 3:

        @pl.when((chunk >= IN_CHUNKS) & (chunk < CHUNKS))
        def _():
            put(tops[2], (chunk - IN_CHUNKS + stream * DOWN_CHUNKS) * 2 * LINE, ((0, 0), (LINE, 0)))


class LineSum:
    def __init__(self, place, core, length, stream):
        self.length, self.stream = length, stream
        self.rank = jnp.where(core == 0, place, length - 1 - place).reshape(1)
        self.came = jnp.zeros((2, LINE, D), BF)
        self.sends = CHUNKS + length - 2
        self.route = [(2 * z, 2 * z + 2) for z in range(length - 1)]
        self.route += [(2 * z + 3, 2 * z + 1) for z in range(length - 1)]
        self.kept = []

    def advance(self, step, owns):
        owns = owns[: 1 + (step >= IN_CHUNKS // 2) + (step >= IN_CHUNKS)]
        self.sent = pl.pallas_call(
            functools.partial(line_kernel, self.stream, len(owns)),
            out_shape=like(self.came),
            in_specs=[SM, SM] + [VM] * (1 + len(owns)),
            out_specs=VM,
            compiler_params=pltpu.CompilerParams(vmem_limit_bytes=TINY_LIMIT),
            cost_estimate=LITTLE,
            name="line_step",
        )(np.array([step], np.int32), self.rank, self.came, *[pin(x) for x in owns])
        self.came = lax.ppermute(self.sent, "dp", self.route)
        self.kept.append(self.came)


def collect_kernel(length, where, rank, *refs):
    kept, (out, zero, sems) = refs[:-3], refs[-3:]
    zero[...] = jnp.zeros_like(zero)

    def move(item, k, ref):
        row, col = where[item][1][k]
        to = out.at[pl.ds(row, LINE), pl.ds(col, D)]
        return pltpu.make_async_copy(ref, to, sems.at[item, k])

    for item, (index, _) in enumerate(where):
        for k in range(2):
            pl.when(rank[0] == 0)(move(item, k, zero).start)
            for r in range(1, length):
                pl.when(rank[0] == r)(move(item, k, kept[index[r - 1]].at[k]).start)
    for item in range(len(where)):
        for k in range(2):
            move(item, k, zero).wait()


def collect_rows(rank, streams, first, count, dims):
    length = streams[0].length
    kept, where = [], []
    for k, stream in enumerate(streams):
        for c in range(count):
            index = []
            for r in range(1, length):
                index.append(len(kept))
                kept.append(stream.kept[first + c + r - 1])
            if dims[1] == FF:
                spots = [(c * LINE, k * FF // 2), (c * LINE, k * FF // 2 + D)]
            else:
                spots = [((c + k * count) * 2 * LINE + half * LINE, 0) for half in range(2)]
            where.append((index, spots))
    return pl.pallas_call(
        functools.partial(collect_kernel, length, where),
        out_shape=pltpu.VMEM(dims, BF),
        in_specs=[SM] + [ANY] * len(kept),
        out_specs=VM,
        scratch_shapes=[pltpu.VMEM((LINE, D), BF), pltpu.SemaphoreType.DMA((len(where), 2))],
        compiler_params=pltpu.CompilerParams(vmem_limit_bytes=TINY_LIMIT),
        cost_estimate=LITTLE,
        name="collect_rows",
    )(rank, *kept)


def added(*parts):
    return sum(p.astype(F32) for p in parts)


def after(x, *first):
    return lax.optimization_barrier((x, *first))[0]


def flat_rows(x):
    return x.transpose(1, 0, 2).reshape(-1, x.shape[2])


def stacked_rows(x, crops):
    return x.reshape(POS, crops, -1).transpose(1, 0, 2)


def on_device(
    tokens,
    cotangent,
    in_weight,
    down_weight,
    norm_gain,
    norm_shift,
    out_bias,
    qv_bias,
    fc1_bias,
    rel_table,
    shift_regions,
    crop_global,
    micro_of,
):
    section = lax.axis_index("pipe")
    dp_index = lax.axis_index("dp")
    core, place = dp_index % 2, dp_index // 2
    dp_size = lax.axis_size("dp")
    mlp = section % 2
    block = section // 2
    crops = tokens.shape[0]
    chunks = (crops + 2 * PAIR - 1) // (2 * PAIR)
    last = SECTIONS - 1

    half = FF // 4
    sent = lax.dynamic_slice_in_dim(down_weight[0], core * half, half, 0)
    mine = lax.ppermute(sent, "pipe", [(s, s + 1) for s in range(0, SECTIONS, 2)])

    bigs_all = jnp.sum(crop_global)
    needed = jnp.maximum(
        (bigs_all + 2 * PAIR - 1) // (2 * PAIR), (crops - bigs_all + 3 * PAIR - 1) // (3 * PAIR)
    )
    info = after(jnp.stack([section, needed, core]).astype(jnp.int32), sent)
    packs = pack_rows(info, crop_global, flat_rows(tokens), flat_rows(cotangent), chunks)
    pieces = [packs[0]] + [
        lax.ppermute(packs[r], "pipe", [(SECTIONS - r, 0), (last - r, last)]) for r in range(1, SECTIONS)
    ]

    w = in_weight[0]

    vec = jnp.stack([norm_gain[section], norm_shift[section], out_bias[section]])
    qv = qv_bias[block]
    wide_attention = jnp.concatenate([qv[0], jnp.zeros((D,), F32), qv[1], jnp.zeros((D,), F32)])
    wide = jnp.where(mlp == 1, fc1_bias[block], wide_attention)[None]

    both, rolled = pair_index()
    regions = jnp.where(block == 1, shift_regions[rolled], 0)
    index = jnp.where(block == 1, both[1], both[0])
    index = jnp.where(regions[:, None] == regions[None, :], index, TABLE - 1)
    table = jnp.pad(
        rel_table[block].T, ((0, 32 - HEADS), (0, TABLE - SPAN)), constant_values=((0, 0), (0, NEGATIVE))
    )
    bias = spread_table(after(index, packs[0]), table)

    member = (micro_of == jnp.arange(MICRO, dtype=jnp.int32)[None, :]).astype(F32)
    crop_rows = jnp.where(crop_global == 1, POS, SMALL).astype(F32)
    counts = jnp.sum(member * crop_rows[:, None], 0)
    counts = jnp.concatenate([counts, needed.astype(F32).reshape(1)])
    count_rounds = [1 << k for k in range((dp_size - 1).bit_length())]
    before = np.tril(np.ones((crops, crops), np.int32), -1)
    bigs = jnp.sum(before * crop_global[None, :], 1)
    smalls = jnp.arange(crops, dtype=jnp.int32) - bigs
    entry = jnp.where(crop_global == 1, bigs // 2 * 8 + bigs % 2, smalls // 3 * 8 + 2 + smalls % 3)
    here = entry[:, None] == jnp.arange(chunks * PAIR * 8, dtype=jnp.int32)[None, :]

    width = tokens.shape[2]
    down_pipe = [(s, s + 1) for s in range(last)]
    up_pipe = [(s, s - 1) for s in range(1, SECTIONS)]

    dsum, sums, xs, keep_n, gs, keep_a, keep_d, keep_b, *outs = make_room(
        [((HEADS, T, T), F32, True), ((8, D), F32, True)]
        + [((chunks, R, D), BF, False)] * 3
        + [((chunks, R, FF), BF, False)] * 2
        + [((chunks, PAIR, HEADS, T, T), BF, False)]
        + [((chunks, R, width), BF, False)] * 4
    )
    usual = max(chunks - 1, 1)
    blank = jnp.zeros((R, D), BF)
    kept = [dsum, sums, xs, keep_n, gs, keep_a, keep_d, keep_b, *outs]

    def slot(at, first, stop):
        if isinstance(first, int):
            return np.array([first + at, first, stop], np.int32)
        return jnp.stack([first + at, first, stop]).astype(jnp.int32)

    def forward(i, first, stop, came, v, kept):
        dsum, sums, xs, keep_n, gs, keep_a, keep_d, keep_b, *outs = kept
        y, (xs, keep_n, keep_a, keep_b, *outs) = run_forward(
            info, slot(i, first, stop), pieces, came, vec, wide, w, v, bias,
            [xs, keep_n, keep_a, keep_b, *outs],
        )
        return y, [dsum, sums, xs, keep_n, gs, keep_a, keep_d, keep_b, *outs]

    def backward(j, first, stop, came, v, kept):
        dsum, sums, xs, keep_n, gs, keep_a, keep_d, keep_b, *outs = kept
        gx, dsum, sums, (xs, keep_a, keep_b, gs, keep_d, *outs) = run_backward(
            info, slot(j, first, stop), scales, pieces, came, vec, w, v,
            dsum, sums, [xs, keep_a, keep_b, gs, keep_d, *outs],
        )
        return gx, [dsum, sums, xs, keep_n, gs, keep_a, keep_d, keep_b, *outs]

    def count_round(counts, bit):
        other = swapped(counts, "dp", bit)
        return jnp.concatenate([counts[:MICRO] + other[:MICRO], jnp.maximum(counts, other)[MICRO:]])

    counts = count_round(counts, count_rounds[0])
    came_f, came_b = after(blank, counts), blank
    v = None
    for i in range(usual + 2 * last):
        if i < usual + last:
            y, kept = forward(i, 0, usual, came_f, v, kept)
            if i < usual + last - 1:
                came_f = lax.ppermute(y, "pipe", [(s, t) for s, t in down_pipe if 0 <= i - s < usual])
            if 0 < i < last:
                take = -(-len(count_rounds[1:]) // (last - 1))
                for bit in count_rounds[1:][(i - 1) * take : i * take]:
                    counts = count_round(after(counts, y), bit)
            if i == 0:
                mine = after(mine, y)
                other = swapped(mine, "dp", 1)
                upper = jnp.where(core == 0, mine, other), jnp.where(core == 0, other, mine)
                v = jnp.concatenate([down_weight[0], *upper], 0)
        if i == last:
            most = counts[MICRO].astype(jnp.int32)
            counts = counts[:MICRO]
            scales = jnp.sum(member * (jnp.sum(counts) / (MICRO * counts))[None], 1)
            scales = jnp.sum(jnp.where(here, scales[:, None], 0.0), 0)
        if i >= last:
            gx, kept = backward(i - last, 0, usual, came_b, v, kept)
            if i < usual + 2 * last - 1:
                came_b = lax.ppermute(gx, "pipe", [(s, t) for s, t in up_pipe if 0 <= i - 2 * last + s < usual])

    turns = 2 * last + 1

    def beyond(k, carry):
        came_f, came_b, kept = carry
        c, at = usual + k // turns, k % turns
        y, kept = forward(at, c, c + 1, came_f, v, kept)
        came_f = lax.ppermute(y, "pipe", down_pipe)
        gx, kept = backward(at - last, c, c + 1, came_b, v, kept)
        came_b = lax.ppermute(gx, "pipe", up_pipe)
        return came_f, came_b, kept

    more = jnp.maximum(most - usual, 0) * turns
    kept = lax.fori_loop(0, more, beyond, (blank, blank, kept))[2]
    dsum, sums, xs, keep_n, gs, keep_a, keep_d, keep_b, *outs = kept
    v_grad = down_grads(info, keep_a, gs, usual)
    w_top, w_low, wide_sums = in_grads(info, after(keep_n, v_grad), keep_a, keep_d, usual)

    route = [
        (s * dp_size + i, s * dp_size + (i ^ 1)) for s in range(1, SECTIONS, 2) for i in range(dp_size)
    ]
    v_came = lax.ppermute(v_grad, ("pipe", "dp"), route)
    out_came = []
    at = FF // 2 + half * core
    parts = [lax.dynamic_slice_in_dim(after(x, w_top), at, half, 0) for x in (v_grad, v_came)]
    v_part = added(*parts).astype(BF)
    v_back = lax.ppermute(v_part, "pipe", [(s + 1, s) for s in range(0, SECTIONS, 2)])
    w_own = [pair_sum(w_top, swapped(w_top, "dp", 1)), None, None]

    length = dp_size // 2
    first, second = streams = [LineSum(place, core, length, k) for k in range(2)]
    ends = streams[0].sends
    ready = [[]] + [[] for _ in range(ends + 8)]
    rounds = [("dp", 1 << k) for k in range((dp_size - 1).bit_length())] + [("pipe", 1), ("pipe", 2)]
    packed = waiting = None

    def turn(step, gap):
        nonlocal packed, waiting
        if waiting is not None:
            packed = packed + after(waiting, gap)
            waiting = None
            ready[step + 1].append(packed)
        if rounds:
            axis, bit = rounds.pop(0)
            if axis == "pipe" and bit == 1:
                packed = (jnp.arange(SECTIONS) == section).astype(F32)[:, None] * packed[None]
            waiting = swapped(after(packed, gap), axis, bit)

    for step in range(ends):
        first.came = after(first.came, *ready[step])
        first.advance(step, w_own)
        second.came = after(second.came, first.sent)
        second.advance(step, w_own)
        gap = second.sent
        ready[step + 1].append(gap)
        if step == 0:
            w_low = after(w_low, gap)
            w_own[1] = pair_sum(w_low, swapped(w_low, "dp", 1))
            rel_grad = fold_table(index, after(dsum, w_top))
            narrow = jnp.where(
                mlp == 1,
                wide_sums[0],
                jnp.concatenate(
                    [wide_sums[0, :D], wide_sums[0, 2 * D : 3 * D], jnp.zeros((2 * D,), F32)]
                ),
            )
            packed = jnp.concatenate([sums[:3].reshape(-1), narrow, rel_grad[:, :SPAN].reshape(-1)])
            ready[1].append(packed)
        else:
            turn(step, gap)
        if step == IN_CHUNKS - 1:
            v_other = swapped(after(v_back, gap), "dp", 1)
            mine, other = after(v_back, first.came), after(v_other, first.came)
            v_high = jnp.concatenate(
                [jnp.where(core == 0, mine, other), jnp.where(core == 0, other, mine)], 0
            )
            v_low = added(v_grad[: FF // 2], v_came[: FF // 2]).astype(BF)
            w_own[2] = jnp.where(mlp == 1, v_low, v_high)
        if 1 < step < 2 + last:
            r = step - 1
            out_came.append(lax.ppermute(after(outs[r], gap), "pipe", [(last, r - 1), (0, r)]))
            ready[step + 3].append(out_came[-1])
        if step == ends - DOWN_CHUNKS:
            w_came = collect_rows(after(first.rank, gap), streams, 0, IN_CHUNKS, (D, FF))
            w_other = swapped(w_came, "dp", 1)
            ready[step + 1].append(w_came)
    while rounds or waiting is not None:
        turn(ends, second.sent)
    rows_flat, grads_flat = unpack_rows(info, after(crop_global, second.sent), outs[0], out_came)
    in_grad = final_sum(w_own[:2], after(w_came, rows_flat), w_other, 8)
    d_came = collect_rows(after(first.rank, in_grad), streams, IN_CHUNKS, DOWN_CHUNKS, (FF // 2, D))
    d_other = swapped(d_came, "dp", 1)
    down_grad = final_sum(w_own[2:], d_came, d_other, 8)
    output_rows, tokens_grad = stacked_rows(rows_flat, crops), stacked_rows(grads_flat, crops)

    gain_grad = packed[:, :D]
    shift_grad = packed[:, D : 2 * D]
    outbias_grad = packed[:, 2 * D : 3 * D]
    qv_grad = packed[0::2, 3 * D : 5 * D].reshape(2, 2, D)
    first_grad = packed[1::2, 3 * D : 3 * D + FF]
    rel_out = packed[0::2, 3 * D + FF :].reshape(2, HEADS, SPAN).transpose(0, 2, 1)

    return (
        output_rows,
        tokens_grad,
        in_grad[None],
        down_grad[None],
        gain_grad,
        shift_grad,
        outbias_grad,
        qv_grad,
        first_grad,
        rel_out,
    )


def solution(mesh):
    return jax.shard_map(
        on_device,
        mesh=mesh,
        in_specs=(
            P("dp", None, "pipe"),
            P("dp", None, "pipe"),
            P("pipe", None, None),
            P("pipe", None, None),
            P(),
            P(),
            P(),
            P(),
            P(),
            P(),
            P(),
            P("dp"),
            P("dp", None),
        ),
        out_specs=(
            P("dp", None, "pipe"),
            P("dp", None, "pipe"),
            P("pipe", None, None),
            P("pipe", None, None),
            P(),
            P(),
            P(),
            P(),
            P(),
            P(),
        ),
        check_vma=False,
    )
```
